32 devices in a mesh: section: 2 (over x), dp: 4 (over y, core), mp: 4 (over z).
Axes of the slice: x: 2, y: 2, z: 4, core: 2. Of those that a mesh axis runs over, the one named last changes fastest.
Arguments:
- tokens: bfloat16 [8, 768, 768], P('dp', 'mp'), may hold values from -6 to 6
- attn_gain: float32 [2, 768], P('section'), may hold values from 0.5 to 1.5
- w_query: bfloat16 [2, 768, 768], P('section', None, 'mp'), may hold values from -0.02734375 to 0.02734375
- w_key: bfloat16 [2, 768, 768], P('section', None, 'mp'), may hold values from -0.21875 to 0.21875
- w_value: bfloat16 [2, 768, 768], P('section', None, 'mp'), may hold values from -0.21875 to 0.21875
- w_out: bfloat16 [2, 768, 768], P('section', 'mp'), may hold values from -1.25 to 1.25
- ffn_gain: float32 [2, 768], P('section'), may hold values from 0.5 to 1.5
- w_gate: bfloat16 [2, 768, 2048], P('section', None, 'mp'), may hold values from -0.21875 to 0.21875
- w_up: bfloat16 [2, 768, 2048], P('section', None, 'mp'), may hold values from -0.21875 to 0.21875
- w_down: bfloat16 [2, 2048, 768], P('section', 'mp'), may hold values from -0.125 to 0.125
- rel_table: float32 [32, 12], P(None, 'mp'), may hold values from -4 to 4
- final_gain: float32 [768], replicated, may hold values from 0.5 to 1.5
- w_proj: bfloat16 [768, 128], replicated, may hold values from -0.21875 to 0.21875
- positives: int32 [64, 4], P('dp'), may hold values from -1 to 7, as said below
- retrieved: int32 [64, 32, 32], P('dp'), may hold values from 0 to 4095
Outputs:
- loss: float32 [], replicated
- d_inputs: bfloat16 [2, 8, 768, 768], P('section', 'dp', 'mp')
- grad_attn_gain: float32 [2, 768], P('section')
- grad_w_query: float32 [2, 768, 768], P('section', None, 'mp')
- grad_w_key: float32 [2, 768, 768], P('section', None, 'mp')
- grad_w_value: float32 [2, 768, 768], P('section', None, 'mp')
- grad_w_out: float32 [2, 768, 768], P('section', 'mp')
- grad_ffn_gain: float32 [2, 768], P('section')
- grad_w_gate: float32 [2, 768, 2048], P('section', None, 'mp')
- grad_w_up: float32 [2, 768, 2048], P('section', None, 'mp')
- grad_w_down: float32 [2, 2048, 768], P('section', 'mp')
- grad_rel_table: float32 [32, 12], P(None, 'mp')
- grad_final_gain: float32 [768], replicated
- grad_w_proj: float32 [768, 128], P(None, 'mp')
The draws below stay inside these ranges and needn't reach their ends.
Inputs may be any that keep to these rules, and one draw needn't show every extreme that they name: `positives`: each row lists 1 to 4 different document numbers first and -1 in its remaining slots; some row lists 4, some row one.
All inputs are finite; a program needn't handle non-finite values.
Results may differ from the reference program's by a relative error of at most 0.035.
Values may be sent and summed in bfloat16 or wider, within the bound.
No kernel may reach another device: no remote copies, remote signals or barrier semaphores. Data moves between devices by JAX's collectives and lax.ppermute only.
A program may use at most 192 MiB of HBM per device.

```python
import jax
import jax.numpy as jnp
from jax import lax

D = 768
HEADS = 12
HEAD_DIM = 64
FF = 2048
BUCKETS = 32
PROJ = 128
DOC_LEN = 512
QRY_LEN = 32
TOPK = 32
MAXPOS = 4
DOCS_MB = 1
QRYS_MB = 8
MB_TOK = 768
NMB = 8
NDOC = 8
NQ = 64
DOC_TOKENS = 4096


def draw_positives(key, part):
    key = jax.random.fold_in(key, 7)
    order_key, count_key = jax.random.split(key)
    row_keys = jax.random.split(order_key, NQ)
    picked = jax.vmap(lambda one_key: jax.random.permutation(one_key, NDOC)[:MAXPOS])(row_keys)
    counts = jax.random.randint(count_key, (NQ,), 1, MAXPOS + 1)
    counts = counts.at[0].set(MAXPOS).at[NQ - 1].set(1)
    slots = jnp.arange(MAXPOS)[None, :]
    return jnp.where(slots < counts[:, None], picked, -1).astype(jnp.int32)


def with_ends(entries, key, least, largest):
    dims = entries.shape
    place = [jax.random.randint(jax.random.fold_in(key, axis), (), 0, dims[axis]) for axis in range(len(dims))]
    entries = entries.at[tuple(place)].set(least)
    longest = dims.index(max(dims))
    place[longest] = (place[longest] + 1) % dims[longest]
    return entries.at[tuple(place)].set(largest)


def shard_levels(stream_key, dims, shards, low, high):
    def one(position, parts):
        draws = jax.random.uniform(jax.random.fold_in(jax.random.fold_in(stream_key, 6), position), (parts,), jnp.float32, low / len(shards), high / len(shards))
        return jnp.repeat(jnp.exp(draws), dims[position] // parts).reshape((-1,) + (1,) * (len(dims) - position - 1))

    level = one(*shards[0])
    for cut in shards[1:]:
        level = level * one(*cut)
    return level


def noise(stream_key, dims, width, limit, cuts=(), held_as=jnp.bfloat16):
    result = jax.random.normal(stream_key, dims, jnp.float32) * width
    if len(cuts) > 0:
        result = shard_levels(stream_key, dims, cuts, -0.22, 0.18) * result
    return jnp.clip(result, min=-limit, max=limit).astype(held_as)


def setup_inputs(seed: int = 0) -> dict:
    splits = jax.random.split(jax.random.key(seed), 16)
    tokens = noise(splits[0], (NMB, MB_TOK, D), 1.0, 6.0, ((0, 4), (1, 4)))
    attn_gain = jnp.clip(1.0 + 0.1 * jax.random.normal(splits[1], (2, D), jnp.float32), 0.5, 1.5)
    w_query = noise(splits[2], (2, D, HEADS * HEAD_DIM), (D * HEAD_DIM) ** -0.5, 0.02734375, ((0, 2), (2, 4)))
    w_key = noise(splits[3], (2, D, HEADS * HEAD_DIM), D ** -0.5, 0.21875, ((0, 2), (2, 4)))
    w_value = noise(splits[4], (2, D, HEADS * HEAD_DIM), D ** -0.5, 0.21875, ((0, 2), (2, 4)))
    w_out = noise(splits[5], (2, HEADS * HEAD_DIM, D), (HEADS * HEAD_DIM // 32) ** -0.5, 1.25, ((0, 2), (1, 4)))
    ffn_gain = jnp.clip(1.0 + 0.1 * jax.random.normal(splits[6], (2, D), jnp.float32), 0.5, 1.5)
    w_gate = noise(splits[7], (2, D, FF), D ** -0.5, 0.21875, ((0, 2), (2, 4)))
    w_up = noise(splits[8], (2, D, FF), D ** -0.5, 0.21875, ((0, 2), (2, 4)))
    w_down = noise(splits[9], (2, FF, D), FF ** -0.5, 0.125, ((0, 2), (1, 4)))
    rel_table = noise(splits[10], (BUCKETS, HEADS), 1.0, 4.0, ((1, 4),), jnp.float32)
    final_gain = jnp.clip(1.0 + 0.1 * jax.random.normal(splits[11], (D,), jnp.float32), 0.5, 1.5)
    w_proj = noise(splits[12], (D, PROJ), D ** -0.5, 0.21875)
    positives = draw_positives(jax.random.fold_in(splits[15], 71), 0)
    retrieved = with_ends(jax.random.randint(splits[14], (NQ, QRY_LEN, TOPK), 0, DOC_TOKENS), jax.random.fold_in(splits[14], 1), 0, DOC_TOKENS - 1).astype(jnp.int32)
    return {"tokens": tokens, "attn_gain": attn_gain, "w_query": w_query, "w_key": w_key, "w_value": w_value, "w_out": w_out, "ffn_gain": ffn_gain, "w_gate": w_gate, "w_up": w_up, "w_down": w_down, "rel_table": rel_table, "final_gain": final_gain, "w_proj": w_proj, "positives": positives, "retrieved": retrieved}


@jax.custom_vjp
def low(v):
    return lax.optimization_barrier(v.astype(jnp.bfloat16)).astype(jnp.float32)

@jax.custom_vjp
def low_back(v):
    return v

def low_keep(v):
    return (low(v), None)

def low_pass(kept, grad):
    return (grad,)

def back_keep(v):
    return (v, None)

def back_low(kept, grad):
    return (low(grad),)
low.defvjp(low_keep, low_pass)
low_back.defvjp(back_keep, back_low)
bucket_edges = (8, 12, 16, 23, 32, 46, 64, 91)
norm_eps = 1e-06
logit_scale = 16.0
highest = lax.Precision.HIGHEST

def bucket_of(length, half_count):
    places = jnp.arange(length, dtype=jnp.int32)
    offset = places[None, :] - places[:, None]
    spread = jnp.abs(offset)
    far_bucket = 7 + sum(((spread >= bucket_edge).astype(jnp.int32) for bucket_edge in bucket_edges))
    near_bucket = jnp.where(spread < 8, spread, far_bucket)
    return near_bucket + half_count * (offset > 0).astype(jnp.int32)

def rms_norm(values, gain_vector):
    return values * lax.rsqrt(lax.optimization_barrier(jnp.mean(values * values, axis=-1, keepdims=True)) + norm_eps) * gain_vector

def matmul(left_side, right_side):
    return jnp.dot(left_side, right_side, precision=highest)

def attend(query_rows, key_rows, value_rows, bias_rows):
    scores = jnp.einsum('bihd,bjhd->bhij', query_rows, key_rows, precision=highest) + bias_rows[None]
    scores = low_back(scores)
    row_peak = lax.optimization_barrier(jnp.max(scores, axis=-1, keepdims=True))
    weights = jnp.exp(scores - row_peak)
    prob_rows = low(weights / lax.optimization_barrier(jnp.sum(weights, axis=-1, keepdims=True)))
    return jnp.einsum('bhij,bjhd->bihd', prob_rows, value_rows, precision=highest)

def self_attend(query_rows, key_rows, value_rows, rel_grid):
    head_count = rel_grid.shape[1]
    doc_rows = DOCS_MB * DOC_LEN
    doc_bias = jnp.moveaxis(rel_grid[bucket_of(DOC_LEN, BUCKETS // 2)], -1, 0)
    qry_bias = jnp.moveaxis(rel_grid[bucket_of(QRY_LEN, BUCKETS // 2)], -1, 0)

    def split_doc(block_rows):
        return block_rows[:doc_rows].reshape(DOCS_MB, DOC_LEN, head_count, HEAD_DIM)

    def split_qry(block_rows):
        return block_rows[doc_rows:].reshape(QRYS_MB, QRY_LEN, head_count, HEAD_DIM)
    doc_mixed = attend(split_doc(query_rows), split_doc(key_rows), split_doc(value_rows), doc_bias)
    qry_mixed = attend(split_qry(query_rows), split_qry(key_rows), split_qry(value_rows), qry_bias)
    return jnp.concatenate([doc_mixed.reshape(doc_rows, head_count * HEAD_DIM), qry_mixed.reshape(QRYS_MB * QRY_LEN, head_count * HEAD_DIM)], axis=0)

def encoder_layer(block_rows, layer_params, rel_grid):
    attn_gain, w_query, w_key, w_value, w_out, ffn_gain, w_gate, w_up, w_down = layer_params
    normed = low(rms_norm(block_rows, attn_gain))
    query_rows = low_back(low(matmul(normed, w_query)))
    key_rows = low_back(low(matmul(normed, w_key)))
    value_rows = low_back(low(matmul(normed, w_value)))
    mixed_rows = low_back(low(self_attend(query_rows, key_rows, value_rows, rel_grid)))
    middle = block_rows + low_back(matmul(mixed_rows, w_out))
    normed_ffn = low(rms_norm(middle, ffn_gain))
    gate_rows = low_back(matmul(normed_ffn, w_gate))
    up_proj = low_back(matmul(normed_ffn, w_up))
    hidden = low(jax.nn.gelu(gate_rows, approximate=True) * up_proj)
    return middle + low_back(matmul(hidden, w_down))

def retrieval_loss(raw_scores, owner_hot, chosen, query_count):
    doc_mass = jnp.einsum('qik,qikd->qid', jnp.exp(raw_scores * PROJ ** (-0.5)), owner_hot, precision=highest)
    doc_logit = logit_scale * lax.optimization_barrier(jnp.mean(jnp.log1p(doc_mass), axis=1))
    row_peak = lax.optimization_barrier(jnp.max(doc_logit, axis=-1, keepdims=True))
    spread = jnp.exp(doc_logit - row_peak)
    all_term = jnp.log(lax.optimization_barrier(jnp.sum(spread, axis=-1)))
    pos_term = jnp.log(lax.optimization_barrier(jnp.sum(chosen * spread, axis=-1)))
    return jnp.sum(all_term - pos_term) / query_count

def reference(tokens, attn_gain, w_query, w_key, w_value, w_out, ffn_gain, w_gate, w_up, w_down, rel_table, final_gain, w_proj, positives, retrieved):
    layer_params = tuple((source_array.astype(jnp.float32) for source_array in (attn_gain, w_query, w_key, w_value, w_out, ffn_gain, w_gate, w_up, w_down)))
    source = tokens.astype(jnp.float32)
    border = jnp.zeros(tokens.shape, jnp.float32)
    rel_grid = rel_table.astype(jnp.float32)
    gain_final = final_gain.astype(jnp.float32)
    projection = w_proj.astype(jnp.float32)
    doc_ids = jnp.arange(NDOC, dtype=jnp.int32)
    owner_hot = ((retrieved // DOC_LEN)[..., None] == doc_ids).astype(jnp.float32)
    chosen = jnp.any(positives[:, :, None] == doc_ids, axis=1).astype(jnp.float32)
    doc_rows = DOCS_MB * DOC_LEN

    def forward(source, border, layer_params, rel_grid, gain_final, projection):

        def both_layers(pair_rows):
            block_rows, extra_rows = pair_rows
            lower_out = encoder_layer(block_rows, tuple((weight[0] for weight in layer_params)), rel_grid)
            middle = low_back(low(lower_out) + extra_rows)
            return encoder_layer(middle, tuple((weight[1] for weight in layer_params)), rel_grid)
        finals = lax.map(jax.checkpoint(both_layers), (source, border))
        doc_hidden = finals[:, :doc_rows].reshape(NDOC * DOC_LEN, D)
        qry_hidden = finals[:, doc_rows:].reshape(NQ * QRY_LEN, D)
        doc_embed = low_back(low(matmul(low(rms_norm(doc_hidden, gain_final)), projection)))
        qry_embed = low_back(low(matmul(low(rms_norm(qry_hidden, gain_final)), projection)))
        qry_embed = qry_embed.reshape(NQ, QRY_LEN, PROJ)
        picked = doc_embed[retrieved]
        raw_scores = jnp.einsum('qip,qikp->qik', qry_embed, picked, precision=highest)
        return retrieval_loss(raw_scores, owner_hot, chosen, NQ)
    loss_value, pull_back = jax.vjp(forward, source, border, layer_params, rel_grid, gain_final, projection)
    grad_source, grad_border, grad_layers, grad_table, grad_gain, grad_proj = pull_back(jnp.ones((), jnp.float32))
    d_inputs = jnp.stack([grad_source, grad_border]).astype(jnp.bfloat16)
    return (loss_value, d_inputs, grad_layers[0], grad_layers[1], grad_layers[2], grad_layers[3], grad_layers[4], grad_layers[5], grad_layers[6], grad_layers[7], grad_layers[8], grad_table, grad_gain, grad_proj)
```

```python
import functools

import jax
import jax.numpy as jnp
from jax import lax
from jax.experimental import pallas as pl
from jax.experimental.pallas import tpu as pltpu
from jax.sharding import PartitionSpec as P

D = 768
HEAD_DIM = 64
FF = 2048
PROJ = 128
DOC_LEN = 512
QRY_LEN = 32
QRYS_MB = 8
QRY_ROWS = QRYS_MB * QRY_LEN
MP = 4
QUARTER = D // MP
FQ = FF // MP
HEADS_Q = QUARTER // HEAD_DIM
BLK = 128
NBLK = DOC_LEN // BLK

bucket_edges = (8, 12, 16, 23, 32, 46, 64, 91)
norm_eps = 1e-06
logit_scale = 16.0
highest = lax.Precision.HIGHEST
f32 = jnp.float32
bf16 = jnp.bfloat16

ACT, IS_DOC, ZPOS, RPOS = range(4)
VMEM_LIMIT = 56 * 1024 * 1024


def mm(a, b):
    return jnp.dot(a, b, preferred_element_type=f32)


def mm_t(a, b):
    return lax.dot_general(a, b, (((1,), (1,)), ((), ())), preferred_element_type=f32)


def t_mm(a, b):
    return lax.dot_general(a, b, (((0,), (0,)), ((), ())), preferred_element_type=f32)


def bucket_of(offset, half_count):
    spread = jnp.abs(offset)
    far_bucket = 7 + sum((spread >= edge).astype(jnp.int32) for edge in bucket_edges)
    near_bucket = jnp.where(spread < 8, spread, far_bucket)
    return near_bucket + half_count * (offset > 0).astype(jnp.int32)


def start_weight_copies(flags, groups, sem):
    z0 = flags[ZPOS]
    r0 = flags[RPOS]
    copies = []
    at = 0
    for owns, slots, place_own, place in groups:
        for k, own in enumerate(owns):
            copies.append(pltpu.make_async_copy(own, place_own(z0, k), sem.at[at]))
            at += 1
        for j, (slot, rbit) in enumerate(zip(slots, (0, 2, 1, 3))):
            for i, zbit in enumerate((2, 1, 3)):
                for src, dst in place(slot.at[i], z0 ^ zbit, r0 ^ rbit):
                    copies.append(pltpu.make_async_copy(src, dst, sem.at[at]))
                    at += 1
    for copy in copies:
        copy.start()
    return copies


def rows_at(index, size):
    return pl.ds(pl.multiple_of(index * size, size), size)


def qkv_group(own, slots, wa):
    return (
        (own,),
        slots,
        lambda z, k: wa.at[z],
        lambda src, z, r: [(src, wa.at[z, rows_at(r, QUARTER), :])],
    )


def ffn_group(own_gate, own_up, slots, wg):
    return (
        (own_gate, own_up),
        slots,
        lambda z, k: wg.at[z, :, pl.ds(k * FQ, FQ)],
        lambda src, z, r: [(src, wg.at[z, rows_at(r, QUARTER), :])],
    )


def down_group(own_down, own_out, slots, wd, wo):
    return (
        (own_down, own_out),
        slots,
        lambda z, k: wd.at[z] if k == 0 else wo.at[z],
        lambda src, z, r: [
            (src.at[pl.ds(0, FQ // 4), :], wd.at[z, rows_at(r, FQ // 4), :]),
            (src.at[pl.ds(FQ // 4, QUARTER // 4), :], wo.at[z, rows_at(r, QUARTER // 4), :]),
        ],
    )


def bias_matrix(bias_ref, table_ref, head, heads):
    far_up = jnp.full((BLK, BLK), table_ref[31, head], f32)
    far_low = jnp.full((BLK, BLK), table_ref[15, head], f32)
    near = {0: bias_ref[head, 0], 1: bias_ref[head, 1], -1: bias_ref[head, 2]}

    def block(bj, bi):
        if bj - bi in near:
            return near[bj - bi]
        return far_up if bj > bi else far_low

    return jnp.concatenate(
        [jnp.concatenate([block(bj, bi) for bi in range(NBLK)], axis=1) for bj in range(NBLK)], axis=0
    )


def rms_parts(values):
    return lax.rsqrt(jnp.mean(values * values, axis=-1, keepdims=True) + norm_eps)


def rms_back(values, gain, grad):
    scale = rms_parts(values)
    weighted = grad * gain
    inner = jnp.mean(values * weighted, axis=-1, keepdims=True)
    out = scale * (weighted - values * (scale * scale * inner))
    gain_grad = jnp.sum(grad * values * scale, axis=0, keepdims=True)
    return out, gain_grad


def attn_fwd_kernel(
    flags, table, x_ref, gain_ref, bias_ref, own, s0, s1, s2, s3,
    normed_ref, qkv_ref, lse_ref, mixed_ref, wa, sem,
):
    heads = MP * HEADS_Q
    copies = start_weight_copies(flags, [qkv_group(own, (s0, s1, s2, s3), wa)], sem)
    x = x_ref[...].astype(f32)
    normed_ref[...] = (x * rms_parts(x) * gain_ref[...]).astype(bf16)
    for copy in copies:
        copy.wait()

    @pl.loop(0, MP)
    def _(z):
        qkv_ref[z] = mm(normed_ref[...], wa[z]).astype(bf16)

    def one_head(z, hh, rows, bias):
        at = hh * HEAD_DIM
        q = qkv_ref[z, rows, at : at + HEAD_DIM]
        k = qkv_ref[z, rows, QUARTER + at : QUARTER + at + HEAD_DIM]
        v = qkv_ref[z, rows, 2 * QUARTER + at : 2 * QUARTER + at + HEAD_DIM]
        scores = mm_t(k, q) + bias
        peak = jnp.max(scores, axis=0, keepdims=True)
        weights = jnp.exp(scores - peak)
        total = jnp.sum(weights, axis=0, keepdims=True)
        mixed = t_mm(v, weights.astype(bf16)) * (1.0 / total)
        lse_ref[z, hh : hh + 1, rows] = peak + jnp.log(total)
        mixed_ref[z, rows, at : at + HEAD_DIM] = mixed.T.astype(bf16)

    @pl.when(flags[IS_DOC] == 1)
    def _():
        @pl.loop(0, MP)
        def _(z):
            for hh in range(HEADS_Q):
                one_head(z, hh, slice(0, DOC_LEN), bias_matrix(bias_ref, table, z * HEADS_Q + hh, heads))

    @pl.when(flags[IS_DOC] == 0)
    def _():
        mixed_ref[...] = jnp.zeros_like(mixed_ref)
        lse_ref[...] = jnp.zeros_like(lse_ref)

        @pl.loop(0, MP)
        def _(z):
            for hh in range(HEADS_Q):
                for b in range(QRY_ROWS // BLK):
                    one_head(z, hh, slice(b * BLK, (b + 1) * BLK), bias_ref[z * HEADS_Q + hh, 0])


def ffn_fwd_kernel(
    flags, x_ref, mixed_ref, gain_ref, own_gate, own_up, g0, g1, g2, g3, own_down, own_out, d0, d1, d2, d3,
    out_ref, middle_ref, normed_ref, hidden_ref, ga_ref, gb_ref, wg, wd, wo, sem,
):
    copies = start_weight_copies(
        flags,
        [
            down_group(own_down, own_out, (d0, d1, d2, d3), wd, wo),
            ffn_group(own_gate, own_up, (g0, g1, g2, g3), wg),
        ],
        sem,
    )
    for copy in copies:
        copy.wait()
    middle = x_ref[...].astype(f32)
    for z in range(MP):
        middle = middle + mm(mixed_ref[z], wo[z])
    middle_ref[...] = middle
    normed_ref[...] = (middle * rms_parts(middle) * gain_ref[...]).astype(bf16)
    out_ref[...] = middle

    @pl.loop(0, MP)
    def _(z):
        normed = normed_ref[...]
        gate = mm(normed, wg[z, :, :FQ])
        up = mm(normed, wg[z, :, FQ:])
        coef = 0.7978845608028654
        square = gate * gate
        tanh = jnp.tanh(coef * gate * (1.0 + 0.044715 * square))
        half = 0.5 + 0.5 * tanh
        gelu = gate * half
        slope = half + (0.5 * coef) * gate * (1.0 - tanh * tanh) * (1.0 + 3 * 0.044715 * square)
        hidden = (gelu * up).astype(bf16)
        hidden_ref[z] = hidden
        ga_ref[z] = (up * slope).astype(bf16)
        gb_ref[z] = gelu.astype(bf16)
        out_ref[...] += mm(hidden, wd[z])


def ffn_bwd_kernel(
    flags, gout_ref, middle_ref, gain_ref, normed_ref, hidden_ref, ga_ref, gb_ref,
    own_gate, own_up, g0, g1, g2, g3, own_down, own_out, d0, d1, d2, d3,
    *refs,
):
    prev, refs = refs[:-16], refs[-16:]
    gmid_ref, dgain_ref, dgk, dgs, ddk, dds, wg, wd, wo, goutb, normed_t, dg_buf, dd_buf, gn, sem, osem = refs

    @pl.when(flags[ACT] == 0)
    def _():
        dgain_ref[...] = prev[0][...] if prev else jnp.zeros_like(dgain_ref)
        gmid_ref[...] = jnp.zeros_like(gmid_ref)

    @pl.when(flags[ACT] == 1)
    def _():
        core = flags[RPOS] % 2
        copies = start_weight_copies(
            flags,
            [
                down_group(own_down, own_out, (d0, d1, d2, d3), wd, wo),
                ffn_group(own_gate, own_up, (g0, g1, g2, g3), wg),
            ],
            sem,
        )
        goutb[...] = gout_ref[...].astype(bf16)
        normed_t[...] = normed_ref[...].T
        gn[...] = jnp.zeros_like(gn)
        for copy in copies:
            copy.wait()

        def outs(z):
            half_g, half_d = D // 2, FQ // 2
            return (
                pltpu.make_async_copy(dg_buf.at[z % 2, rows_at(core, half_g), :], dgk.at[z], osem.at[z % 2, 0]),
                pltpu.make_async_copy(dg_buf.at[z % 2, rows_at(1 - core, half_g), :], dgs.at[z], osem.at[z % 2, 1]),
                pltpu.make_async_copy(dd_buf.at[z % 2, rows_at(core, half_d), :], ddk.at[z], osem.at[z % 2, 2]),
                pltpu.make_async_copy(dd_buf.at[z % 2, rows_at(1 - core, half_d), :], dds.at[z], osem.at[z % 2, 3]),
            )

        for z in range(MP):
            if z >= 2:
                for copy in outs(z - 2):
                    copy.wait()
            grad_hidden = mm_t(goutb[...], wd[z])
            grad_gate = (grad_hidden * ga_ref[z].astype(f32)).astype(bf16)
            grad_up = (grad_hidden * gb_ref[z].astype(f32)).astype(bf16)
            dd_buf[z % 2] = t_mm(hidden_ref[z], goutb[...]).astype(bf16)
            dg_buf[z % 2, :, :FQ] = mm(normed_t[...], grad_gate).astype(bf16)
            dg_buf[z % 2, :, FQ:] = mm(normed_t[...], grad_up).astype(bf16)
            for copy in outs(z):
                copy.start()
            gn[...] += mm_t(grad_gate, wg[z, :, :FQ]) + mm_t(grad_up, wg[z, :, FQ:])
        back, gain_grad = rms_back(middle_ref[...], gain_ref[...], gn[...])
        gmid_ref[...] = gout_ref[...] + back
        dgain_ref[...] = gain_grad
        for z in (MP - 2, MP - 1):
            for copy in outs(z):
                copy.wait()


def attn_bwd_kernel(
    flags, table, gmid_ref, x_ref, gain_ref, bias_ref, normed_ref, qkv_ref, lse_ref, mixed_ref,
    own, s0, s1, s2, s3, own_out, d0, d1, d2, d3,
    *refs,
):
    prev, refs = refs[:-18], refs[-18:]
    gx_ref, dgain_ref, diag_ref, dak, das, dok, dos = refs[:7]
    wa, wo, gmb, normed_t, gmix, gqkv, da_buf, do_buf, gn, sem, osem = refs[7:]
    heads = MP * HEADS_Q

    @pl.when(flags[ACT] == 0)
    def _():
        for at, ref in enumerate((gx_ref, dgain_ref, diag_ref)):
            ref[...] = prev[at][...] if prev else jnp.zeros_like(ref)

    def out_group():
        return (
            (own_out,),
            (d0, d1, d2, d3),
            lambda z, k: wo.at[z],
            lambda src, z, r: [(src.at[pl.ds(FQ // 4, QUARTER // 4), :], wo.at[z, rows_at(r, QUARTER // 4), :])],
        )

    def one_head(z, hh, rows, bias):
        at = hh * HEAD_DIM
        q = qkv_ref[z, rows, at : at + HEAD_DIM]
        k = qkv_ref[z, rows, QUARTER + at : QUARTER + at + HEAD_DIM]
        v = qkv_ref[z, rows, 2 * QUARTER + at : 2 * QUARTER + at + HEAD_DIM]
        go = gmix[rows, at : at + HEAD_DIM]
        out = mixed_ref[z, rows, at : at + HEAD_DIM].astype(f32)
        delta = jnp.sum((go.astype(f32) * out).T, axis=0, keepdims=True)
        probs = jnp.exp(mm_t(k, q) + bias - lse_ref[z, hh : hh + 1, rows])
        grad_probs = mm_t(v, go)
        grad_scores = probs * (grad_probs - delta)
        low = grad_scores.astype(bf16)
        gqkv[z, rows, at : at + HEAD_DIM] = t_mm(k, low).T.astype(bf16)
        gqkv[z, rows, QUARTER + at : QUARTER + at + HEAD_DIM] = mm(low, q).astype(bf16)
        gqkv[z, rows, 2 * QUARTER + at : 2 * QUARTER + at + HEAD_DIM] = mm(probs.astype(bf16), go).astype(bf16)
        return grad_scores

    def band_sums(up, mid, low):
        blank = jnp.zeros((BLK, BLK), f32)
        band = jnp.concatenate([up, mid, low, blank], axis=1)
        width = 4 * BLK

        def left(part, by):
            return pltpu.roll(part, width - by, 1) if by else part

        eight = functools.reduce(jnp.add, [left(band[g : g + 8], g) for g in range(0, BLK, 8)])
        return functools.reduce(jnp.add, [left(eight[r : r + 1], r) for r in range(8)])

    @pl.when(flags[ACT] == 1)
    def _():
        core = flags[RPOS] % 2
        copies = start_weight_copies(
            flags, [out_group(), qkv_group(own, (s0, s1, s2, s3), wa)], sem
        )
        gmb[...] = gmid_ref[...].astype(bf16)
        normed_t[...] = normed_ref[...].T
        gn[...] = jnp.zeros_like(gn)
        for copy in copies:
            copy.wait()

        def outs(z):
            half_a, half_o = D // 2, QUARTER // 2
            return (
                pltpu.make_async_copy(da_buf.at[z % 2, rows_at(core, half_a), :], dak.at[z], osem.at[z % 2, 0]),
                pltpu.make_async_copy(da_buf.at[z % 2, rows_at(1 - core, half_a), :], das.at[z], osem.at[z % 2, 1]),
                pltpu.make_async_copy(do_buf.at[z % 2, rows_at(core, half_o), :], dok.at[z], osem.at[z % 2, 2]),
                pltpu.make_async_copy(do_buf.at[z % 2, rows_at(1 - core, half_o), :], dos.at[z], osem.at[z % 2, 3]),
            )

        for z in range(MP):
            if z >= 2:
                for copy in outs(z - 2):
                    copy.wait()
            gmix[...] = mm_t(gmb[...], wo[z]).astype(bf16)
            do_buf[z % 2] = t_mm(mixed_ref[z], gmb[...]).astype(bf16)

            @pl.when(flags[IS_DOC] == 1)
            def _():
                for hh in range(HEADS_Q):
                    grads = one_head(
                        z, hh, slice(0, DOC_LEN), bias_matrix(bias_ref, table, z * HEADS_Q + hh, heads)
                    )

                    def blocks(test):
                        picked = [
                            grads[bj * BLK : (bj + 1) * BLK, bi * BLK : (bi + 1) * BLK]
                            for bj in range(NBLK)
                            for bi in range(NBLK)
                            if test(bj - bi)
                        ]
                        return functools.reduce(jnp.add, picked)

                    sums = band_sums(blocks(lambda d: d == 1), blocks(lambda d: d == 0), blocks(lambda d: d == -1))
                    far_up = jnp.sum(blocks(lambda d: d > 1), axis=0, keepdims=True)
                    far_low = jnp.sum(blocks(lambda d: d < -1), axis=0, keepdims=True)
                    diag_ref[z, hh : hh + 1, :] = jnp.concatenate([sums, far_up, far_low], axis=1)

            @pl.when(flags[IS_DOC] == 0)
            def _():
                gqkv[z] = jnp.zeros((DOC_LEN, 3 * QUARTER), bf16)
                for hh in range(HEADS_Q):
                    grads = jnp.zeros((BLK, BLK), f32)
                    for b in range(QRY_ROWS // BLK):
                        grads = grads + one_head(
                            z, hh, slice(b * BLK, (b + 1) * BLK), bias_ref[z * HEADS_Q + hh, 0]
                        )
                    blank = jnp.zeros((BLK, BLK), f32)
                    sums = band_sums(blank, grads, blank)
                    diag_ref[z, hh : hh + 1, :] = jnp.concatenate([sums, jnp.zeros((1, 2 * BLK), f32)], axis=1)

            grads = gqkv[z]
            da_buf[z % 2] = mm(normed_t[...], grads).astype(bf16)
            for copy in outs(z):
                copy.start()
            gn[...] += mm_t(grads, wa[z])
        back, gain_grad = rms_back(x_ref[...].astype(f32), gain_ref[...], gn[...])
        gx_ref[...] = (gmid_ref[...] + back).astype(bf16)
        dgain_ref[...] = gain_grad
        for z in (MP - 2, MP - 1):
            for copy in outs(z):
                copy.wait()


def vmem():
    return pl.BlockSpec(memory_space=pltpu.VMEM)


def smem():
    return pl.BlockSpec(memory_space=pltpu.SMEM)


def hbm():
    return pl.BlockSpec(memory_space=pl.ANY)


def shape(dims, kind):
    return jax.ShapeDtypeStruct(dims, kind)


def params():
    return pltpu.CompilerParams(vmem_limit_bytes=VMEM_LIMIT)


def attn_fwd(flags, table, x, gain, bias, wa_parts):
    return pl.pallas_call(
        attn_fwd_kernel,
        in_specs=[smem(), smem()] + [vmem()] * 3 + [hbm()] * 5,
        out_specs=[vmem()] * 4,
        out_shape=[
            shape((DOC_LEN, D), bf16),
            shape((MP, DOC_LEN, 3 * QUARTER), bf16),
            shape((MP, 8, DOC_LEN), f32),
            shape((MP, DOC_LEN, QUARTER), bf16),
        ],
        scratch_shapes=[pltpu.VMEM((MP, D, 3 * QUARTER), bf16), pltpu.SemaphoreType.DMA((13,))],
        compiler_params=params(),
        name="attn_fwd",
    )(flags, table, x, gain, bias, *wa_parts)


def ffn_fwd(flags, x, mixed, gain, wg_parts, wd_parts):
    quarter = (MP, DOC_LEN, FQ)
    return pl.pallas_call(
        ffn_fwd_kernel,
        in_specs=[smem()] + [vmem()] * 3 + [hbm()] * 12,
        out_specs=[vmem()] * 6,
        out_shape=[
            shape((DOC_LEN, D), f32),
            shape((DOC_LEN, D), f32),
            shape((DOC_LEN, D), bf16),
            shape(quarter, bf16),
            shape(quarter, bf16),
            shape(quarter, bf16),
        ],
        scratch_shapes=[
            pltpu.VMEM((MP, D, 2 * FQ), bf16),
            pltpu.VMEM((MP, FQ, D), bf16),
            pltpu.VMEM((MP, QUARTER, D), bf16),
            pltpu.SemaphoreType.DMA((40,)),
        ],
        compiler_params=params(),
        name="ffn_fwd",
    )(flags, x, mixed, gain, *wg_parts, *wd_parts)


def ffn_bwd(flags, gout, middle, gain, normed, hidden, ga, gb, wg_parts, wd_parts, prev):
    n_in = 8 + 12
    big = [
        shape((MP, D // 2, 2 * FQ), bf16),
        shape((MP, D // 2, 2 * FQ), bf16),
        shape((MP, FQ // 2, D), bf16),
        shape((MP, FQ // 2, D), bf16),
    ]
    prev = prev or []
    return pl.pallas_call(
        ffn_bwd_kernel,
        in_specs=[smem()] + [vmem()] * 7 + [hbm()] * 12 + ([vmem()] + [hbm()] * 4 if prev else []),
        out_specs=[vmem()] * 2 + [hbm()] * 4,
        out_shape=[shape((DOC_LEN, D), f32), shape((1, D), f32)] + big,
        input_output_aliases={n_in + 1 + i: 2 + i for i in range(4)} if prev else {},
        scratch_shapes=[
            pltpu.VMEM((MP, D, 2 * FQ), bf16),
            pltpu.VMEM((MP, FQ, D), bf16),
            pltpu.VMEM((MP, QUARTER, D), bf16),
            pltpu.VMEM((DOC_LEN, D), bf16),
            pltpu.VMEM((D, DOC_LEN), bf16),
            pltpu.VMEM((2, D, 2 * FQ), bf16),
            pltpu.VMEM((2, FQ, D), bf16),
            pltpu.VMEM((DOC_LEN, D), f32),
            pltpu.SemaphoreType.DMA((40,)),
            pltpu.SemaphoreType.DMA((2, 4)),
        ],
        compiler_params=params(),
        name="ffn_bwd",
    )(flags, gout, middle, gain, normed, hidden, ga, gb, *wg_parts, *wd_parts, *prev)


def attn_bwd(flags, table, gmid, x, gain, bias, normed, qkv, lse, mixed, wa_parts, wo_parts, prev):
    n_in = 10 + 10
    small = [shape((DOC_LEN, D), bf16), shape((1, D), f32), shape((MP, 8, 6 * BLK), f32)]
    big = [
        shape((MP, D // 2, 3 * QUARTER), bf16),
        shape((MP, D // 2, 3 * QUARTER), bf16),
        shape((MP, QUARTER // 2, D), bf16),
        shape((MP, QUARTER // 2, D), bf16),
    ]
    prev = prev or []
    return pl.pallas_call(
        attn_bwd_kernel,
        in_specs=[smem()] * 2 + [vmem()] * 8 + [hbm()] * 10 + ([vmem()] * 3 + [hbm()] * 4 if prev else []),
        out_specs=[vmem()] * 3 + [hbm()] * 4,
        out_shape=small + big,
        input_output_aliases={n_in + 3 + i: 3 + i for i in range(4)} if prev else {},
        scratch_shapes=[
            pltpu.VMEM((MP, D, 3 * QUARTER), bf16),
            pltpu.VMEM((MP, QUARTER, D), bf16),
            pltpu.VMEM((DOC_LEN, D), bf16),
            pltpu.VMEM((D, DOC_LEN), bf16),
            pltpu.VMEM((DOC_LEN, QUARTER), bf16),
            pltpu.VMEM((MP, DOC_LEN, 3 * QUARTER), bf16),
            pltpu.VMEM((2, D, 3 * QUARTER), bf16),
            pltpu.VMEM((2, QUARTER, D), bf16),
            pltpu.VMEM((DOC_LEN, D), f32),
            pltpu.SemaphoreType.DMA((26,)),
            pltpu.SemaphoreType.DMA((2, 4)),
        ],
        compiler_params=params(),
        name="attn_bwd",
    )(flags, table, gmid, x, gain, bias, normed, qkv, lse, mixed, *wa_parts, *wo_parts, *prev)


def swap(values, axis, bit):
    count = lax.axis_size(axis)
    return lax.ppermute(values, axis, [(i, i ^ bit) for i in range(count)])


def gather_pieces(piece):
    far = swap(piece, "mp", 2)
    near = swap(jnp.stack([piece, far]), "mp", 1)
    mine = jnp.concatenate([far[None], near])
    across = swap(mine, "dp", 2)
    return (mine, across, swap(mine, "dp", 1), swap(across, "dp", 1))


def pick(values, axis, index):
    return lax.dynamic_index_in_dim(values, index, axis, keepdims=False)


def add_low(a, b):
    return (a.astype(f32) + b.astype(f32)).astype(bf16)


def split_step(values, dim, axis, bit, mine):
    return add_low(pick(values, dim, mine), swap(pick(values, dim, 1 - mine), axis, bit))


def join_step(values, axis, bit, mine):
    other = swap(values, axis, bit)
    return jnp.where(mine == 0, jnp.stack([values, other]), jnp.stack([other, values]))


def reduce_chunk(keep, send, place, y_first):
    core, y, z = place
    total = add_low(keep, swap(send, "dp", 1))
    total = total.reshape(2, 2, 2, total.shape[1] // 2, total.shape[2])
    if y_first:
        total = split_step(total, 2, "dp", 2, y)
    total = split_step(total, 1, "mp", 1, z % 2)
    total = split_step(total, 0, "mp", 2, z // 2)
    if not y_first:
        total = add_low(total, swap(total, "dp", 2))
    bit = 4
    while bit < lax.axis_size("dp"):
        total = add_low(total, swap(total, "dp", bit))
        bit *= 2
    if y_first:
        total = join_step(total, "dp", 2, y)
    return join_step(total, "dp", 1, core)


def spread_tokens(tokens, place, pairs):
    core, _, z = place
    got = []
    for turn in range(2):
        perm = []
        for j in range(pairs):
            for c in range(2):
                for zz in range(MP):
                    u = (turn + zz) % 2
                    perm.append(((2 * j + c) * MP + zz, (2 * j + zz // 2) * MP + 2 * c + u))
        block = pick(tokens, 0, (turn + z) % 2)
        got.append(lax.ppermute(block, ("dp", "mp"), perm))
    low, high = jnp.where(z % 2 == 0, jnp.stack(got), jnp.stack(got[::-1]))
    cut = DOC_LEN - 2 * QUARTER
    tail = swap(low[:cut], "dp", 1)
    doc = jnp.concatenate([low, high, tail])
    qry = jnp.concatenate([low[cut:], high, jnp.zeros((DOC_LEN - QRY_ROWS, D), low.dtype)])
    return jnp.where(core == 0, doc, qry)


def collect_rows(rows, place, pairs):
    core, _, z = place
    cut = DOC_LEN - 2 * QUARTER
    tail = swap(rows[2 * QUARTER :], "dp", 1)
    low_q = jnp.concatenate([tail, rows[: QUARTER - cut]])
    high_q = rows[QUARTER - cut : QRY_ROWS]
    low = jnp.where(core == 0, rows[:QUARTER], low_q)
    high = jnp.where(core == 0, rows[QUARTER : 2 * QUARTER], high_q)
    got = []
    for turn in range(2):
        perm = []
        for j in range(pairs):
            for c in range(2):
                for zz in range(MP):
                    u = (turn + zz) % 2
                    perm.append(((2 * j + zz // 2) * MP + 2 * c + u, (2 * j + c) * MP + zz))
        block = jnp.where((z + turn) % 2 == 0, low, high)
        got.append(lax.ppermute(block, ("dp", "mp"), perm))
    return jnp.where(z % 2 == 0, jnp.stack(got), jnp.stack(got[::-1]))


def gather_slots(values, steps):
    for axis, bit in steps:
        values = jnp.concatenate([values, swap(values, axis, bit)])
    return values


def scatter_slots(values, steps):
    for axis, bit in reversed(steps):
        half = values.shape[0] // 2
        values = add_low(values[:half], swap(values[half:], axis, bit))
    return values[0]


def on_device(
    tokens,
    attn_gain,
    w_query,
    w_key,
    w_value,
    w_out,
    ffn_gain,
    w_gate,
    w_up,
    w_down,
    rel_table,
    final_gain,
    w_proj,
    positives,
    retrieved,
):
    section = lax.axis_index("section")
    dp = lax.axis_index("dp")
    dp_count = lax.axis_size("dp")
    z = lax.axis_index("mp")
    core, y = dp % 2, (dp // 2) % 2
    place = (core, y, z)
    pairs = dp_count // 2
    chip = (dp // 2) * MP + z
    chips = pairs * MP
    is_doc = core == 0
    first = section == 0
    quad = dp % 4

    qkv_own = jnp.concatenate([w_query[0], w_key[0], w_value[0]], axis=1)
    qkv_piece = lax.dynamic_slice_in_dim(qkv_own, quad * QUARTER, QUARTER, 0)
    gate_piece = jnp.concatenate(
        [lax.dynamic_slice_in_dim(w[0], quad * QUARTER, QUARTER, 0) for w in (w_gate, w_up)], axis=1
    )
    down_piece = jnp.concatenate(
        [
            lax.dynamic_slice_in_dim(w_down[0], quad * (FQ // 4), FQ // 4, 0),
            lax.dynamic_slice_in_dim(w_out[0], quad * (QUARTER // 4), QUARTER // 4, 0),
        ]
    )
    x_first = spread_tokens(tokens, place, pairs)
    wa_parts = (qkv_own,) + gather_pieces(qkv_piece)
    down_slots = gather_pieces(down_piece)
    wg_parts = (w_gate[0], w_up[0]) + gather_pieces(gate_piece)
    wd_parts = (w_down[0], w_out[0]) + down_slots
    wo_parts = (w_out[0],) + down_slots

    heads_dev = rel_table.shape[1]
    buckets = rel_table.shape[0]
    half_count = buckets // 2
    table = lax.all_gather(rel_table, "mp", axis=1, tiled=True)
    at = jnp.arange(BLK, dtype=jnp.int32)
    offset = at[:, None] - at[None, :]
    offsets = jnp.stack([offset, offset + BLK, offset - BLK])
    bucket_ids = jnp.arange(buckets, dtype=jnp.int32)
    pick_near = (bucket_of(offsets, half_count)[..., None] == bucket_ids).astype(f32)
    bias = jnp.einsum("bh,mjib->hmji", table, pick_near, precision=highest)
    same_query = (at[:, None] // QRY_LEN) == (at[None, :] // QRY_LEN)
    bias = jnp.where(jnp.logical_or(is_doc, same_query), bias, -1e30)

    def flags_for(active):
        return jnp.stack([jnp.asarray(active).astype(jnp.int32), is_doc.astype(jnp.int32), z, quad])

    slot_ids = jnp.arange(chips, dtype=jnp.int32)
    mb_of_slot = chip ^ slot_ids
    all_retrieved = lax.all_gather(retrieved, "dp", axis=0, tiled=True)
    all_positives = lax.all_gather(positives, "dp", axis=0, tiled=True)
    topk = retrieved.shape[2]
    slot_retrieved = jnp.take(all_retrieved.reshape(chips, QRY_ROWS, topk), mb_of_slot, axis=0)
    places = jnp.arange(DOC_LEN, dtype=jnp.int32) + chip * DOC_LEN
    counts = jnp.sum(
        (slot_retrieved.reshape(-1, topk)[:, :, None] == places).astype(f32), axis=1
    )

    flags_f = flags_for(1)
    kept = []
    x = x_first
    for step in range(2):
        normed, qkv, lse, mixed = attn_fwd(flags_f, table, x, attn_gain, bias, wa_parts)
        out, middle, normed_ffn, hidden, ga, gb = ffn_fwd(flags_f, x, mixed, ffn_gain, wg_parts, wd_parts)
        kept.append((x, normed, qkv, lse, mixed, middle, normed_ffn, hidden, ga, gb))
        if step == 0:
            x = lax.ppermute(out.astype(bf16), "section", [(0, 1)])

    scale = PROJ ** (-0.5)
    normed_final = (out * rms_parts(out) * final_gain).astype(bf16)
    embed = mm(normed_final, w_proj).astype(bf16)
    steps = [("mp", 1), ("mp", 2)]
    bit = 2
    while bit < dp_count:
        steps.append(("dp", bit))
        bit *= 2
    query_slots = swap(gather_slots(embed[None, :QRY_ROWS], steps), "dp", 1).reshape(-1, PROJ)
    sims = mm_t(query_slots, embed)
    weighted = jnp.exp(sims * scale) * counts
    mass = jnp.sum(weighted, axis=1)
    logit = logit_scale * jnp.mean(jnp.log1p(mass).reshape(chips * QRYS_MB, QRY_LEN), axis=1)
    logit = jnp.take(logit.reshape(chips, QRYS_MB), mb_of_slot, axis=0).reshape(1, -1)
    logits = gather_slots(logit, steps)
    chosen = jnp.any(all_positives[None] == mb_of_slot[:, None, None], axis=2).astype(f32)
    peak = jnp.max(logits, axis=0)
    spread = jnp.exp(logits - peak)
    all_total = jnp.sum(spread, axis=0)
    pos_total = jnp.sum(chosen * spread, axis=0)
    n_queries = logits.shape[1]
    loss_here = jnp.sum(jnp.log(all_total) - jnp.log(pos_total)) / n_queries
    grad_logit = (spread[0] / all_total - chosen[0] * spread[0] / pos_total) / n_queries
    grad_logit = jnp.take(grad_logit.reshape(chips, QRYS_MB), mb_of_slot, axis=0).reshape(-1)
    coef = jnp.repeat(grad_logit * (logit_scale / QRY_LEN * scale), QRY_LEN) / (1.0 + mass)
    grad_sims = (weighted * coef[:, None]).astype(bf16)
    grad_doc = t_mm(grad_sims, query_slots).astype(bf16)
    grad_query = mm(grad_sims, embed).astype(bf16).reshape(chips, QRY_ROWS, PROJ)
    grad_query = scatter_slots(swap(grad_query, "dp", 1), steps)
    grad_query = jnp.concatenate([grad_query, jnp.zeros((DOC_LEN - QRY_ROWS, PROJ), bf16)])
    grad_embed = jnp.where(is_doc, grad_doc, grad_query)
    grad_proj = t_mm(normed_final, grad_embed)
    grad_final, grad_final_gain = rms_back(out, final_gain, mm_t(grad_embed, w_proj))
    live = jnp.logical_not(first)
    lead = jnp.logical_and(live, jnp.logical_and(dp == 0, z == 0))
    early = jnp.concatenate(
        [
            jnp.where(live, grad_proj, 0.0),
            jnp.where(live, grad_final_gain, 0.0).reshape(-1, PROJ),
            jnp.full((2, PROJ), jnp.where(lead, loss_here, 0.0)),
        ]
    )
    early = lax.psum(early, ("section", "dp", "mp"))

    grad_out = grad_final
    ffn_prev = attn_prev = None
    for step in (1, 0):
        x, normed, qkv, lse, mixed, middle, normed_ffn, hidden, ga, gb = kept[step]
        flags_b = flags_for(section == step)
        gmid, *ffn_prev = ffn_bwd(
            flags_b, grad_out, middle, ffn_gain, normed_ffn, hidden, ga, gb, wg_parts, wd_parts, ffn_prev
        )
        attn_prev = attn_bwd(
            flags_b, table, gmid, x, attn_gain, bias, normed, qkv, lse, mixed, wa_parts, wo_parts, attn_prev
        )
        if step == 1:
            grad_out = lax.ppermute(attn_prev[0], "section", [(1, 0)]).astype(f32)
    grad_ffn_gain, dgk, dgs, ddk, dds = ffn_prev
    gx, grad_attn_gain, diag, dak, das, dok, dos = attn_prev

    sum_gate = reduce_chunk(dgk, dgs, place, True).reshape(D, 2 * FQ)
    sum_down = reduce_chunk(ddk, dds, place, False).reshape(FQ, D)
    lanes = jnp.arange(4 * BLK, dtype=jnp.int32)
    band_offset = jnp.where(lanes <= 2 * BLK + BLK - 1, BLK - lanes, 5 * BLK - lanes)
    band_bucket = jnp.concatenate(
        [
            bucket_of(band_offset, half_count),
            jnp.full((BLK,), buckets - 1, jnp.int32),
            jnp.full((BLK,), half_count - 1, jnp.int32),
        ]
    )
    pick_band = (band_bucket[:, None] == bucket_ids).astype(f32)
    table_part = jnp.einsum("zhc,cb->zhb", diag[:, :heads_dev], pick_band, precision=highest)
    table_part = table_part + swap(table_part, "section", 1)
    small = jnp.concatenate(
        [
            jnp.broadcast_to(grad_attn_gain[None], (MP, 1, D)),
            jnp.broadcast_to(grad_ffn_gain[None], (MP, 1, D)),
            jnp.pad(table_part.reshape(MP, 1, -1), ((0, 0), (0, 0), (0, D - heads_dev * buckets))),
            jnp.zeros((MP, 13, D), f32),
        ],
        axis=1,
    ).astype(bf16)
    small = jnp.broadcast_to(small[:, None], (MP, 2, 16, D))

    def with_small(values):
        parts = values.reshape(MP, 2, QUARTER // 4, D)
        return jnp.concatenate([parts, small], axis=2).reshape(MP, -1, D)

    sum_out = reduce_chunk(with_small(dok), with_small(dos), place, False)
    sum_qkv = reduce_chunk(dak, das, place, True).reshape(D, 3 * QUARTER).astype(f32)
    small_sum = sum_out[0, 0, QUARTER // 4 :].astype(f32)
    sum_out = sum_out[:, :, : QUARTER // 4].reshape(QUARTER, D).astype(f32)
    grad_table = small_sum[2, : heads_dev * buckets].reshape(heads_dev, buckets).T
    d_inputs = collect_rows(gx, place, pairs)[None]
    col_width = w_proj.shape[1] // MP
    sum_gate = sum_gate.astype(f32)
    return (
        early[-1, 0],
        d_inputs,
        small_sum[0:1],
        sum_qkv[None, :, :QUARTER],
        sum_qkv[None, :, QUARTER : 2 * QUARTER],
        sum_qkv[None, :, 2 * QUARTER :],
        sum_out[None],
        small_sum[1:2],
        sum_gate[None, :, :FQ],
        sum_gate[None, :, FQ:],
        sum_down.astype(f32)[None],
        grad_table,
        early[D : D + D // PROJ].reshape(D),
        lax.dynamic_slice_in_dim(early[:D], z * col_width, col_width, 1),
    )


def solution(mesh):
    return jax.shard_map(
        on_device,
        mesh=mesh,
        in_specs=(
            P("dp", "mp", None),
            P("section", None),
            P("section", None, "mp"),
            P("section", None, "mp"),
            P("section", None, "mp"),
            P("section", "mp", None),
            P("section", None),
            P("section", None, "mp"),
            P("section", None, "mp"),
            P("section", "mp", None),
            P(None, "mp"),
            P(),
            P(),
            P("dp", None),
            P("dp", None, None),
        ),
        out_specs=(
            P(),
            P("section", "dp", "mp", None),
            P("section", None),
            P("section", None, "mp"),
            P("section", None, "mp"),
            P("section", None, "mp"),
            P("section", "mp", None),
            P("section", None),
            P("section", None, "mp"),
            P("section", None, "mp"),
            P("section", "mp", None),
            P(None, "mp"),
            P(),
            P(None, "mp"),
        ),
        check_vma=False,
    )
```

```python
import functools

import jax
import jax.numpy as jnp
from jax import lax
from jax.experimental import pallas as pl
from jax.experimental.pallas import tpu as pltpu
from jax.sharding import PartitionSpec as P

D = 768
HEAD_DIM = 64
FF = 2048
PROJ = 128
DOC_LEN = 512
QRY_LEN = 32
QRYS_MB = 8
QRY_ROWS = QRYS_MB * QRY_LEN
MP = 4
QUARTER = D // MP
FQ = FF // MP
HEADS_Q = QUARTER // HEAD_DIM
BLK = 128
NBLK = DOC_LEN // BLK
PAD = 64
SMALL = 32
F_HALF = 3 * FQ // 2
A_HALF = D // 2

bucket_edges = (8, 12, 16, 23, 32, 46, 64, 91)
norm_eps = 1e-06
logit_scale = 16.0
highest = lax.Precision.HIGHEST
f32 = jnp.float32
bf16 = jnp.bfloat16

ACT, IS_DOC, ZPOS, RPOS = range(4)
VMEM_LIMIT = 56 * 1024 * 1024


def mm(a, b):
    return jnp.dot(a, b, preferred_element_type=f32)


def mm_t(a, b):
    return lax.dot_general(a, b, (((1,), (1,)), ((), ())), preferred_element_type=f32)


def t_mm(a, b):
    return lax.dot_general(a, b, (((0,), (0,)), ((), ())), preferred_element_type=f32)


def bucket_of(offset, half_count):
    spread = jnp.abs(offset)
    far_bucket = 7 + sum((spread >= edge).astype(jnp.int32) for edge in bucket_edges)
    near_bucket = jnp.where(spread < 8, spread, far_bucket)
    return near_bucket + half_count * (offset > 0).astype(jnp.int32)


class Copies:
    def __init__(self, sem, first=0):
        self.sem = sem
        self.next = first

    def __call__(self, source, target):
        copy = pltpu.make_async_copy(source, target, self.sem.at[self.next])
        self.next += 1
        copy.start()
        return copy


def wait_all(copies):
    for copy in copies:
        copy.wait()


def weights_of(pieces, lanes, target, sem, z):
    return [
        pltpu.make_async_copy(pieces.at[r, z, :, lanes], target.at[z, pl.ds(r * QUARTER, QUARTER), :], sem.at[z, r])
        for r in range(4)
    ]


def start_all(copies):
    for copy in copies:
        copy.start()


ATTN_LANES = pl.ds(0, D)
FFN_LANES = pl.ds(D, 3 * FQ)


def rows_at(index, size):
    return pl.ds(pl.multiple_of(index * size, size), size)


def bias_matrix(bias_ref, table_ref, head):
    far_up = jnp.full((BLK, BLK), table_ref[31, head], f32)
    far_low = jnp.full((BLK, BLK), table_ref[15, head], f32)
    near = {0: bias_ref[head, 0], 1: bias_ref[head, 1], -1: bias_ref[head, 2]}

    def block(bj, bi):
        if bj - bi in near:
            return near[bj - bi]
        return far_up if bj > bi else far_low

    return jnp.concatenate(
        [jnp.concatenate([block(bj, bi) for bi in range(NBLK)], axis=1) for bj in range(NBLK)], axis=0
    )


def rms_parts(values):
    return lax.rsqrt(jnp.mean(values * values, axis=-1, keepdims=True) + norm_eps)


def rms_back(values, gain, grad):
    scale = rms_parts(values)
    weighted = grad * gain
    inner = jnp.mean(values * weighted, axis=-1, keepdims=True)
    out = scale * (weighted - values * (scale * scale * inner))
    gain_grad = jnp.sum(grad * values * scale, axis=0, keepdims=True)
    return out, gain_grad


def by_kind(flags, body):
    pl.when(flags[IS_DOC] == 1)(lambda: body(DOC_LEN, True))
    pl.when(flags[IS_DOC] == 0)(lambda: body(QRY_ROWS, False))


def head_slices(hh):
    at = hh * HEAD_DIM
    return (
        slice(at, at + HEAD_DIM),
        slice(QUARTER + at, QUARTER + at + HEAD_DIM),
        slice(2 * QUARTER + at, 2 * QUARTER + at + HEAD_DIM),
        slice(PAD + at, PAD + at + HEAD_DIM),
    )


def layer_fwd_kernel(
    flags, table, attn_gain_ref, ffn_gain_ref, x_hbm, bias_hbm, pieces,
    normed_out, qkv_out, lse_out, mixed_out, out_out, low_out, middle_out, normed_ffn_out, hidden_out, ga_out, gb_out,
    x_ref, bias_ref, normed_ref, qkv_ref, lse_ref, mixed_ref, out_ref, low_ref, middle_ref, normed_ffn_ref,
    hidden_ref, ga_ref, gb_ref, wa, wf, sem, asem, fsem, zsem,
):
    copy = Copies(sem)
    get_x = copy(x_hbm, x_ref)
    start_all(weights_of(pieces, ATTN_LANES, wa, asem, 0))
    get_bias = copy(bias_hbm, bias_ref)
    for z in range(1, MP):
        start_all(weights_of(pieces, ATTN_LANES, wa, asem, z))
    get_x.wait()
    first_out = copy.next

    def one_head(z, hh, rows, bias):
        qs, ks, vs, ms = head_slices(hh)
        q, k, v = qkv_ref[z, rows, qs], qkv_ref[z, rows, ks], qkv_ref[z, rows, vs]
        scores = mm_t(k, q) + bias
        peak = jnp.max(scores, axis=0, keepdims=True)
        weights = jnp.exp(scores - peak)
        total = jnp.sum(weights, axis=0, keepdims=True)
        mixed = t_mm(v, weights.astype(bf16)) * (1.0 / total)
        lse_ref[z, hh : hh + 1, rows] = peak + jnp.log(total)
        mixed_ref[z, rows, ms] = mixed.T.astype(bf16)

    def body(rows, doc):
        put = Copies(sem, first_out)
        outs = []

        def send(source, target):
            outs.append(put(source.at[pl.ds(0, rows)], target.at[pl.ds(0, rows)]))

        def parts(z, pairs, at):
            return [
                pltpu.make_async_copy(a.at[z, pl.ds(0, rows)], b.at[z, pl.ds(0, rows)], zsem.at[z, at + i])
                for i, (a, b) in enumerate(pairs)
            ]

        attn_outs = ((qkv_ref, qkv_out), (mixed_ref, mixed_out))
        ffn_outs = ((hidden_ref, hidden_out), (ga_ref, ga_out), (gb_ref, gb_out))
        x = x_ref[:rows].astype(f32)
        normed_ref[:rows] = (x * rms_parts(x) * attn_gain_ref[...]).astype(bf16)
        send(normed_ref, normed_out)
        get_bias.wait()

        @pl.loop(0, MP)
        def _(z):
            wait_all(weights_of(pieces, ATTN_LANES, wa, asem, z))
            start_all(weights_of(pieces, FFN_LANES, wf, fsem, z))
            qkv_ref[z, :rows] = mm(normed_ref[:rows], wa[z]).astype(bf16)
            mixed_ref[z, :rows, :PAD] = jnp.zeros((rows, PAD), bf16)
            for hh in range(HEADS_Q):
                head = z * HEADS_Q + hh
                if doc:
                    one_head(z, hh, slice(0, DOC_LEN), bias_matrix(bias_ref, table, head))
                else:
                    for b in range(QRY_ROWS // BLK):
                        one_head(z, hh, slice(b * BLK, (b + 1) * BLK), bias_ref[head, 0])
            start_all(parts(z, attn_outs, 0))

        outs.append(put(lse_ref, lse_out))
        middle_ref[:rows] = x_ref[:rows].astype(f32)

        @pl.loop(0, MP)
        def _(z):
            middle_ref[:rows] += mm_t(mixed_ref[z, :rows], wa[z, :, 2 * QUARTER + PAD + PAD :])

        middle = middle_ref[:rows]
        send(middle_ref, middle_out)
        normed_ffn_ref[:rows] = (middle * rms_parts(middle) * ffn_gain_ref[...]).astype(bf16)
        send(normed_ffn_ref, normed_ffn_out)
        out_ref[:rows] = middle

        @pl.loop(0, MP)
        def _(z):
            wait_all(weights_of(pieces, FFN_LANES, wf, fsem, z))
            normed = normed_ffn_ref[:rows]
            gate = mm(normed, wf[z, :, :FQ])
            up = mm(normed, wf[z, :, FQ : 2 * FQ])
            coef = 0.7978845608028654
            square = gate * gate
            tanh = jnp.tanh(coef * gate * (1.0 + 0.044715 * square))
            half = 0.5 + 0.5 * tanh
            gelu = gate * half
            slope = half + (0.5 * coef) * gate * (1.0 - tanh * tanh) * (1.0 + 3 * 0.044715 * square)
            hidden = (gelu * up).astype(bf16)
            hidden_ref[z, :rows] = hidden
            ga_ref[z, :rows] = (up * slope).astype(bf16)
            gb_ref[z, :rows] = gelu.astype(bf16)
            start_all(parts(z, ffn_outs, 2))
            out_ref[:rows] += mm_t(hidden, wf[z, :, 2 * FQ :])

        low_ref[:rows] = out_ref[:rows].astype(bf16)
        if not doc:
            out_ref[rows:] = jnp.zeros((DOC_LEN - rows, D), f32)
        outs.append(put(out_ref, out_out))
        send(low_ref, low_out)

        @pl.loop(0, MP)
        def _(z):
            wait_all(parts(z, attn_outs, 0))
            wait_all(parts(z, ffn_outs, 2))

        wait_all(outs)

    by_kind(flags, body)


def ffn_bwd_kernel(
    flags, gain_ref, gout_hbm, middle_hbm, normed_hbm, hidden_hbm, ga_hbm, gb_hbm, pieces,
    *refs,
):
    gmid_out, dgain_out, *df_outs = refs[-22:-16]
    gout_ref, middle_ref, normed_ref, hidden_ref, ga_ref, gb_ref, gmid_ref, dgain_ref = refs[-16:-8]
    wf, gout_t, normed_t, df_buf, gn, sem, fsem, osem = refs[-8:]

    def outs(z, core):
        slot, half = z % 2, D // 2
        copies = []
        for i, out in enumerate(df_outs):
            rows = pl.ds((core if i % 2 == 0 else 1 - core) * half, half)
            lanes = pl.ds(i // 2 * F_HALF, F_HALF)
            copies.append(pltpu.make_async_copy(df_buf.at[slot, rows, lanes], out.at[z], osem.at[slot, i]))
        return copies

    def body(rows, doc):
        core = 0 if doc else 1
        copy = Copies(sem)

        def get(source, target):
            return copy(source.at[pl.ds(0, rows)], target.at[pl.ds(0, rows)])

        get_gout = get(gout_hbm, gout_ref)
        get_normed = get(normed_hbm, normed_ref)
        kept = ((ga_hbm, ga_ref), (gb_hbm, gb_ref), (hidden_hbm, hidden_ref))

        def part(z):
            return weights_of(pieces, FFN_LANES, wf, fsem, z) + [
                pltpu.make_async_copy(a.at[z, pl.ds(0, rows)], b.at[z, pl.ds(0, rows)], fsem.at[z, 4 + i])
                for i, (a, b) in enumerate(kept)
            ]

        start_all(part(0))
        get_middle = get(middle_hbm, middle_ref)
        get_gout.wait()
        gout_t[:, :rows] = gout_ref[:rows].T
        get_normed.wait()
        normed_t[:, :rows] = normed_ref[:rows].T
        gn[:rows] = jnp.zeros((rows, D), f32)

        @pl.loop(0, MP)
        def _(z):
            pl.when(z >= 2)(lambda: wait_all(outs(z - 2, core)))
            pl.when(z + 1 < MP)(lambda: start_all(part(z + 1)))
            wait_all(part(z))
            slot = z % 2
            grad_hidden = mm(gout_ref[:rows], wf[z, :, 2 * FQ :])
            grad_gate = (grad_hidden * ga_ref[z, :rows].astype(f32)).astype(bf16)
            grad_up = (grad_hidden * gb_ref[z, :rows].astype(f32)).astype(bf16)
            df_buf[slot, :, :FQ] = mm(normed_t[:, :rows], grad_gate).astype(bf16)
            df_buf[slot, :, FQ : 2 * FQ] = mm(normed_t[:, :rows], grad_up).astype(bf16)
            df_buf[slot, :, 2 * FQ :] = mm(gout_t[:, :rows], hidden_ref[z, :rows]).astype(bf16)
            start_all(outs(z, core))
            gn[:rows] += mm_t(grad_gate, wf[z, :, :FQ]) + mm_t(grad_up, wf[z, :, FQ : 2 * FQ])

        get_middle.wait()
        back, gain_grad = rms_back(middle_ref[:rows], gain_ref[...], gn[:rows])
        gmid_ref[:rows] = gout_ref[:rows].astype(f32) + back
        dgain_ref[...] = gain_grad
        last = [copy(gmid_ref.at[pl.ds(0, rows)], gmid_out.at[pl.ds(0, rows)]), copy(dgain_ref, dgain_out)]
        for z in (MP - 2, MP - 1):
            wait_all(outs(z, core))
        wait_all(last)

    @pl.when(flags[ACT] == 1)
    def _():
        by_kind(flags, body)


def attn_bwd_kernel(
    flags, table, gain_ref, gmid_hbm, x_hbm, bias_hbm, normed_hbm, qkv_hbm, lse_hbm, mixed_hbm, pieces,
    *refs,
):
    gx_out, dgain_out, diag_out, *da_outs = refs[-28:-21]
    gmid_ref, x_ref, bias_ref, normed_ref, qkv_ref, lse_ref, mixed_ref, gx_ref, dgain_ref, diag_ref = refs[-21:-11]
    wa, gmb, gmid_t, normed_t, gmix, gqkv, da_buf, gn, sem, asem, osem = refs[-11:]

    def one_head(z, hh, rows, bias):
        qs, ks, vs, ms = head_slices(hh)
        q, k, v = qkv_ref[z, rows, qs], qkv_ref[z, rows, ks], qkv_ref[z, rows, vs]
        go = gmix[rows, ms]
        out = mixed_ref[z, rows, ms].astype(f32)
        delta = jnp.sum((go.astype(f32) * out).T, axis=0, keepdims=True)
        probs = jnp.exp(mm_t(k, q) + bias - lse_ref[z, hh : hh + 1, rows])
        grad_scores = probs * (mm_t(v, go) - delta)
        low = grad_scores.astype(bf16)
        gqkv[rows, qs] = t_mm(k, low).T.astype(bf16)
        gqkv[rows, ks] = mm(low, q).astype(bf16)
        gqkv[rows, vs] = mm(probs.astype(bf16), go).astype(bf16)
        return grad_scores

    def band_sums(up, mid, low):
        blank = jnp.zeros((BLK, BLK), f32)
        band = jnp.concatenate([up, mid, low, blank], axis=1)
        width = 4 * BLK

        def left(part, by):
            return pltpu.roll(part, width - by, 1) if by else part

        eight = functools.reduce(jnp.add, [left(band[g : g + 8], g) for g in range(0, BLK, 8)])
        return functools.reduce(jnp.add, [left(eight[r : r + 1], r) for r in range(8)])

    def outs(z, core):
        slot = z % 2
        copies = []
        for i, out in enumerate(da_outs):
            for half in range(2):
                rows = pl.ds((core if i % 2 == 0 else 1 - core) * (D // 2) + half * QUARTER, QUARTER)
                lanes = pl.ds(i // 2 * A_HALF, A_HALF)
                target = out.at[z, half, pl.ds(0, QUARTER), :]
                copies.append(pltpu.make_async_copy(da_buf.at[slot, rows, lanes], target, osem.at[slot, 2 * i + half]))
        return copies

    def body(rows, doc):
        core = 0 if doc else 1
        tail = 2 * QUARTER + PAD + PAD
        copy = Copies(sem)

        def get(source, target):
            return copy(source.at[pl.ds(0, rows)], target.at[pl.ds(0, rows)])

        get_gmid = get(gmid_hbm, gmid_ref)
        get_lse = copy(lse_hbm, lse_ref)
        kept = ((qkv_hbm, qkv_ref), (mixed_hbm, mixed_ref))

        def part(z):
            return weights_of(pieces, ATTN_LANES, wa, asem, z) + [
                pltpu.make_async_copy(a.at[z, pl.ds(0, rows)], b.at[z, pl.ds(0, rows)], asem.at[z, 4 + i])
                for i, (a, b) in enumerate(kept)
            ]

        start_all(part(0))
        get_bias = copy(bias_hbm, bias_ref)
        get_normed = get(normed_hbm, normed_ref)
        get_x = get(x_hbm, x_ref)
        get_gmid.wait()
        gmb[:rows] = gmid_ref[:rows].astype(bf16)
        gmid_t[:, :rows] = gmb[:rows].T
        gqkv[:rows, 3 * QUARTER :] = jnp.zeros((rows, QUARTER), bf16)
        gn[:rows] = jnp.zeros((rows, D), f32)
        get_lse.wait()
        get_normed.wait()
        normed_t[:, :rows] = normed_ref[:rows].T
        get_bias.wait()

        @pl.loop(0, MP)
        def _(z):
            pl.when(z >= 2)(lambda: wait_all(outs(z - 2, core)))
            pl.when(z + 1 < MP)(lambda: start_all(part(z + 1)))
            wait_all(part(z))
            slot = z % 2
            gmix[:rows] = mm(gmb[:rows], wa[z, :, tail:]).astype(bf16)
            for hh in range(HEADS_Q):
                head = z * HEADS_Q + hh
                if doc:
                    grads = one_head(z, hh, slice(0, DOC_LEN), bias_matrix(bias_ref, table, head))

                    def blocks(test):
                        picked = [
                            grads[bj * BLK : (bj + 1) * BLK, bi * BLK : (bi + 1) * BLK]
                            for bj in range(NBLK)
                            for bi in range(NBLK)
                            if test(bj - bi)
                        ]
                        return functools.reduce(jnp.add, picked)

                    sums = band_sums(blocks(lambda d: d == 1), blocks(lambda d: d == 0), blocks(lambda d: d == -1))
                    far_up = jnp.sum(blocks(lambda d: d > 1), axis=0, keepdims=True)
                    far_low = jnp.sum(blocks(lambda d: d < -1), axis=0, keepdims=True)
                    diag_ref[z, hh : hh + 1, :] = jnp.concatenate([sums, far_up, far_low], axis=1)
                else:
                    grads = jnp.zeros((BLK, BLK), f32)
                    for b in range(QRY_ROWS // BLK):
                        grads = grads + one_head(z, hh, slice(b * BLK, (b + 1) * BLK), bias_ref[head, 0])
                    blank = jnp.zeros((BLK, BLK), f32)
                    sums = band_sums(blank, grads, blank)
                    diag_ref[z, hh : hh + 1, :] = jnp.concatenate([sums, jnp.zeros((1, 2 * BLK), f32)], axis=1)
            grads = gqkv[:rows]
            main = mm(normed_t[:, :rows], grads)
            extra = mm(gmid_t[:, :rows], mixed_ref[z, :rows])
            da_buf[slot, :, :tail] = main[:, :tail].astype(bf16)
            da_buf[slot, :, tail:] = (main[:, tail:] + extra).astype(bf16)
            start_all(outs(z, core))
            gn[:rows] += mm_t(grads, wa[z])

        get_x.wait()
        back, gain_grad = rms_back(x_ref[:rows].astype(f32), gain_ref[...], gn[:rows])
        gx_ref[:rows] = (gmid_ref[:rows] + back).astype(bf16)
        dgain_ref[...] = gain_grad
        last = [
            copy(gx_ref.at[pl.ds(0, rows)], gx_out.at[pl.ds(0, rows)]),
            copy(dgain_ref, dgain_out),
            copy(diag_ref, diag_out),
        ]
        for z in (MP - 2, MP - 1):
            wait_all(outs(z, core))
        wait_all(last)

    @pl.when(flags[ACT] == 1)
    def _():
        by_kind(flags, body)


def put_all(refs):
    count = len(refs) // 2
    copies = [pltpu.make_async_copy(refs[count + i], refs[i], refs[-1].at[i]) for i in range(count)]
    start_all(copies)
    wait_all(copies)


def finish_ffn_kernel(flags, mine1, other1, mine2, other2, *refs):
    gate_ref, up_ref, down_ref = refs[3:6]
    core = flags[RPOS] % 2
    half = D // 2
    for side, first, second in ((core, mine1, mine2), (1 - core, other1, other2)):
        rows = rows_at(side, half)
        low = first[...].reshape(half, F_HALF).astype(f32)
        high = second[...].reshape(half, F_HALF).astype(f32)
        gate_ref[rows, :] = low[:, :FQ]
        up_ref[rows, : F_HALF - FQ] = low[:, FQ:]
        up_ref[rows, F_HALF - FQ :] = high[:, : 2 * FQ - F_HALF]
        down = high[:, 2 * FQ - F_HALF :].T

        @pl.when(side == 0)
        def _():
            down_ref[:, :half] = down

        @pl.when(side == 1)
        def _():
            down_ref[:, half:] = down

    put_all(refs)


def finish_attn_kernel(flags, mine1, other1, mine2, other2, *refs):
    q_ref, k_ref, v_ref, o_ref = refs[4:8]
    core = flags[RPOS] % 2
    half = D // 2
    for side, first, second in ((core, mine1, mine2), (1 - core, other1, other2)):
        rows = rows_at(side, half)
        low = first[...].reshape(half, A_HALF).astype(f32)
        high = second[:, :QUARTER].reshape(half, A_HALF).astype(f32)
        q_ref[rows, :] = low[:, :QUARTER]
        k_ref[rows, :] = low[:, QUARTER:]
        v_ref[rows, :] = high[:, :QUARTER]
        out = high[:, QUARTER:].T

        @pl.when(side == 0)
        def _():
            o_ref[:, :half] = out

        @pl.when(side == 1)
        def _():
            o_ref[:, half:] = out

    put_all(refs)


def vmem():
    return pl.BlockSpec(memory_space=pltpu.VMEM)


def smem():
    return pl.BlockSpec(memory_space=pltpu.SMEM)


def hbm():
    return pl.BlockSpec(memory_space=pl.ANY)


def shape(dims, kind):
    return jax.ShapeDtypeStruct(dims, kind)


def params():
    return pltpu.CompilerParams(vmem_limit_bytes=VMEM_LIMIT)


def cost(microseconds):
    return pl.CostEstimate(flops=int(microseconds * 1e9), bytes_accessed=16 * 1024 * 1024, transcendentals=0)


def count_kernel(flags, hits_ref, counts_ref):
    @pl.when(flags[ACT] == 1)
    def _():
        places = lax.broadcasted_iota(jnp.int32, counts_ref.shape, 1)
        hits = hits_ref[...]
        total = jnp.zeros(counts_ref.shape, f32)
        for k in range(hits.shape[1]):
            total = total + (hits[:, k : k + 1] == places).astype(f32)
        counts_ref[...] = total

    @pl.when(flags[ACT] == 0)
    def _():
        counts_ref[...] = jnp.zeros_like(counts_ref)


def count_hits(flags, hits):
    rows, topk = hits.shape
    block = min(rows, 128)
    return pl.pallas_call(
        count_kernel,
        grid=(rows // block,),
        in_specs=[smem(), pl.BlockSpec((block, topk), lambda i: (i, 0))],
        out_specs=pl.BlockSpec((block, DOC_LEN), lambda i: (i, 0)),
        out_shape=shape((rows, DOC_LEN), f32),
        compiler_params=params(),
        cost_estimate=cost(10),
        name="count_hits",
    )(flags, hits)


QUARTERS = (MP, DOC_LEN, FQ)
ROWS = (DOC_LEN, D)


def on_vmem(shapes):
    return [pltpu.VMEM(s.shape, s.dtype) for s in shapes]


def layer_fwd(flags, table, x, attn_gain, ffn_gain, bias, pieces):
    results = [
        shape(ROWS, bf16),
        shape((MP, DOC_LEN, D), bf16),
        shape((MP, 8, DOC_LEN), f32),
        shape((MP, DOC_LEN, PAD + QUARTER), bf16),
        shape(ROWS, f32),
        shape(ROWS, bf16),
        shape(ROWS, f32),
        shape(ROWS, bf16),
        shape(QUARTERS, bf16),
        shape(QUARTERS, bf16),
        shape(QUARTERS, bf16),
    ]
    return pl.pallas_call(
        layer_fwd_kernel,
        in_specs=[smem()] * 2 + [vmem()] * 2 + [hbm()] * 3,
        out_specs=[hbm()] * 11,
        out_shape=results,
        scratch_shapes=on_vmem([shape(ROWS, bf16), shape(bias.shape, f32)] + results)
        + [
            pltpu.VMEM((MP, D, D), bf16),
            pltpu.VMEM((MP, D, 3 * FQ), bf16),
            pltpu.SemaphoreType.DMA((8,)),
            pltpu.SemaphoreType.DMA((MP, 4)),
            pltpu.SemaphoreType.DMA((MP, 4)),
            pltpu.SemaphoreType.DMA((MP, 5)),
        ],
        compiler_params=params(),
        cost_estimate=cost(25),
        name="layer_fwd",
    )(flags, table, attn_gain, ffn_gain, x, bias, pieces)


def finish(kernel, flags, results, *values):
    return pl.pallas_call(
        kernel,
        in_specs=[smem()] + [vmem()] * 4,
        out_specs=[hbm()] * len(results),
        out_shape=[shape(r, f32) for r in results],
        scratch_shapes=on_vmem([shape(r, f32) for r in results]) + [pltpu.SemaphoreType.DMA((len(results),))],
        compiler_params=params(),
        cost_estimate=cost(3),
        name="finish",
    )(flags, *values)


def ffn_bwd(flags, gout, middle, gain, normed, hidden, ga, gb, pieces, prev):
    results = [shape(ROWS, f32), shape((1, D), f32)]
    results += [shape((MP, D // 2, F_HALF), bf16)] * 4
    prev = prev or []
    return pl.pallas_call(
        ffn_bwd_kernel,
        in_specs=[smem(), vmem()] + [hbm()] * (7 + len(prev)),
        out_specs=[hbm()] * 6,
        out_shape=results,
        input_output_aliases={9 + i: 1 + i for i in range(len(prev))},
        scratch_shapes=on_vmem([shape(ROWS, bf16), shape(ROWS, f32), shape(ROWS, bf16)] + [shape(QUARTERS, bf16)] * 3)
        + on_vmem(results[:2])
        + [
            pltpu.VMEM((MP, D, 3 * FQ), bf16),
            pltpu.VMEM((D, DOC_LEN), bf16),
            pltpu.VMEM((D, DOC_LEN), bf16),
            pltpu.VMEM((2, D, 3 * FQ), bf16),
            pltpu.VMEM(ROWS, f32),
            pltpu.SemaphoreType.DMA((8,)),
            pltpu.SemaphoreType.DMA((MP, 7)),
            pltpu.SemaphoreType.DMA((2, 4)),
        ],
        compiler_params=params(),
        cost_estimate=cost(20),
        name="ffn_bwd",
    )(flags, gain, gout, middle, normed, hidden, ga, gb, pieces, *prev)


def attn_bwd(flags, table, gmid, x, gain, bias, normed, qkv, lse, mixed, pieces, prev):
    results = [shape(ROWS, bf16), shape((1, D), f32), shape((MP, 8, 6 * BLK), f32)]
    results += [shape((MP, 2, QUARTER, A_HALF), bf16)] * 2 + [shape((MP, 2, QUARTER + SMALL, A_HALF), bf16)] * 2
    prev = prev or []
    held = (gmid, x, bias, normed, qkv, lse, mixed)
    return pl.pallas_call(
        attn_bwd_kernel,
        in_specs=[smem()] * 2 + [vmem()] + [hbm()] * (8 + len(prev)),
        out_specs=[hbm()] * 7,
        out_shape=results,
        input_output_aliases={11 + i: i for i in range(len(prev))},
        scratch_shapes=on_vmem(held)
        + on_vmem(results[:3])
        + [
            pltpu.VMEM((MP, D, D), bf16),
            pltpu.VMEM(ROWS, bf16),
            pltpu.VMEM((D, DOC_LEN), bf16),
            pltpu.VMEM((D, DOC_LEN), bf16),
            pltpu.VMEM((DOC_LEN, PAD + QUARTER), bf16),
            pltpu.VMEM(ROWS, bf16),
            pltpu.VMEM((2, D, D), bf16),
            pltpu.VMEM(ROWS, f32),
            pltpu.SemaphoreType.DMA((8,)),
            pltpu.SemaphoreType.DMA((MP, 6)),
            pltpu.SemaphoreType.DMA((2, 8)),
        ],
        compiler_params=params(),
        cost_estimate=cost(25),
        name="attn_bwd",
    )(flags, table, gain, gmid, x, bias, normed, qkv, lse, mixed, pieces, *prev)


def swap(values, axis, bit):
    count = lax.axis_size(axis)
    return lax.ppermute(values, axis, [(i, i ^ bit) for i in range(count)])


def swap_cores(values, axis, bit, core):
    dp_count, mp_count = lax.axis_size("dp"), lax.axis_size("mp")
    perm = []
    for i in range(core, dp_count, 2):
        for j in range(mp_count):
            to = (i ^ bit) * mp_count + j if axis == "dp" else i * mp_count + (j ^ bit)
            perm.append((i * mp_count + j, to))
    return lax.ppermute(values, ("dp", "mp"), perm)


def hop(rows, source):
    first = lax.ppermute(rows[:QRY_ROWS], "section", [(source, 1 - source)])
    dp_count = lax.axis_size("dp")
    perm = [(source * dp_count + i, (1 - source) * dp_count + i) for i in range(0, dp_count, 2)]
    return jnp.concatenate([first, lax.ppermute(rows[QRY_ROWS:], ("section", "dp"), perm)])


def gather_all(piece, quad, z):
    if lax.axis_size("dp") == 4:
        return lax.all_gather(piece, ("dp", "mp")).reshape(4, MP, *piece.shape)
    pieces = piece[None]
    for axis, bit in (("mp", 1), ("mp", 2), ("dp", 1), ("dp", 2)):
        pieces = jnp.concatenate([pieces, swap(pieces, axis, bit)])
    return jnp.take(pieces, (quad * MP + z) ^ jnp.arange(4 * MP), axis=0).reshape(4, MP, *piece.shape)


def pick(values, axis, index):
    return lax.dynamic_index_in_dim(values, index, axis, keepdims=False)


def add_low(a, b):
    return (a.astype(f32) + b.astype(f32)).astype(bf16)


def fence(*values):
    return lax.optimization_barrier(values)


def total_of(terms):
    return functools.reduce(jnp.add, [term.astype(f32) for term in terms]).astype(bf16)


def give(terms, dim, axis, bit, mine):
    return swap(total_of([pick(term, dim, 1 - mine) for term in terms]), axis, bit)


def take(terms, dim, mine, got):
    return [pick(term, dim, mine) for term in terms] + [got]


def in_order(mine, values, other):
    return jnp.where(mine == 0, jnp.stack([values, other]), jnp.stack([other, values]))


def over_rest(total):
    bit = 4
    while bit < lax.axis_size("dp"):
        total = add_low(total, swap(total, "dp", bit))
        bit *= 2
    return total


def spread_tokens(tokens, place, pairs):
    core, _, z = place
    got = []
    for turn in range(2):
        perm = []
        for j in range(pairs):
            for c in range(2):
                for zz in range(MP):
                    u = (turn + zz) % 2
                    perm.append(((2 * j + c) * MP + zz, (2 * j + zz // 2) * MP + 2 * c + u))
        block = pick(tokens, 0, (turn + z) % 2)
        got.append(lax.ppermute(block, ("dp", "mp"), perm))
    low, high = jnp.where(z % 2 == 0, jnp.stack(got), jnp.stack(got[::-1]))
    cut = DOC_LEN - 2 * QUARTER
    tail = swap(low[:cut], "dp", 1)
    doc = jnp.concatenate([low, high, tail])
    qry = jnp.concatenate([low[cut:], high, jnp.zeros((DOC_LEN - QRY_ROWS, D), low.dtype)])
    return jnp.where(core == 0, doc, qry)


def collect_rows(rows, place, pairs):
    core, _, z = place
    cut = DOC_LEN - 2 * QUARTER
    tail = swap(rows[2 * QUARTER :], "dp", 1)
    low_q = jnp.concatenate([tail, rows[: QUARTER - cut]])
    high_q = rows[QUARTER - cut : QRY_ROWS]
    low = jnp.where(core == 0, rows[:QUARTER], low_q)
    high = jnp.where(core == 0, rows[QUARTER : 2 * QUARTER], high_q)
    got = []
    for turn in range(2):
        perm = []
        for j in range(pairs):
            for c in range(2):
                for zz in range(MP):
                    u = (turn + zz) % 2
                    perm.append(((2 * j + zz // 2) * MP + 2 * c + u, (2 * j + c) * MP + zz))
        block = jnp.where((z + turn) % 2 == 0, low, high)
        got.append(lax.ppermute(block, ("dp", "mp"), perm))
    return jnp.where(z % 2 == 0, jnp.stack(got), jnp.stack(got[::-1]))


def gather_slots(values, steps, core):
    for axis, bit in steps:
        values = jnp.concatenate([values, swap_cores(values, axis, bit, core)])
    return values


def scatter_slots(values, steps, core):
    for axis, bit in reversed(steps):
        half = values.shape[0] // 2
        values = add_low(values[:half], swap_cores(values[half:], axis, bit, core))
    return values[0]


def on_device(
    tokens,
    attn_gain,
    w_query,
    w_key,
    w_value,
    w_out,
    ffn_gain,
    w_gate,
    w_up,
    w_down,
    rel_table,
    final_gain,
    w_proj,
    positives,
    retrieved,
):
    section = lax.axis_index("section")
    dp = lax.axis_index("dp")
    dp_count = lax.axis_size("dp")
    z = lax.axis_index("mp")
    core, y = dp % 2, (dp // 2) % 2
    place = (core, y, z)
    pairs = dp_count // 2
    chip = (dp // 2) * MP + z
    chips = pairs * MP
    is_doc = core == 0
    first = section == 0
    quad = dp % 4

    rows = [lax.dynamic_slice_in_dim(w[0], quad * QUARTER, QUARTER, 0) for w in (w_query, w_key, w_value)]
    rows.append(lax.dynamic_slice_in_dim(w_out[0], quad * QUARTER, QUARTER, 1).T)
    rows += [lax.dynamic_slice_in_dim(w[0], quad * QUARTER, QUARTER, 0) for w in (w_gate, w_up)]
    rows.append(lax.dynamic_slice_in_dim(w_down[0], quad * QUARTER, QUARTER, 1).T)
    pieces = gather_all(jnp.concatenate(rows, axis=1), quad, z)
    x_first = spread_tokens(tokens, place, pairs)

    heads_dev = rel_table.shape[1]
    buckets = rel_table.shape[0]
    half_count = buckets // 2
    table = jnp.stack([rel_table, swap(rel_table, "mp", 1)])
    table = jnp.concatenate([table, swap(table, "mp", 2)])
    table = jnp.take(table, z ^ jnp.arange(MP), axis=0)
    table = jnp.swapaxes(table, 0, 1).reshape(rel_table.shape[0], -1)
    at = jnp.arange(BLK, dtype=jnp.int32)
    offset = at[:, None] - at[None, :]
    offsets = jnp.stack([offset, offset + BLK, offset - BLK])
    bucket_ids = jnp.arange(buckets, dtype=jnp.int32)
    pick_near = (bucket_of(offsets, half_count)[..., None] == bucket_ids).astype(f32)
    bias = jnp.einsum("bh,mjib->hmji", table, pick_near, precision=highest)
    same_query = (at[:, None] // QRY_LEN) == (at[None, :] // QRY_LEN)
    bias = jnp.where(jnp.logical_or(is_doc, same_query), bias, -1e30)

    def flags_for(active):
        return jnp.stack([jnp.asarray(active).astype(jnp.int32), is_doc.astype(jnp.int32), z, quad])

    slot_ids = jnp.arange(chips, dtype=jnp.int32)
    mb_of_slot = chip ^ slot_ids
    topk = retrieved.shape[2]
    hits = jnp.concatenate([retrieved.reshape(retrieved.shape[0], -1), positives], axis=1)[None]
    bit = 1
    while bit < dp_count:
        hits = jnp.concatenate([hits, swap(hits, "dp", bit)])
        bit *= 2
    hits = jnp.take(hits, dp ^ jnp.arange(dp_count), axis=0).reshape(chips * QRYS_MB, -1)
    all_positives = hits[:, QRY_LEN * topk :]
    slot_retrieved = jnp.take(hits[:, : QRY_LEN * topk].reshape(chips, QRY_ROWS, topk), mb_of_slot, axis=0)
    counts = count_hits(flags_for(jnp.logical_not(first)), slot_retrieved.reshape(-1, topk) - chip * DOC_LEN)
    x_first, counts = lax.optimization_barrier((x_first, counts))

    flags_f = flags_for(1)
    kept = []
    x = x_first
    for step in range(2):
        normed, qkv, lse, mixed, out, low, middle, normed_ffn, hidden, ga, gb = layer_fwd(
            flags_f, table, x, attn_gain, ffn_gain, bias, pieces
        )
        kept.append((x, normed, qkv, lse, mixed, middle, normed_ffn, hidden, ga, gb))
        if step == 0:
            x = hop(low, 0)

    scale = PROJ ** (-0.5)
    normed_final = (out * rms_parts(out) * final_gain).astype(bf16)
    embed = mm(normed_final, w_proj).astype(bf16)
    steps = [("mp", 1), ("mp", 2)]
    bit = 2
    while bit < dp_count:
        steps.append(("dp", bit))
        bit *= 2
    query_slots = swap(gather_slots(embed[None, :QRY_ROWS], steps, 1), "dp", 1).reshape(-1, PROJ)
    sims = mm_t(query_slots, embed)
    weighted = jnp.exp(sims * scale) * counts
    mass = jnp.sum(weighted, axis=1)
    logit = logit_scale * jnp.mean(jnp.log1p(mass).reshape(chips * QRYS_MB, QRY_LEN), axis=1)
    logit = jnp.take(logit.reshape(chips, QRYS_MB), mb_of_slot, axis=0).reshape(1, -1)
    logits = gather_slots(logit, steps, 0)
    chosen = jnp.any(all_positives[None] == mb_of_slot[:, None, None], axis=2).astype(f32)
    peak = jnp.max(logits, axis=0)
    spread = jnp.exp(logits - peak)
    all_total = jnp.sum(spread, axis=0)
    pos_total = jnp.sum(chosen * spread, axis=0)
    n_queries = logits.shape[1]
    loss_here = jnp.sum(jnp.log(all_total) - jnp.log(pos_total)) / n_queries
    grad_logit = (spread[0] / all_total - chosen[0] * spread[0] / pos_total) / n_queries
    grad_logit = jnp.take(grad_logit.reshape(chips, QRYS_MB), mb_of_slot, axis=0).reshape(-1)
    coef = jnp.repeat(grad_logit * (logit_scale / QRY_LEN * scale), QRY_LEN) / (1.0 + mass)
    grad_sims = (weighted * coef[:, None]).astype(bf16)
    grad_doc = t_mm(grad_sims, query_slots).astype(bf16)
    grad_query = mm(grad_sims, embed).astype(bf16).reshape(chips, QRY_ROWS, PROJ)
    grad_query = scatter_slots(swap(grad_query, "dp", 1), steps, 1)
    grad_query = jnp.concatenate([grad_query, jnp.zeros((DOC_LEN - QRY_ROWS, PROJ), bf16)])
    grad_embed = jnp.where(is_doc, grad_doc, grad_query)
    grad_final, grad_final_gain = rms_back(out, final_gain, mm_t(grad_embed, w_proj))
    live = jnp.logical_not(first)
    lead = jnp.logical_and(live, jnp.logical_and(dp == 0, z == 0))
    loss_here = jnp.where(lead, loss_here, 0.0)
    loss_high = loss_here.astype(bf16)
    loss_low = (loss_here - loss_high.astype(f32)).astype(bf16)
    early = jnp.concatenate(
        [
            t_mm(grad_embed, normed_final).astype(bf16),
            grad_final_gain.astype(bf16),
            jnp.full((1, D), loss_high),
            jnp.full((1, D), loss_low),
        ]
    )
    early = jnp.where(live, early, 0.0)
    early = early + swap(early, "section", 1)

    def ffn_back(step, grad_out, prev):
        x, normed, qkv, lse, mixed, middle, normed_ffn, hidden, ga, gb = kept[step]
        flags = flags_for(section == step)
        return ffn_bwd(flags, grad_out, middle, ffn_gain, normed_ffn, hidden, ga, gb, pieces, prev)

    def attn_back(step, gmid, prev):
        x, normed, qkv, lse, mixed, middle, normed_ffn, hidden, ga, gb = kept[step]
        flags = flags_for(section == step)
        return attn_bwd(flags, table, gmid, x, attn_gain, bias, normed, qkv, lse, mixed, pieces, prev)

    gmid, *ffn_prev = ffn_back(1, grad_final.astype(bf16), None)
    attn_prev = attn_back(1, gmid, None)
    gmid, grad_ffn_gain, f1_keep, f1_send, f2_keep, f2_send = ffn_back(0, hop(attn_prev[0], 1), ffn_prev)

    zl, zh = z % 2, z // 2

    def parts(values):
        return values.reshape(2, 2, 2, -1, values.shape[-1])

    f1 = [parts(f1_keep), parts(swap(f1_send, "dp", 1))]
    f2 = [parts(f2_keep), parts(swap(f2_send, "dp", 1))]
    f1, f2, gmid = fence(f1, f2, gmid)

    f1_got = give(f1, 2, "dp", 2, y)
    f2_got = give(f2, 1, "mp", 1, zl)
    gx, grad_attn_gain, diag, *attn_grads = attn_back(0, gmid, attn_prev)
    lanes = jnp.arange(4 * BLK, dtype=jnp.int32)
    band_offset = jnp.where(lanes <= 2 * BLK + BLK - 1, BLK - lanes, 5 * BLK - lanes)
    band_bucket = jnp.concatenate(
        [
            bucket_of(band_offset, half_count),
            jnp.full((BLK,), buckets - 1, jnp.int32),
            jnp.full((BLK,), half_count - 1, jnp.int32),
        ]
    )
    pick_band = (band_bucket[:, None] == bucket_ids).astype(f32)
    table_part = jnp.einsum("zhc,cb->zhb", diag[:, :heads_dev], pick_band, precision=highest)
    table_rows = jnp.pad(table_part.reshape(MP, 1, -1), ((0, 0), (0, 0), (0, A_HALF - heads_dev * buckets)))
    shared = jnp.concatenate([grad_attn_gain.astype(bf16), grad_ffn_gain.astype(bf16), early[PROJ:]]).reshape(-1, A_HALF)
    small = jnp.concatenate([table_rows.astype(bf16), jnp.broadcast_to(shared[None], (MP,) + shared.shape)], axis=1)
    n_small = SMALL - 16
    small = jnp.pad(small, ((0, 0), (0, n_small - small.shape[1]), (0, 0)))
    small = jnp.broadcast_to(small[:, None], (MP, 2, n_small, A_HALF))
    proj_parts = early[:PROJ].reshape(MP, 2, 2, 16, A_HALF)

    def with_small(values, half):
        rows = jnp.concatenate([small, pick(proj_parts, 1, half)], axis=2)
        return lax.dynamic_update_slice_in_dim(values, rows, QUARTER, 2)

    a1_keep, a1_send, a2_keep, a2_send = attn_grads
    a2_keep, a2_send = with_small(a2_keep, core), with_small(a2_send, 1 - core)
    f1, f1_got, f2, f2_got, a1_keep, a1_send, a2_keep, a2_send, gx = fence(
        f1, f1_got, f2, f2_got, a1_keep, a1_send, a2_keep, a2_send, gx
    )

    a1 = [parts(a1_keep), parts(swap(a1_send, "dp", 1))]
    a2 = [parts(a2_keep), parts(swap(a2_send, "dp", 1))]
    f1, f2 = take(f1, 2, y, f1_got), take(f2, 1, zl, f2_got)
    f1_got = give(f1, 1, "mp", 1, zl)
    f2_got = give(f2, 0, "mp", 2, zh)
    a1_got = give(a1, 2, "dp", 2, y)
    f1, f1_got, f2, f2_got, a1, a1_got, a2, gx = fence(f1, f1_got, f2, f2_got, a1, a1_got, a2, gx)

    f1, f2, a1 = take(f1, 1, zl, f1_got), take(f2, 0, zh, f2_got), take(a1, 2, y, a1_got)
    f1_got = give(f1, 0, "mp", 2, zh)
    f2 = total_of(f2)
    f2_got = swap(f2, "dp", 2)
    a1_got = give(a1, 1, "mp", 1, zl)
    a2_got = give(a2, 1, "mp", 1, zl)
    f1, f1_got, f2, f2_got, a1, a1_got, a2, a2_got, gx = fence(f1, f1_got, f2, f2_got, a1, a1_got, a2, a2_got, gx)

    a1, a2 = take(a1, 1, zl, a1_got), take(a2, 1, zl, a2_got)
    a1_got = give(a1, 0, "mp", 2, zh)
    a2_got = give(a2, 0, "mp", 2, zh)
    f1 = over_rest(total_of(take(f1, 0, zh, f1_got)))
    f1_got = swap(f1, "dp", 2)
    f2 = over_rest(add_low(f2, f2_got))
    f2_other = swap(f2, "dp", 1)
    f1, f1_got, f2, f2_other, a1, a1_got, a2, a2_got, gx = fence(
        f1, f1_got, f2, f2_other, a1, a1_got, a2, a2_got, gx
    )

    a1, a2 = total_of(take(a1, 0, zh, a1_got)), total_of(take(a2, 0, zh, a2_got))
    a1 = over_rest(a1)
    a1_got = swap(a1, "dp", 2)
    a2_got = swap(a2, "dp", 2)
    f1 = in_order(y, f1, f1_got)
    f1_other = swap(f1, "dp", 1)
    d_inputs = collect_rows(gx, place, pairs)[None]
    flags_end = flags_for(1)
    ffn_sums = finish(finish_ffn_kernel, flags_end, [(D, FQ), (D, FQ), (FQ, D)], f1, f1_other, f2, f2_other)
    ffn_sums, a1, a1_got, a2, a2_got, d_inputs = fence(ffn_sums, a1, a1_got, a2, a2_got, d_inputs)

    a1 = in_order(y, a1, a1_got)
    a2 = over_rest(add_low(a2, a2_got))
    a1_other, a2_other = swap(a1, "dp", 1), swap(a2, "dp", 1)
    small_sum = a2[0, QUARTER : QUARTER + n_small].astype(f32)
    table_other = swap(small_sum[:1], "section", 1)
    attn_sums = finish(
        finish_attn_kernel, flags_end, [(D, QUARTER)] * 3 + [(QUARTER, D)], a1, a1_other, a2, a2_other
    )
    proj_sum = in_order(core, a2[:, QUARTER + n_small :], a2_other[:, QUARTER + n_small :])
    proj_sum = proj_sum.astype(f32).reshape(PROJ // MP, D)
    shared_sum = small_sum[1 : 1 + shared.shape[0]].reshape(-1, D)
    grad_table = (small_sum[:1] + table_other)[0, : heads_dev * buckets].reshape(heads_dev, buckets).T
    return (
        shared_sum[3, 0] + shared_sum[4, 0],
        d_inputs,
        shared_sum[0:1],
        attn_sums[0][None],
        attn_sums[1][None],
        attn_sums[2][None],
        attn_sums[3][None],
        shared_sum[1:2],
        ffn_sums[0][None],
        ffn_sums[1][None],
        ffn_sums[2][None],
        grad_table,
        shared_sum[2],
        proj_sum.T,
    )


def solution(mesh):
    return jax.shard_map(
        on_device,
        mesh=mesh,
        in_specs=(
            P("dp", "mp", None),
            P("section", None),
            P("section", None, "mp"),
            P("section", None, "mp"),
            P("section", None, "mp"),
            P("section", "mp", None),
            P("section", None),
            P("section", None, "mp"),
            P("section", None, "mp"),
            P("section", "mp", None),
            P(None, "mp"),
            P(),
            P(),
            P("dp", None),
            P("dp", None, None),
        ),
        out_specs=(
            P(),
            P("section", "dp", "mp", None),
            P("section", None),
            P("section", None, "mp"),
            P("section", None, "mp"),
            P("section", None, "mp"),
            P("section", "mp", None),
            P("section", None),
            P("section", None, "mp"),
            P("section", None, "mp"),
            P("section", "mp", None),
            P(None, "mp"),
            P(),
            P(None, "mp"),
        ),
        check_vma=False,
    )
```

```python
import functools

import jax
import jax.numpy as jnp
from jax import lax
from jax.experimental import pallas as pl
from jax.experimental.pallas import tpu as pltpu
from jax.sharding import PartitionSpec as P

D = 768
HEAD_DIM = 64
FF = 2048
PROJ = 128
DOC_LEN = 512
QRY_LEN = 32
QRYS_MB = 8
QRY_ROWS = QRYS_MB * QRY_LEN
MP = 4
QUARTER = D // MP
FQ = FF // MP
HEADS_Q = QUARTER // HEAD_DIM
BLK = 128
NBLK = DOC_LEN // BLK
QKV = 3 * QUARTER
SMALL = 16
F_HALF = 3 * FQ // 2

bucket_edges = (8, 12, 16, 23, 32, 46, 64, 91)
norm_eps = 1e-06
logit_scale = 16.0
highest = lax.Precision.HIGHEST
f32 = jnp.float32
bf16 = jnp.bfloat16

ACT, IS_DOC, ZPOS, RPOS = range(4)
VMEM_LIMIT = 56 * 1024 * 1024


def mm(a, b):
    return jnp.dot(a, b, preferred_element_type=f32)


def mm_t(a, b):
    return lax.dot_general(a, b, (((1,), (1,)), ((), ())), preferred_element_type=f32)


def t_mm(a, b):
    return lax.dot_general(a, b, (((0,), (0,)), ((), ())), preferred_element_type=f32)


def bucket_of(offset, half_count):
    spread = jnp.abs(offset)
    far_bucket = 7 + sum((spread >= edge).astype(jnp.int32) for edge in bucket_edges)
    near_bucket = jnp.where(spread < 8, spread, far_bucket)
    return near_bucket + half_count * (offset > 0).astype(jnp.int32)


class Copies:
    def __init__(self, sem, first=0):
        self.sem = sem
        self.next = first

    def __call__(self, source, target):
        copy = pltpu.make_async_copy(source, target, self.sem.at[self.next])
        self.next += 1
        copy.start()
        return copy


def get_rows(copy, halves, target, doc):
    count = 2 if doc else 1
    return [copy(halves[i], target.at[pl.ds(i * QRY_ROWS, QRY_ROWS)]) for i in range(count)]


def put_rows(copy, source, halves, doc):
    count = 2 if doc else 1
    return [copy(source.at[pl.ds(i * QRY_ROWS, QRY_ROWS)], halves[i]) for i in range(count)]


def wait_all(copies):
    for copy in copies:
        copy.wait()


class Weights:
    def __init__(self, flags, chunk, target, sem, lanes=None):
        self.z, self.r = flags[ZPOS], flags[RPOS]
        self.own, self.pieces = chunk[0], chunk[1:]
        self.target, self.sem = target, sem
        self.lanes = pl.ds(0, target.shape[2]) if lanes is None else lanes

    def copies(self, s):
        if s == 0:
            return [pltpu.make_async_copy(self.own, self.target.at[self.z, :, self.lanes], self.sem.at[0, 0])]
        return [
            pltpu.make_async_copy(
                self.pieces[4 * (s - 1) + k],
                self.target.at[self.z ^ s, rows_at(self.r ^ bits, QUARTER), self.lanes],
                self.sem.at[s, k],
            )
            for k, bits in enumerate((0, 2, 1, 3))
        ]

    def start(self):
        for s in range(MP):
            start_all(self.copies(s))

    def each(self, s, act):
        for k in range(MP):
            pl.when(s == k)(lambda k=k: act(self.copies(k)))

    def start_slot(self, s):
        self.each(s, start_all)

    def wait_slot(self, s):
        self.each(s, wait_all)


N_CHUNK = 13


def start_all(copies):
    for copy in copies:
        copy.start()


def rows_at(index, size):
    return pl.ds(pl.multiple_of(index * size, size), size)


def bias_matrix(bias_ref, table_ref, head):
    far_up = jnp.full((BLK, BLK), table_ref[31, head], f32)
    far_low = jnp.full((BLK, BLK), table_ref[15, head], f32)
    near = {0: bias_ref[head, 0], 1: bias_ref[head, 1], -1: bias_ref[head, 2]}

    def block(bj, bi):
        if bj - bi in near:
            return near[bj - bi]
        return far_up if bj > bi else far_low

    return jnp.concatenate(
        [jnp.concatenate([block(bj, bi) for bi in range(NBLK)], axis=1) for bj in range(NBLK)], axis=0
    )


def rms_parts(values):
    return lax.rsqrt(jnp.mean(values * values, axis=-1, keepdims=True) + norm_eps)


def rms_back(values, gain, grad):
    scale = rms_parts(values)
    weighted = grad * gain
    inner = jnp.mean(values * weighted, axis=-1, keepdims=True)
    out = scale * (weighted - values * (scale * scale * inner))
    gain_grad = jnp.sum(grad * values * scale, axis=0, keepdims=True)
    return out, gain_grad


def by_kind(flags, body):
    pl.when(flags[IS_DOC] == 1)(lambda: body(DOC_LEN, True))
    pl.when(flags[IS_DOC] == 0)(lambda: body(QRY_ROWS, False))


def head_slices(hh):
    at = hh * HEAD_DIM
    return (
        slice(at, at + HEAD_DIM),
        slice(QUARTER + at, QUARTER + at + HEAD_DIM),
        slice(2 * QUARTER + at, 2 * QUARTER + at + HEAD_DIM),
        slice(at, at + HEAD_DIM),
    )


def attn_fwd_kernel(flags, table, attn_gain_ref, ffn_gain_ref, x_low, x_high, bias_hbm, *refs):
    weights, refs = refs[:N_CHUNK], refs[N_CHUNK:]
    normed_out, qkv_out, lse_out, mixed_out, middle_out, normed_ffn_out = refs[:6]
    x_ref, bias_ref, normed_ref, qkv_ref, lse_ref, mixed_ref, middle_ref, normed_ffn_ref = refs[6:14]
    wa, sem, asem, zsem = refs[14:]
    weights = Weights(flags, weights, wa, asem)
    def one_head(z, hh, rows, bias):
        qs, ks, vs, ms = head_slices(hh)
        q, k, v = qkv_ref[z, rows, qs], qkv_ref[z, rows, ks], qkv_ref[z, rows, vs]
        scores = mm_t(k, q) + bias
        peak = jnp.max(scores, axis=0, keepdims=True)
        weights = jnp.exp(scores - peak)
        total = jnp.sum(weights, axis=0, keepdims=True)
        mixed = t_mm(v, weights.astype(bf16)) * (1.0 / total)
        lse_ref[z, hh : hh + 1, rows] = peak + jnp.log(total)
        mixed_ref[z, rows, ms] = mixed.T.astype(bf16)

    def body(rows, doc):
        put = Copies(sem)
        outs = []
        get_x = get_rows(put, (x_low, x_high), x_ref, doc)
        weights.start()
        get_bias = put(bias_hbm, bias_ref)
        wait_all(get_x)

        def send(source, target):
            outs.append(put(source.at[pl.ds(0, rows)], target.at[pl.ds(0, rows)]))

        def parts(z):
            return [
                pltpu.make_async_copy(a.at[z, pl.ds(0, rows)], b.at[z, pl.ds(0, rows)], zsem.at[z, i])
                for i, (a, b) in enumerate(((qkv_ref, qkv_out), (mixed_ref, mixed_out)))
            ]

        x = x_ref[:rows].astype(f32)
        normed_ref[:rows] = (x * rms_parts(x) * attn_gain_ref[...]).astype(bf16)
        send(normed_ref, normed_out)
        get_bias.wait()

        @pl.loop(0, MP)
        def _(s):
            z = flags[ZPOS] ^ s
            weights.wait_slot(s)
            qkv_ref[z, :rows] = mm_t(normed_ref[:rows], wa[z, :QKV]).astype(bf16)
            for hh in range(HEADS_Q):
                head = z * HEADS_Q + hh
                if doc:
                    one_head(z, hh, slice(0, DOC_LEN), bias_matrix(bias_ref, table, head))
                else:
                    for b in range(QRY_ROWS // BLK):
                        one_head(z, hh, slice(b * BLK, (b + 1) * BLK), bias_ref[head, 0])
            start_all(parts(z))

        outs.append(put(lse_ref, lse_out))
        middle_ref[:rows] = x_ref[:rows].astype(f32)

        @pl.loop(0, MP)
        def _(z):
            middle_ref[:rows] += mm(mixed_ref[z, :rows], wa[z, QKV:])

        middle = middle_ref[:rows]
        send(middle_ref, middle_out)
        normed_ffn_ref[:rows] = (middle * rms_parts(middle) * ffn_gain_ref[...]).astype(bf16)
        send(normed_ffn_ref, normed_ffn_out)

        @pl.loop(0, MP)
        def _(z):
            wait_all(parts(z))

        wait_all(outs)

    @pl.when(flags[ACT] == 1)
    def _():
        by_kind(flags, body)


def ffn_fwd_kernel(flags, final_gain_ref, proj_ref, middle_hbm, normed_hbm, *refs):
    first, second, refs = refs[:N_CHUNK], refs[N_CHUNK : 2 * N_CHUNK], refs[2 * N_CHUNK :]
    out_out, low_low, low_high, hidden_out, ga_out, gb_out, final_out, embed_out = refs[:8]
    normed_ref, out_ref, low_ref, hidden_ref, ga_ref, gb_ref, final_ref, embed_ref = refs[8:16]
    wf, sem, fsem, gsem, zsem = refs[16:]
    first = Weights(flags, first, wf, fsem, pl.ds(0, F_HALF))
    second = Weights(flags, second, wf, gsem, pl.ds(F_HALF, F_HALF))

    def body(rows, doc):
        copy = Copies(sem)
        get_normed = copy(normed_hbm.at[pl.ds(0, rows)], normed_ref.at[pl.ds(0, rows)])
        get_middle = copy(middle_hbm.at[pl.ds(0, rows)], out_ref.at[pl.ds(0, rows)])
        first.start_slot(0)
        second.start_slot(0)

        def parts(z):
            pairs = ((hidden_ref, hidden_out), (ga_ref, ga_out), (gb_ref, gb_out))
            return [
                pltpu.make_async_copy(a.at[z, pl.ds(0, rows)], b.at[z, pl.ds(0, rows)], zsem.at[z, i])
                for i, (a, b) in enumerate(pairs)
            ]

        get_normed.wait()
        get_middle.wait()

        @pl.loop(0, MP)
        def _(s):
            z = flags[ZPOS] ^ s

            first.start_slot(s + 1)
            second.start_slot(s + 1)
            first.wait_slot(s)
            second.wait_slot(s)
            normed = normed_ref[:rows]
            gate = mm(normed, wf[z, :, :FQ])
            up = mm(normed, wf[z, :, FQ : 2 * FQ])
            coef = 0.7978845608028654
            square = gate * gate
            tanh = jnp.tanh(coef * gate * (1.0 + 0.044715 * square))
            half = 0.5 + 0.5 * tanh
            gelu = gate * half
            slope = half + (0.5 * coef) * gate * (1.0 - tanh * tanh) * (1.0 + 3 * 0.044715 * square)
            hidden = (gelu * up).astype(bf16)
            hidden_ref[z, :rows] = hidden
            ga_ref[z, :rows] = (up * slope).astype(bf16)
            gb_ref[z, :rows] = gelu.astype(bf16)
            start_all(parts(z))
            out_ref[:rows] += mm_t(hidden, wf[z, :, 2 * FQ :])

        low_ref[:rows] = out_ref[:rows].astype(bf16)
        if not doc:
            out_ref[rows:] = jnp.zeros((DOC_LEN - rows, D), f32)
            final_ref[rows:] = jnp.zeros((DOC_LEN - rows, D), bf16)
        outs = put_rows(copy, low_ref, (low_low, low_high), doc) + [copy(out_ref, out_out)]
        out = out_ref[:rows]
        final_ref[:rows] = (out * rms_parts(out) * final_gain_ref[...]).astype(bf16)
        embed_ref[:rows] = mm(final_ref[:rows], proj_ref[...]).astype(bf16)
        outs.append(copy(embed_ref.at[pl.ds(0, rows)], embed_out.at[pl.ds(0, rows)]))
        outs.append(copy(final_ref, final_out))

        @pl.loop(0, MP)
        def _(z):
            wait_all(parts(z))

        wait_all(outs)

    @pl.when(flags[ACT] == 1)
    def _():
        by_kind(flags, body)


def ffn_bwd_kernel(
    flags, gain_ref, gout_low, gout_high, middle_hbm, normed_hbm, hidden_hbm, ga_hbm, gb_hbm,
    *refs,
):
    gmid_out, dgain_out, *df_outs = refs[-24:-18]
    gout_ref, middle_ref, normed_ref, hidden_ref, ga_ref, gb_ref, gmid_ref, dgain_ref = refs[-18:-10]
    wf, gout_t, normed_t, df_buf, gn, sem, fsem, gsem, ksem, osem = refs[-10:]
    first = Weights(flags, refs[:N_CHUNK], wf, fsem, pl.ds(0, F_HALF))
    second = Weights(flags, refs[N_CHUNK : 2 * N_CHUNK], wf, gsem, pl.ds(F_HALF, F_HALF))

    def outs(s, core):
        slot, half, z = s % 2, D // 2, flags[ZPOS] ^ s
        copies = []
        for i, out in enumerate(df_outs):
            rows = pl.ds((core if i % 2 == 0 else 1 - core) * half, half)
            lanes = pl.ds(i // 2 * F_HALF, F_HALF)
            copies.append(pltpu.make_async_copy(df_buf.at[slot, rows, lanes], out.at[z], osem.at[slot, i]))
        return copies

    def body(rows, doc):
        core = 0 if doc else 1
        copy = Copies(sem)

        def get(source, target):
            return copy(source.at[pl.ds(0, rows)], target.at[pl.ds(0, rows)])

        get_gout = get_rows(copy, (gout_low, gout_high), gout_ref, doc)
        get_normed = get(normed_hbm, normed_ref)
        kept = ((ga_hbm, ga_ref), (gb_hbm, gb_ref), (hidden_hbm, hidden_ref))

        def part(z):
            return [
                pltpu.make_async_copy(a.at[z, pl.ds(0, rows)], b.at[z, pl.ds(0, rows)], ksem.at[z, i])
                for i, (a, b) in enumerate(kept)
            ]

        first.start_slot(0)
        second.start_slot(0)
        start_all(part(flags[ZPOS]))
        get_middle = get(middle_hbm, middle_ref)
        wait_all(get_gout)
        gout_t[:, :rows] = gout_ref[:rows].T
        get_normed.wait()
        normed_t[:, :rows] = normed_ref[:rows].T
        gn[:rows] = jnp.zeros((rows, D), f32)

        @pl.loop(0, MP)
        def _(s):
            z = flags[ZPOS] ^ s
            pl.when(s >= 2)(lambda: wait_all(outs(s - 2, core)))

            first.start_slot(s + 1)
            second.start_slot(s + 1)
            pl.when(s + 1 < MP)(lambda: start_all(part(flags[ZPOS] ^ (s + 1))))
            first.wait_slot(s)
            second.wait_slot(s)
            wait_all(part(z))
            slot = s % 2
            grad_hidden = mm(gout_ref[:rows], wf[z, :, 2 * FQ :])
            grad_gate = (grad_hidden * ga_ref[z, :rows].astype(f32)).astype(bf16)
            grad_up = (grad_hidden * gb_ref[z, :rows].astype(f32)).astype(bf16)
            df_buf[slot, :, :FQ] = mm(normed_t[:, :rows], grad_gate).astype(bf16)
            df_buf[slot, :, FQ : 2 * FQ] = mm(normed_t[:, :rows], grad_up).astype(bf16)
            df_buf[slot, :, 2 * FQ :] = mm(gout_t[:, :rows], hidden_ref[z, :rows]).astype(bf16)
            start_all(outs(s, core))
            gn[:rows] += mm_t(grad_gate, wf[z, :, :FQ]) + mm_t(grad_up, wf[z, :, FQ : 2 * FQ])

        get_middle.wait()
        back, gain_grad = rms_back(middle_ref[:rows], gain_ref[...], gn[:rows])
        gmid_ref[:rows] = gout_ref[:rows].astype(f32) + back
        dgain_ref[...] = gain_grad
        last = [copy(gmid_ref.at[pl.ds(0, rows)], gmid_out.at[pl.ds(0, rows)]), copy(dgain_ref, dgain_out)]
        for s in (MP - 2, MP - 1):
            wait_all(outs(s, core))
        wait_all(last)

    @pl.when(flags[ACT] == 1)
    def _():
        by_kind(flags, body)


def attn_bwd_kernel(
    flags, table, gain_ref, band_ref, ffn_gain_ref, early_ref, gmid_hbm, x_low, x_high, bias_hbm, normed_hbm, qkv_hbm, lse_hbm,
    mixed_hbm, *refs,
):
    gx_low, gx_high, dgain_out, *da_outs = refs[-27:-22]
    gmid_ref, x_ref, bias_ref, normed_ref, qkv_ref, lse_ref, mixed_ref, gx_ref, dgain_ref, diag_ref = refs[-22:-12]
    wa, gmb, gmix, gqkv, da_buf, gn, rows_buf, sem, asem, ksem, osem, rsem = refs[-12:]
    weights = Weights(flags, refs[:N_CHUNK], wa, asem)

    def one_head(z, hh, rows, bias):
        qs, ks, vs, ms = head_slices(hh)
        q, k, v = qkv_ref[z, rows, qs], qkv_ref[z, rows, ks], qkv_ref[z, rows, vs]
        go = gmix[rows, ms]
        out = mixed_ref[z, rows, ms].astype(f32)
        delta = jnp.sum((go.astype(f32) * out).T, axis=0, keepdims=True)
        probs = jnp.exp(mm_t(k, q) + bias - lse_ref[z, hh : hh + 1, rows])
        grad_scores = probs * (mm_t(v, go) - delta)
        low = grad_scores.astype(bf16)
        gqkv[rows, qs] = t_mm(k, low).T.astype(bf16)
        gqkv[rows, ks] = mm(low, q).astype(bf16)
        gqkv[rows, vs] = mm(probs.astype(bf16), go).astype(bf16)
        return grad_scores

    def band_sums(up, mid, low):
        blank = jnp.zeros((BLK, BLK), f32)
        band = jnp.concatenate([up, mid, low, blank], axis=1)
        width = 4 * BLK

        def left(part, by):
            return pltpu.roll(part, width - by, 1) if by else part

        eight = functools.reduce(jnp.add, [left(band[g : g + 8], g) for g in range(0, BLK, 8)])
        return functools.reduce(jnp.add, [left(eight[r : r + 1], r) for r in range(8)])

    def outs(s, core):
        slot, z = s % 2, flags[ZPOS] ^ s
        copies = []
        for i, out in enumerate(da_outs):
            for half in range(2):
                rows = pl.ds((core if i == 0 else 1 - core) * (D // 2) + half * QUARTER, QUARTER)
                target = out.at[z, half, pl.ds(0, QUARTER), :]
                copies.append(pltpu.make_async_copy(da_buf.at[slot, rows, :], target, osem.at[slot, 2 * i + half]))
        return copies

    def body(rows, doc):
        core = 0 if doc else 1
        copy = Copies(sem)

        def get(source, target):
            return copy(source.at[pl.ds(0, rows)], target.at[pl.ds(0, rows)])

        get_gmid = get(gmid_hbm, gmid_ref)
        get_lse = copy(lse_hbm, lse_ref)
        kept = ((qkv_hbm, qkv_ref), (mixed_hbm, mixed_ref))

        def part(z):
            return [
                pltpu.make_async_copy(a.at[z, pl.ds(0, rows)], b.at[z, pl.ds(0, rows)], ksem.at[z, i])
                for i, (a, b) in enumerate(kept)
            ]

        weights.start_slot(0)
        start_all(part(flags[ZPOS]))
        get_bias = copy(bias_hbm, bias_ref)
        get_normed = get(normed_hbm, normed_ref)
        get_x = get_rows(copy, (x_low, x_high), x_ref, doc)
        get_gmid.wait()
        gmb[:rows] = gmid_ref[:rows].astype(bf16)
        gn[:rows] = jnp.zeros((rows, D), f32)
        get_lse.wait()
        get_normed.wait()
        get_bias.wait()

        @pl.loop(0, MP)
        def _(s):
            z = flags[ZPOS] ^ s
            pl.when(s >= 2)(lambda: wait_all(outs(s - 2, core)))

            weights.start_slot(s + 1)
            pl.when(s + 1 < MP)(lambda: start_all(part(flags[ZPOS] ^ (s + 1))))
            weights.wait_slot(s)
            wait_all(part(z))
            slot = s % 2
            gmix[:rows] = mm_t(gmb[:rows], wa[z, QKV:]).astype(bf16)
            for hh in range(HEADS_Q):
                head = z * HEADS_Q + hh
                if doc:
                    grads = one_head(z, hh, slice(0, DOC_LEN), bias_matrix(bias_ref, table, head))

                    def blocks(test):
                        picked = [
                            grads[bj * BLK : (bj + 1) * BLK, bi * BLK : (bi + 1) * BLK]
                            for bj in range(NBLK)
                            for bi in range(NBLK)
                            if test(bj - bi)
                        ]
                        return functools.reduce(jnp.add, picked)

                    sums = band_sums(blocks(lambda d: d == 1), blocks(lambda d: d == 0), blocks(lambda d: d == -1))
                    far_up = jnp.sum(blocks(lambda d: d > 1), axis=0, keepdims=True)
                    far_low = jnp.sum(blocks(lambda d: d < -1), axis=0, keepdims=True)
                    diag_ref[z, hh : hh + 1, :] = jnp.concatenate([sums, far_up, far_low], axis=1)
                else:
                    grads = jnp.zeros((BLK, BLK), f32)
                    for b in range(QRY_ROWS // BLK):
                        grads = grads + one_head(z, hh, slice(b * BLK, (b + 1) * BLK), bias_ref[head, 0])
                    blank = jnp.zeros((BLK, BLK), f32)
                    sums = band_sums(blank, grads, blank)
                    diag_ref[z, hh : hh + 1, :] = jnp.concatenate([sums, jnp.zeros((1, 2 * BLK), f32)], axis=1)
            grads = gqkv[:rows]
            da_buf[slot, :QKV] = t_mm(grads, normed_ref[:rows]).astype(bf16)
            da_buf[slot, QKV:] = t_mm(mixed_ref[z, :rows], gmb[:rows]).astype(bf16)
            start_all(outs(s, core))
            gn[:rows] += mm(grads, wa[z, :QKV])

        wait_all(get_x)
        back, gain_grad = rms_back(x_ref[:rows].astype(f32), gain_ref[...], gn[:rows])
        gx_ref[:rows] = (gmid_ref[:rows] + back).astype(bf16)
        dgain_ref[...] = gain_grad
        last = put_rows(copy, gx_ref, (gx_low, gx_high), doc) + [copy(dgain_ref, dgain_out)]
        for z in range(MP):
            sums = jnp.dot(diag_ref[z], band_ref[...], precision=highest, preferred_element_type=f32)
            shared = [
                jnp.concatenate([sums[:HEADS_Q], jnp.zeros((HEADS_Q, D - BLK), f32)], axis=1),
                gain_grad,
                ffn_gain_ref[...],
                early_ref[PROJ : PROJ + 3],
            ]
            shared = jnp.concatenate(shared, axis=0)
            for which, side in enumerate((core, 1 - core)):
                for half in range(2):
                    first = z * (PROJ // MP) + side * 16 + half * 8
                    both = jnp.concatenate([shared, early_ref[first : first + 8]], axis=0)
                    rows_buf[which, z, half] = both.astype(bf16)
        for which, out in enumerate(da_outs):
            target = out.at[:, :, pl.ds(QUARTER, SMALL), :]
            last.append(pltpu.make_async_copy(rows_buf.at[which], target, rsem.at[which]))
            last[-1].start()
        for s in (MP - 2, MP - 1):
            wait_all(outs(s, core))
        wait_all(last)

    @pl.when(flags[ACT] == 1)
    def _():
        by_kind(flags, body)


def put_all(refs):
    count = len(refs) // 2
    copies = [pltpu.make_async_copy(refs[count + i], refs[i], refs[-1].at[i]) for i in range(count)]
    start_all(copies)
    wait_all(copies)


def finish_ffn_kernel(flags, mine1, other1, mine2, other2, *refs):
    gate_ref, up_ref, down_ref = refs[3:6]
    core = flags[RPOS] % 2
    half = D // 2
    for side, first, second in ((core, mine1, mine2), (1 - core, other1, other2)):
        rows = rows_at(side, half)
        low = first[...].reshape(half, F_HALF).astype(f32)
        high = second[...].reshape(half, F_HALF).astype(f32)
        gate_ref[rows, :] = low[:, :FQ]
        up_ref[rows, : F_HALF - FQ] = low[:, FQ:]
        up_ref[rows, F_HALF - FQ :] = high[:, : 2 * FQ - F_HALF]
        down = high[:, 2 * FQ - F_HALF :].T

        @pl.when(side == 0)
        def _():
            down_ref[:, :half] = down

        @pl.when(side == 1)
        def _():
            down_ref[:, half:] = down

    put_all(refs)


def finish_attn_kernel(flags, mine, other, *refs):
    buffers = refs[4:8]
    core = flags[RPOS] % 2
    for side in range(2):

        @pl.when(core == side)
        def _():
            for i in range(2):
                buffers[2 * side + i][...] = mine[i, :QUARTER].astype(f32)
                buffers[2 - 2 * side + i][...] = other[i, :QUARTER].astype(f32)

    put_all(refs)


def vmem():
    return pl.BlockSpec(memory_space=pltpu.VMEM)


def smem():
    return pl.BlockSpec(memory_space=pltpu.SMEM)


def hbm():
    return pl.BlockSpec(memory_space=pl.ANY)


def shape(dims, kind):
    return jax.ShapeDtypeStruct(dims, kind)


def params():
    return pltpu.CompilerParams(vmem_limit_bytes=VMEM_LIMIT)


def cost(microseconds):
    return pl.CostEstimate(flops=int(microseconds * 1e9), bytes_accessed=16 * 1024 * 1024, transcendentals=0)


def count_kernel(flags, hits_ref, counts_out, buffer, sem):
    width = buffer.shape[2]
    blocks = hits_ref.shape[1] // width

    def put(i):
        lanes = pl.ds(pl.multiple_of(i * width, width), width)
        return pltpu.make_async_copy(buffer.at[i % 2], counts_out.at[:, lanes], sem.at[i % 2])

    @pl.when(jnp.logical_and(flags[ACT] == 1, flags[IS_DOC] == 1))
    def _():
        @pl.loop(0, blocks)
        def _(i):
            pl.when(i >= 2)(lambda: put(i - 2).wait())
            hits = hits_ref[:, pl.ds(pl.multiple_of(i * width, width), width)]
            for row in range(0, DOC_LEN, BLK):
                places = lax.broadcasted_iota(jnp.int32, (BLK, width), 0) + row
                total = jnp.zeros((BLK, width), f32)
                for k in range(hits.shape[0]):
                    total = total + (hits[k : k + 1] == places).astype(f32)
                buffer[i % 2, row : row + BLK] = total.astype(bf16)
            put(i).start()

        put(blocks - 2).wait()
        put(blocks - 1).wait()


def count_hits(flags, hits):
    width = BLK
    return pl.pallas_call(
        count_kernel,
        in_specs=[smem(), vmem()],
        out_specs=hbm(),
        out_shape=shape((DOC_LEN, hits.shape[1]), bf16),
        scratch_shapes=[pltpu.VMEM((2, DOC_LEN, width), bf16), pltpu.SemaphoreType.DMA((2,))],
        compiler_params=params(),
        cost_estimate=cost(8),
        name="count_hits",
    )(flags, hits)


QUARTERS = (MP, DOC_LEN, FQ)
ROWS = (DOC_LEN, D)
HALF_ROWS = (QRY_ROWS, D)


def on_vmem(shapes):
    return [pltpu.VMEM(s.shape, s.dtype) for s in shapes]


def attn_fwd(flags, table, x, attn_gain, ffn_gain, bias, attn_weights):
    results = [
        shape(ROWS, bf16),
        shape((MP, DOC_LEN, QKV), bf16),
        shape((MP, 8, DOC_LEN), f32),
        shape((MP, DOC_LEN, QUARTER), bf16),
        shape(ROWS, f32),
        shape(ROWS, bf16),
    ]
    return pl.pallas_call(
        attn_fwd_kernel,
        in_specs=[smem()] * 2 + [vmem()] * 2 + [hbm()] * (3 + N_CHUNK),
        out_specs=[hbm()] * 6,
        out_shape=results,
        scratch_shapes=on_vmem([shape(ROWS, bf16), shape(bias.shape, f32)] + results)
        + [
            pltpu.VMEM((MP, D, D), bf16),
            pltpu.SemaphoreType.DMA((10,)),
            pltpu.SemaphoreType.DMA((MP, 4)),
            pltpu.SemaphoreType.DMA((MP, 2)),
        ],
        compiler_params=params(),
        cost_estimate=cost(14),
        name="attn_fwd",
    )(flags, table, attn_gain, ffn_gain, *x, bias, *attn_weights)


def ffn_fwd(flags, final_gain, w_proj, middle, normed, ffn_weights):
    buffers = [shape(ROWS, f32), shape(ROWS, bf16)] + [shape(QUARTERS, bf16)] * 3
    buffers += [shape(ROWS, bf16), shape((DOC_LEN, PROJ), bf16)]
    results = buffers[:1] + [shape(HALF_ROWS, bf16)] * 2 + buffers[2:]
    return pl.pallas_call(
        ffn_fwd_kernel,
        in_specs=[smem()] + [vmem()] * 2 + [hbm()] * (2 + 2 * N_CHUNK),
        out_specs=[hbm()] * 8,
        out_shape=results,
        scratch_shapes=on_vmem([shape(ROWS, bf16)] + buffers)
        + [
            pltpu.VMEM((MP, D, 3 * FQ), bf16),
            pltpu.SemaphoreType.DMA((8,)),
            pltpu.SemaphoreType.DMA((MP, 4)),
            pltpu.SemaphoreType.DMA((MP, 4)),
            pltpu.SemaphoreType.DMA((MP, 3)),
        ],
        compiler_params=params(),
        cost_estimate=cost(10),
        name="ffn_fwd",
    )(flags, final_gain, w_proj, middle, normed, *ffn_weights)


def score_kernel(flags, query_ref, embed_ref, counts_ref, shares_ref, share_query_ref, mass_ref):
    @pl.when(jnp.logical_and(flags[ACT] == 1, flags[IS_DOC] == 1))
    def _():
        sims = mm_t(embed_ref[...], query_ref[...])
        weighted = jnp.exp(sims * PROJ ** (-0.5)) * counts_ref[...].astype(f32)
        mass = jnp.sum(weighted, axis=0, keepdims=True)
        mass_ref[...] = mass
        shares = (weighted * (1.0 / (1.0 + mass))).astype(bf16)
        shares_ref[...] = shares
        share_query_ref[...] = t_mm(shares, embed_ref[...])


def score(flags, query_slots, embed, counts):
    tokens = query_slots.shape[0]
    width = DOC_LEN
    return pl.pallas_call(
        score_kernel,
        grid=(tokens // width,),
        in_specs=[
            smem(),
            pl.BlockSpec((width, PROJ), lambda i: (i, 0)),
            pl.BlockSpec((DOC_LEN, PROJ), lambda i: (0, 0)),
            pl.BlockSpec((DOC_LEN, width), lambda i: (0, i)),
        ],
        out_specs=[
            pl.BlockSpec((DOC_LEN, width), lambda i: (0, i)),
            pl.BlockSpec((width, PROJ), lambda i: (i, 0)),
            pl.BlockSpec((1, width), lambda i: (0, i)),
        ],
        out_shape=[shape((DOC_LEN, tokens), bf16), shape((tokens, PROJ), f32), shape((1, tokens), f32)],
        compiler_params=params(),
        cost_estimate=cost(4),
        name="score",
    )(flags, query_slots, embed, counts)


def coef_kernel(flags, logits_ref, chosen_ref, expand_ref, share_ref, coef_ref, grad_ref, loss_ref):
    @pl.when(jnp.logical_and(flags[ACT] == 1, flags[IS_DOC] == 1))
    def _():
        logits = logits_ref[...]
        n_queries = logits.shape[1]
        spread = jnp.exp(logits - jnp.max(logits, axis=0, keepdims=True))
        all_total = jnp.sum(spread, axis=0, keepdims=True)
        pos_total = jnp.sum(chosen_ref[...] * spread, axis=0, keepdims=True)
        own = spread[0:1]
        grad = own / all_total - chosen_ref[0:1] * own / pos_total
        loss = jnp.sum(jnp.log(all_total) - jnp.log(pos_total), axis=1, keepdims=True) / n_queries
        loss_ref[...] = jnp.broadcast_to(loss, loss_ref.shape)
        grad = jnp.broadcast_to(grad * (logit_scale / QRY_LEN * PROJ ** (-0.5) / n_queries), (8, n_queries))
        coef = jnp.dot(grad, expand_ref[...], precision=highest, preferred_element_type=f32)
        coef_ref[...] = coef[0:1]
        grad_ref[...] = (share_ref[...] * coef.T[:, 0:1]).astype(bf16)


def coefs(flags, logits, chosen, expand, share_query):
    return pl.pallas_call(
        coef_kernel,
        in_specs=[smem()] + [vmem()] * 4,
        out_specs=[vmem()] * 3,
        out_shape=[
            shape((1, share_query.shape[0]), f32),
            shape(share_query.shape, bf16),
            shape((1, BLK), f32),
        ],
        compiler_params=params(),
        cost_estimate=cost(3),
        name="coefs",
    )(flags, logits, chosen, expand, share_query)


def head_bwd_kernel(
    flags, shares_ref, query_ref, coef_ref, grad_query_ref, loss_ref, normed_ref, out_ref, gain_ref, proj_ref,
    gout_low, gout_high, early_ref, grad_embed,
):
    @pl.when(jnp.logical_and(flags[ACT] == 1, flags[IS_DOC] == 1))
    def _():
        scaled = (shares_ref[...].astype(f32) * coef_ref[...]).astype(bf16)
        grad_embed[...] = mm(scaled, query_ref[...]).astype(bf16)

    @pl.when(flags[IS_DOC] == 0)
    def _():
        grad_embed[:QRY_ROWS] = grad_query_ref[...]
        grad_embed[QRY_ROWS:] = jnp.zeros((DOC_LEN - QRY_ROWS, PROJ), bf16)

    @pl.when(flags[ACT] == 1)
    def _():
        back, gain_grad = rms_back(out_ref[...], gain_ref[...], mm_t(grad_embed[...], proj_ref[...]))
        back = back.astype(bf16)
        gout_low[...] = back[:QRY_ROWS]
        gout_high[...] = back[QRY_ROWS:]
        early_ref[:PROJ] = t_mm(grad_embed[...], normed_ref[...]).astype(bf16)
        loss = jnp.concatenate([loss_ref[...]] * (D // BLK), axis=1)
        high = loss.astype(bf16).astype(f32)
        rest = jnp.zeros((13, D), f32)
        early_ref[PROJ:] = jnp.concatenate([gain_grad, high, loss - high, rest], axis=0).astype(bf16)

    @pl.when(flags[ACT] == 0)
    def _():
        early_ref[...] = jnp.zeros_like(early_ref)


def head_bwd(flags, shares, query_slots, coef, grad_query, loss, normed, out, gain, proj):
    return pl.pallas_call(
        head_bwd_kernel,
        in_specs=[smem()] + [vmem()] * 9,
        out_specs=[vmem()] * 3,
        out_shape=[shape(HALF_ROWS, bf16)] * 2 + [shape((PROJ + 16, D), bf16)],
        scratch_shapes=[pltpu.VMEM((DOC_LEN, PROJ), bf16)],
        compiler_params=params(),
        cost_estimate=cost(5),
        name="head_bwd",
    )(flags, shares, query_slots, coef, grad_query, loss, normed, out, gain, proj)


def finish(kernel, flags, results, *values):
    return pl.pallas_call(
        kernel,
        in_specs=[smem()] + [vmem()] * len(values),
        out_specs=[pl.BlockSpec(memory_space=pltpu.HBM)] * len(results),
        out_shape=[pltpu.HBM(r, f32) for r in results],
        scratch_shapes=on_vmem([shape(r, f32) for r in results]) + [pltpu.SemaphoreType.DMA((len(results),))],
        compiler_params=params(),
        cost_estimate=cost(3),
        name="finish",
    )(flags, *values)


def ffn_bwd(flags, gout, middle, gain, normed, hidden, ga, gb, ffn_weights, prev):
    results = [shape(ROWS, f32), shape((1, D), f32)]
    results += [shape((MP, D // 2, F_HALF), bf16)] * 4
    prev = prev or []
    return pl.pallas_call(
        ffn_bwd_kernel,
        in_specs=[smem(), vmem()] + [hbm()] * (7 + 2 * N_CHUNK + len(prev)),
        out_specs=[hbm()] * 6,
        out_shape=results,
        input_output_aliases={9 + 2 * N_CHUNK + i: 1 + i for i in range(len(prev))},
        scratch_shapes=on_vmem([shape(ROWS, bf16), shape(ROWS, f32), shape(ROWS, bf16)] + [shape(QUARTERS, bf16)] * 3)
        + on_vmem(results[:2])
        + [
            pltpu.VMEM((MP, D, 3 * FQ), bf16),
            pltpu.VMEM((D, DOC_LEN), bf16),
            pltpu.VMEM((D, DOC_LEN), bf16),
            pltpu.VMEM((2, D, 3 * FQ), bf16),
            pltpu.VMEM(ROWS, f32),
            pltpu.SemaphoreType.DMA((8,)),
            pltpu.SemaphoreType.DMA((MP, 4)),
            pltpu.SemaphoreType.DMA((MP, 4)),
            pltpu.SemaphoreType.DMA((MP, 3)),
            pltpu.SemaphoreType.DMA((2, 4)),
        ],
        compiler_params=params(),
        cost_estimate=cost(20),
        name="ffn_bwd",
    )(flags, gain, *gout, middle, normed, hidden, ga, gb, *ffn_weights, *prev)


def attn_bwd(flags, table, gmid, x, gain, bias, band, ffn_gain, early, normed, qkv, lse, mixed, attn_weights, prev):
    results = [shape(HALF_ROWS, bf16)] * 2 + [shape((1, D), f32)] + [shape((MP, 2, QUARTER + SMALL, D), bf16)] * 2
    prev = prev or []
    held = (gmid, normed, bias, normed, qkv, lse, mixed)
    return pl.pallas_call(
        attn_bwd_kernel,
        in_specs=[smem()] * 2 + [vmem()] * 4 + [hbm()] * (8 + N_CHUNK + len(prev)),
        out_specs=[hbm()] * 5,
        out_shape=results,
        input_output_aliases={14 + N_CHUNK + i: i for i in range(len(prev))},
        scratch_shapes=on_vmem(held)
        + on_vmem([shape(ROWS, bf16), shape((1, D), f32)])
        + [
            pltpu.VMEM((MP, 8, 6 * BLK), f32),
            pltpu.VMEM((MP, D, D), bf16),
            pltpu.VMEM(ROWS, bf16),
            pltpu.VMEM((DOC_LEN, QUARTER), bf16),
            pltpu.VMEM((DOC_LEN, QKV), bf16),
            pltpu.VMEM((2, D, D), bf16),
            pltpu.VMEM(ROWS, f32),
            pltpu.VMEM((2, MP, 2, SMALL, D), bf16),
            pltpu.SemaphoreType.DMA((10,)),
            pltpu.SemaphoreType.DMA((MP, 4)),
            pltpu.SemaphoreType.DMA((MP, 2)),
            pltpu.SemaphoreType.DMA((2, 4)),
            pltpu.SemaphoreType.DMA((2,)),
        ],
        compiler_params=params(),
        cost_estimate=cost(25),
        name="attn_bwd",
    )(flags, table, gain, band, ffn_gain, early, gmid, *x, bias, normed, qkv, lse, mixed, *attn_weights, *prev)


def swap(values, axis, bit):
    count = lax.axis_size(axis)
    return lax.ppermute(values, axis, [(i, i ^ bit) for i in range(count)])


def swap_cores(values, axis, bit, core):
    dp_count, mp_count = lax.axis_size("dp"), lax.axis_size("mp")
    perm = []
    for i in range(core, dp_count, 2):
        for j in range(mp_count):
            to = (i ^ bit) * mp_count + j if axis == "dp" else i * mp_count + (j ^ bit)
            perm.append((i * mp_count + j, to))
    return lax.ppermute(values, ("dp", "mp"), perm)


def hop(rows, source):
    first = lax.ppermute(rows[0], "section", [(source, 1 - source)])
    dp_count = lax.axis_size("dp")
    perm = [(source * dp_count + i, (1 - source) * dp_count + i) for i in range(0, dp_count, 2)]
    return first, lax.ppermute(rows[1], ("section", "dp"), perm)


def pick(values, axis, index):
    return lax.dynamic_index_in_dim(values, index, axis, keepdims=False)


def add_low(a, b):
    return (a.astype(f32) + b.astype(f32)).astype(bf16)


def fence(*values):
    return lax.optimization_barrier(values)


def total_of(terms, more=()):
    def part(array, picks):
        for dim, index in picks:
            array = pick(array, dim, index)
        return array.astype(f32)

    return functools.reduce(jnp.add, [part(array, picks + more) for array, picks in terms]).astype(bf16)


def give(terms, dim, axis, bit, mine):
    return swap(total_of(terms, ((dim, 1 - mine),)), axis, bit)


def take(terms, dim, mine, got):
    return [(array, picks + ((dim, mine),)) for array, picks in terms] + [(got, ())]


def fence_terms(terms, *values):
    arrays, values = lax.optimization_barrier(([[array for array, _ in one] for one in terms], values))
    terms = [[(array, picks) for array, (_, picks) in zip(new, old)] for new, old in zip(arrays, terms)]
    return *terms, *values


def in_order(mine, values, other):
    return jnp.where(mine == 0, jnp.stack([values, other]), jnp.stack([other, values]))


def over_rest(total):
    bit = 4
    while bit < lax.axis_size("dp"):
        total = add_low(total, swap(total, "dp", bit))
        bit *= 2
    return total


def spread_tokens(tokens, place, pairs):
    z = place[2]
    got = []
    for turn in range(2):
        perm = []
        for j in range(pairs):
            for c in range(2):
                for zz in range(MP):
                    u = (turn + zz) % 2
                    perm.append(((2 * j + c) * MP + zz, (2 * j + zz // 2) * MP + 2 * c + u))
        block = pick(tokens, 0, (turn + z) % 2)
        got.append(lax.ppermute(block, ("dp", "mp"), perm))
    return got


def arrange_tokens(got, place):
    core, _, z = place
    low, high = jnp.where(z % 2 == 0, jnp.stack(got), jnp.stack(got[::-1]))
    cut = DOC_LEN - 2 * QUARTER
    tail = swap(low[:cut], "dp", 1)
    doc = jnp.concatenate([low, high, tail])
    qry = jnp.concatenate([low[cut:], high, jnp.zeros((DOC_LEN - QRY_ROWS, D), low.dtype)])
    rows = jnp.where(core == 0, doc, qry)
    return rows[:QRY_ROWS], rows[QRY_ROWS:]


def split_rows(rows, place):
    core = place[0]
    cut = DOC_LEN - 2 * QUARTER
    tail = swap(rows[2 * QUARTER :], "dp", 1)
    low_q = jnp.concatenate([tail, rows[: QUARTER - cut]])
    high_q = rows[QUARTER - cut : QRY_ROWS]
    low = jnp.where(core == 0, rows[:QUARTER], low_q)
    high = jnp.where(core == 0, rows[QUARTER : 2 * QUARTER], high_q)
    return low, high


def collect_rows(blocks, place, pairs):
    low, high = blocks
    z = place[2]
    got = []
    for turn in range(2):
        perm = []
        for j in range(pairs):
            for c in range(2):
                for zz in range(MP):
                    u = (turn + zz) % 2
                    perm.append(((2 * j + zz // 2) * MP + 2 * c + u, (2 * j + c) * MP + zz))
        block = jnp.where((z + turn) % 2 == 0, low, high)
        got.append(lax.ppermute(block, ("dp", "mp"), perm))
    return jnp.where(z % 2 == 0, jnp.stack(got), jnp.stack(got[::-1]))


def gather_slots(values, steps, core):
    for axis, bit in steps:
        values = jnp.concatenate([values, swap_cores(values, axis, bit, core)])
    return values


def scatter_slots(values, steps, core):
    for axis, bit in reversed(steps):
        half = values.shape[0] // 2
        values = add_low(values[:half], swap_cores(values[half:], axis, bit, core))
    return values[0]


def on_device(
    tokens,
    attn_gain,
    w_query,
    w_key,
    w_value,
    w_out,
    ffn_gain,
    w_gate,
    w_up,
    w_down,
    rel_table,
    final_gain,
    w_proj,
    positives,
    retrieved,
):
    section = lax.axis_index("section")
    dp = lax.axis_index("dp")
    dp_count = lax.axis_size("dp")
    z = lax.axis_index("mp")
    core, y = dp % 2, (dp // 2) % 2
    place = (core, y, z)
    pairs = dp_count // 2
    chip = (dp // 2) * MP + z
    chips = pairs * MP
    is_doc = core == 0
    first = section == 0
    quad = dp % 4

    def piece_of(quarter):
        return lax.dynamic_slice_in_dim(quarter, quad * QUARTER, QUARTER, 0)

    attn_own = jnp.concatenate([w_query[0].T, w_key[0].T, w_value[0].T, w_out[0]])
    def ffn_owns(gate, up, down):
        whole = jnp.concatenate([gate[0], up[0], down[0].T], axis=1)
        return [whole[:, :F_HALF], whole[:, F_HALF:]]

    owns = [attn_own]
    own_pieces = [piece_of(attn_own)]
    got = {}

    def along_z(k, *which):
        for at in which:
            source = own_pieces[k] if at < 3 else got[k, 2, 0]
            got[k, at, 0] = swap(source, "mp", 1 if at == 3 else at)

    def along_y(k, *which):
        for at in which:
            got[k, at, 1] = swap(got[k, at, 0], "dp", 2)

    def to_core(k, m, *which):
        for at in which:
            got[k, at, 2 + m] = swap(got[k, at, m], "dp", 1)

    def hold(keys, *values):
        held, values = lax.optimization_barrier(([got[key] for key in keys], values))
        got.update(zip(keys, held))
        return values

    def chunk_of(k):
        return (owns[k],) + tuple(got[k, at, m] for at in range(1, MP) for m in range(4))

    heads_dev = rel_table.shape[1]
    buckets = rel_table.shape[0]
    half_count = buckets // 2
    bucket_ids = jnp.arange(buckets, dtype=jnp.int32)

    def flags_for(active):
        return jnp.stack([jnp.asarray(active).astype(jnp.int32), is_doc.astype(jnp.int32), z, quad])

    def bias_blocks(table):
        table = jnp.take(table, z ^ jnp.arange(MP), axis=0, mode="clip")
        table = jnp.swapaxes(table, 0, 1).reshape(buckets, -1)
        at = jnp.arange(BLK, dtype=jnp.int32)
        offset = at[:, None] - at[None, :]
        offsets = jnp.stack([offset, offset + BLK, offset - BLK])
        pick_near = (bucket_of(offsets, half_count)[..., None] == bucket_ids).astype(f32)
        bias = jnp.einsum("bh,mjib->hmji", table, pick_near, precision=highest)
        same_query = (at[:, None] // QRY_LEN) == (at[None, :] // QRY_LEN)
        return table, jnp.where(jnp.logical_or(is_doc, same_query), bias, -1e30)

    def band_picks(lanes):
        band_offset = jnp.where(lanes <= 2 * BLK + BLK - 1, BLK - lanes, 5 * BLK - lanes)
        ends = [jnp.full((BLK,), buckets - 1, jnp.int32), jnp.full((BLK,), half_count - 1, jnp.int32)]
        band_bucket = jnp.concatenate([bucket_of(band_offset, half_count)] + ends)
        return (band_bucket[:, None] == jnp.arange(BLK, dtype=jnp.int32)).astype(f32)

    topk = retrieved.shape[2]
    mb_of_slot = chip ^ jnp.arange(chips, dtype=jnp.int32)

    def counts_of(hits):
        hits = jnp.take(jnp.concatenate(hits), dp ^ jnp.arange(dp_count), axis=0, mode="clip").reshape(chips * QRYS_MB, -1)
        slot_retrieved = jnp.take(hits[:, : QRY_LEN * topk].reshape(chips, QRY_ROWS, topk), mb_of_slot, axis=0, mode="clip")
        flags = flags_for(jnp.logical_not(first))
        positives_slot = jnp.take(
            hits[:, QRY_LEN * topk :].reshape(chips, QRYS_MB, -1), mb_of_slot, axis=0, mode="clip"
        ).reshape(chips * QRYS_MB, -1)
        chosen = jnp.any(positives_slot[None] == mb_of_slot[:, None, None], axis=2).astype(f32)
        return chosen, count_hits(flags, slot_retrieved.reshape(-1, topk).T - chip * DOC_LEN)

    along_z(0, 2, 1)
    table = [rel_table] + [swap(rel_table, "mp", by) for by in range(1, MP)]
    w_gate, w_up, w_down, tokens, table, retrieved, positives = hold(
        [(0, 1, 0), (0, 2, 0)], w_gate, w_up, w_down, tokens, table, retrieved, positives
    )
    along_z(0, 3)
    along_y(0, 1, 2)
    to_core(0, 0, 1, 2)
    tokens = spread_tokens(tokens, place, pairs)
    owns += ffn_owns(w_gate, w_up, w_down)
    own_pieces += [piece_of(own) for own in owns[1:]]
    owns, own_pieces, tokens, table, retrieved, positives = hold(
        [(0, 3, 0), (0, 1, 1), (0, 2, 1)], owns, own_pieces, tokens, table, retrieved, positives
    )
    along_y(0, 3)
    to_core(0, 0, 3)
    to_core(0, 1, 1, 2)
    along_z(1, 2, 1)
    x_first = arrange_tokens(tokens, place)
    table, bias = bias_blocks(jnp.stack(table))
    x_first, table, bias, own_pieces[2], retrieved, positives = hold(
        [(0, 3, 1), (1, 1, 0), (1, 2, 0)], x_first, table, bias, own_pieces[2], retrieved, positives
    )
    hits = jnp.concatenate([retrieved.reshape(retrieved.shape[0], -1), positives], axis=1)[None]
    hits = [hits] + [swap(hits, "dp", by) for by in range(1, dp_count)]
    lanes = jnp.arange(chips * QRY_ROWS, dtype=jnp.int32)
    to_core(0, 1, 3)
    along_z(1, 3)
    along_z(2, 2, 1)
    along_y(1, 1, 2)
    to_core(1, 0, 1, 2)
    attn_weights = chunk_of(0)

    kept = []
    x = x_first
    for step in range(2):
        flags = flags_for(section == step)
        normed, qkv, lse, mixed, middle, normed_ffn = attn_fwd(flags, table, x, attn_gain, ffn_gain, bias, attn_weights)
        if step == 0:
            middle, normed_ffn, hits, lanes = hold(
                [(1, 3, 0), (1, 1, 1), (1, 2, 1), (2, 1, 0), (2, 2, 0)], middle, normed_ffn, hits, lanes
            )
            along_z(2, 3)
            along_y(2, 1, 2)
            along_y(1, 3)
            to_core(1, 0, 3)
            to_core(1, 1, 1, 2)
            to_core(2, 0, 1, 2)
            chosen, counts = counts_of(hits)
            expand = (lanes // QRY_LEN == jnp.arange(chips * QRYS_MB)[:, None]).astype(f32)
            chosen, counts, expand, pick_band = hold(
                [(2, 3, 0), (2, 1, 1), (2, 2, 1), (1, 3, 1)], chosen, counts, expand, band_picks(lanes[: 4 * BLK])
            )
            along_y(2, 3)
            to_core(1, 1, 3)
            to_core(2, 0, 3)
            to_core(2, 1, 1, 2)
            hold([(2, 3, 1)])
            to_core(2, 1, 3)
            ffn_weights = chunk_of(1) + chunk_of(2)
        out, low, low_high, hidden, ga, gb, normed_final, embed = ffn_fwd(
            flags, final_gain[None], w_proj, middle, normed_ffn, ffn_weights
        )
        kept.append((x, normed, qkv, lse, mixed, middle, normed_ffn, hidden, ga, gb))
        if step == 0:
            x = hop((low, low_high), 0)

    live = jnp.logical_not(first)
    scale = PROJ ** (-0.5)
    steps = [("mp", 1), ("mp", 2)]
    bit = 2
    while bit < dp_count:
        steps.append(("dp", bit))
        bit *= 2
    query_slots = swap(gather_slots(embed[None, :QRY_ROWS], steps, 1), "dp", 1).reshape(-1, PROJ)
    shares, share_query, mass = score(flags_for(live), query_slots, embed, counts)
    logit = logit_scale * jnp.mean(jnp.log1p(mass).reshape(chips * QRYS_MB, QRY_LEN), axis=1)
    logits = logit[None]
    for at, (axis, bit) in enumerate(steps):
        got_logits = swap_cores(logits, axis, bit, 0)
        turned = got_logits.reshape(got_logits.shape[0], -1, 2, QRYS_MB << at)[:, :, ::-1]
        logits = jnp.concatenate([logits, turned.reshape(got_logits.shape)])
    coef, grad_query, loss_here = coefs(flags_for(live), logits, chosen, expand, share_query)
    grad_query = scatter_slots(swap(grad_query.reshape(chips, QRY_ROWS, PROJ), "dp", 1), steps, 1)
    lead = jnp.logical_and(live, jnp.logical_and(dp == 0, z == 0))
    loss_here = jnp.where(lead, loss_here, 0.0)
    *grad_final, early_own = head_bwd(
        flags_for(live), shares, query_slots, coef, grad_query, loss_here, normed_final, out, final_gain[None], w_proj
    )
    early = (early_own + swap(early_own, "section", 1)).astype(f32)

    def ffn_back(step, grad_out, prev):
        x, normed, qkv, lse, mixed, middle, normed_ffn, hidden, ga, gb = kept[step]
        flags = flags_for(section == step)
        return ffn_bwd(flags, grad_out, middle, ffn_gain, normed_ffn, hidden, ga, gb, ffn_weights, prev)

    def attn_back(step, gmid, ffn_gain_grad, prev):
        x, normed, qkv, lse, mixed, middle, normed_ffn, hidden, ga, gb = kept[step]
        flags = flags_for(section == step)
        return attn_bwd(
            flags, table, gmid, x, attn_gain, bias, pick_band, ffn_gain_grad, early, normed, qkv, lse, mixed, attn_weights, prev
        )

    gmid, *ffn_prev = ffn_back(1, grad_final, None)
    attn_prev = attn_back(1, gmid, ffn_prev[0], None)
    gmid, grad_ffn_gain, f1_keep, f1_send, f2_keep, f2_send = ffn_back(0, hop(attn_prev[:2], 1), ffn_prev)

    zl, zh = z % 2, z // 2

    def parts(values):
        return values.reshape(2, 2, 2, -1, values.shape[-1])

    def both(keep, send):
        return [(parts(keep), ()), (parts(swap(send, "dp", 1)), ())]

    f1, f2, gmid = fence_terms((both(f1_keep, f1_send), both(f2_keep, f2_send)), gmid)
    f1_got = give(f1, 2, "dp", 2, y)
    f2_got = give(f2, 1, "mp", 1, zl)
    gx, gx_high, _, a_keep, a_send = attn_back(0, gmid, grad_ffn_gain, attn_prev)
    f1, f2, f1_got, f2_got, a_keep, a_send, gx = fence_terms((f1, f2), f1_got, f2_got, a_keep, a_send, gx)
    f1, f2 = take(f1, 2, y, f1_got), take(f2, 1, zl, f2_got)
    out_f1, out_f2 = total_of(f1, ((1, 1 - zl),)), total_of(f2, ((0, 1 - zh),))
    n_small = SMALL - 8
    a = both(a_keep, a_send)
    a, out_f1, out_f2 = fence_terms((a,), out_f1, out_f2)
    f1_got, f2_got = swap(out_f1, "mp", 1), swap(out_f2, "mp", 2)
    a_got = give(a, 2, "dp", 2, y)
    f1, f2, a, f1_got, f2_got, a_got, gx = fence_terms((f1, f2, a), f1_got, f2_got, a_got, gx)

    blocks = split_rows(jnp.concatenate([gx, gx_high]), place)
    f1, f2, a = take(f1, 1, zl, f1_got), take(f2, 0, zh, f2_got), take(a, 2, y, a_got)
    a_got = give(a, 1, "mp", 1, zl)
    f1_got = give(f1, 0, "mp", 2, zh)
    f2 = total_of(f2)
    f2_got = swap(f2, "dp", 2)

    a = take(a, 1, zl, a_got)
    a_got = give(a, 0, "mp", 2, zh)
    f1 = over_rest(total_of(take(f1, 0, zh, f1_got)))
    f1_got = swap(f1, "dp", 2)
    f2 = over_rest(add_low(f2, f2_got))
    f2_other = swap(f2, "dp", 1)

    a, blocks = fence(over_rest(total_of(take(a, 0, zh, a_got))), blocks)
    a_got = swap(a, "dp", 2)
    d_inputs = collect_rows(blocks, place, pairs)[None]
    f1 = in_order(y, f1, f1_got)
    f1_other = swap(f1, "dp", 1)
    flags_end = flags_for(1)
    ffn_sums = finish(finish_ffn_kernel, flags_end, [(D, FQ), (D, FQ), (FQ, D)], f1, f1_other, f2, f2_other)

    a, a_got, d_inputs = fence(a, a_got, d_inputs)
    small_sum = a[QUARTER : QUARTER + n_small].astype(f32)
    table_other = swap(small_sum[:heads_dev], "section", 1)
    a = in_order(y, a, a_got)
    a_other = swap(a, "dp", 1)
    attn_sums = finish(finish_attn_kernel, flags_end, [(QUARTER, D)] * 4, a, a_other)
    proj_sum = in_order(core, a[:, QUARTER + n_small :], a_other[:, QUARTER + n_small :])
    proj_sum = proj_sum.astype(f32).reshape(PROJ // MP, D)
    shared_sum = small_sum[heads_dev:]
    grad_table = (small_sum[:heads_dev] + table_other)[:, :buckets].T
    return (
        shared_sum[3, 0] + shared_sum[4, 0],
        d_inputs,
        shared_sum[0:1],
        attn_sums[0].T[None],
        attn_sums[1].T[None],
        attn_sums[2].T[None],
        attn_sums[3][None],
        shared_sum[1:2],
        ffn_sums[0][None],
        ffn_sums[1][None],
        ffn_sums[2][None],
        grad_table,
        shared_sum[2],
        proj_sum.T,
    )


def solution(mesh):
    return jax.shard_map(
        on_device,
        mesh=mesh,
        in_specs=(
            P("dp", "mp", None),
            P("section", None),
            P("section", None, "mp"),
            P("section", None, "mp"),
            P("section", None, "mp"),
            P("section", "mp", None),
            P("section", None),
            P("section", None, "mp"),
            P("section", None, "mp"),
            P("section", "mp", None),
            P(None, "mp"),
            P(),
            P(),
            P("dp", None),
            P("dp", None, None),
        ),
        out_specs=(
            P(),
            P("section", "dp", "mp", None),
            P("section", None),
            P("section", None, "mp"),
            P("section", None, "mp"),
            P("section", None, "mp"),
            P("section", "mp", None),
            P("section", None),
            P("section", None, "mp"),
            P("section", None, "mp"),
            P("section", "mp", None),
            P(None, "mp"),
            P(),
            P(None, "mp"),
        ),
        check_vma=False,
    )
```

```python
import functools

import jax
import jax.numpy as jnp
from jax import lax
from jax.experimental import pallas as pl
from jax.experimental.pallas import tpu as pltpu
from jax.sharding import PartitionSpec as P

D = 768
HEAD_DIM = 64
FF = 2048
PROJ = 128
DOC_LEN = 512
QRY_LEN = 32
QRYS_MB = 8
QRY_ROWS = QRYS_MB * QRY_LEN
MP = 4
QUARTER = D // MP
FQ = FF // MP
HEADS_Q = QUARTER // HEAD_DIM
BLK = 128
NBLK = DOC_LEN // BLK
QKV = 3 * QUARTER
SMALL = 16
F_HALF = 3 * FQ // 2

bucket_edges = (8, 12, 16, 23, 32, 46, 64, 91)
norm_eps = 1e-06
logit_scale = 16.0
highest = lax.Precision.HIGHEST
f32 = jnp.float32
bf16 = jnp.bfloat16

ACT, IS_DOC, ZPOS, RPOS = range(4)
VMEM_LIMIT = 56 * 1024 * 1024


def mm(a, b):
    return jnp.dot(a, b, preferred_element_type=f32)


def mm_t(a, b):
    return lax.dot_general(a, b, (((1,), (1,)), ((), ())), preferred_element_type=f32)


def t_mm(a, b):
    return lax.dot_general(a, b, (((0,), (0,)), ((), ())), preferred_element_type=f32)


def bucket_of(offset, half_count):
    spread = jnp.abs(offset)
    far_bucket = 7 + sum((spread >= edge).astype(jnp.int32) for edge in bucket_edges)
    near_bucket = jnp.where(spread < 8, spread, far_bucket)
    return near_bucket + half_count * (offset > 0).astype(jnp.int32)


class Copies:
    def __init__(self, sem, first=0):
        self.sem = sem
        self.next = first

    def __call__(self, source, target):
        copy = pltpu.make_async_copy(source, target, self.sem.at[self.next])
        self.next += 1
        copy.start()
        return copy


def get_rows(copy, halves, target, doc):
    count = 2 if doc else 1
    return [copy(halves[i], target.at[pl.ds(i * QRY_ROWS, QRY_ROWS)]) for i in range(count)]


def put_rows(copy, source, halves, doc):
    count = 2 if doc else 1
    return [copy(source.at[pl.ds(i * QRY_ROWS, QRY_ROWS)], halves[i]) for i in range(count)]


def wait_all(copies):
    for copy in copies:
        copy.wait()


class Weights:
    def __init__(self, flags, chunk, target, sem, lanes=None):
        self.z, self.r = flags[ZPOS], flags[RPOS]
        self.own, self.pieces = chunk[0], chunk[1:]
        self.target, self.sem = target, sem
        self.lanes = pl.ds(0, target.shape[2]) if lanes is None else lanes

    def copies(self, s):
        if s == 0:
            return [pltpu.make_async_copy(self.own, self.target.at[self.z, :, self.lanes], self.sem.at[0, 0])]
        return [
            pltpu.make_async_copy(
                self.pieces[4 * (s - 1) + k],
                self.target.at[self.z ^ s, rows_at(self.r ^ bits, QUARTER), self.lanes],
                self.sem.at[s, k],
            )
            for k, bits in enumerate((0, 2, 1, 3))
        ]

    def start(self):
        for s in range(MP):
            start_all(self.copies(s))

    def each(self, s, act):
        for k in range(MP):
            pl.when(s == k)(lambda k=k: act(self.copies(k)))

    def start_slot(self, s):
        self.each(s, start_all)

    def wait_slot(self, s):
        self.each(s, wait_all)


N_CHUNK = 13


def start_all(copies):
    for copy in copies:
        copy.start()


def rows_at(index, size):
    return pl.ds(pl.multiple_of(index * size, size), size)


def offset_bias(table):
    column = lax.broadcasted_iota(jnp.int32, (table.shape[0], 4 * BLK), 1)
    bucket = lax.broadcasted_iota(jnp.int32, (table.shape[0], 4 * BLK), 0)
    offset = jnp.where(column < 2 * BLK, -column, 4 * BLK - column)
    hot = (bucket_of(offset, table.shape[0] // 2) == bucket).astype(f32)
    return lax.dot_general(table, hot, (((0,), (0,)), ((), ())), precision=highest, preferred_element_type=f32)


def near_blocks(offsets_ref, head):
    row = jnp.broadcast_to(offsets_ref[pl.ds(head, 1), :], (BLK, 4 * BLK))
    rolled = pltpu.roll(row, 0, 1, stride=1, stride_axis=0)
    return {0: rolled[:, :BLK], -1: rolled[:, BLK : 2 * BLK], 1: rolled[:, 3 * BLK :]}


def bias_matrix(offsets_ref, table_ref, head):
    far_up = jnp.full((BLK, BLK), table_ref[31, head], f32)
    far_low = jnp.full((BLK, BLK), table_ref[15, head], f32)
    near = near_blocks(offsets_ref, head)

    def block(bj, bi):
        if bj - bi in near:
            return near[bj - bi]
        return far_up if bj > bi else far_low

    return jnp.concatenate(
        [jnp.concatenate([block(bj, bi) for bi in range(NBLK)], axis=1) for bj in range(NBLK)], axis=0
    )


def query_bias(offsets_ref, head):
    j = lax.broadcasted_iota(jnp.int32, (BLK, BLK), 0) // QRY_LEN
    i = lax.broadcasted_iota(jnp.int32, (BLK, BLK), 1) // QRY_LEN
    return jnp.where(i == j, near_blocks(offsets_ref, head)[0], -1e30)


def rms_parts(values):
    return lax.rsqrt(jnp.mean(values * values, axis=-1, keepdims=True) + norm_eps)


def rms_back(values, gain, grad):
    scale = rms_parts(values)
    weighted = grad * gain
    inner = jnp.mean(values * weighted, axis=-1, keepdims=True)
    out = scale * (weighted - values * (scale * scale * inner))
    gain_grad = jnp.sum(grad * values * scale, axis=0, keepdims=True)
    return out, gain_grad


def by_kind(flags, body):
    pl.when(flags[IS_DOC] == 1)(lambda: body(DOC_LEN, True))
    pl.when(flags[IS_DOC] == 0)(lambda: body(QRY_ROWS, False))


def head_slices(hh):
    at = hh * HEAD_DIM
    return (
        slice(at, at + HEAD_DIM),
        slice(QUARTER + at, QUARTER + at + HEAD_DIM),
        slice(2 * QUARTER + at, 2 * QUARTER + at + HEAD_DIM),
        slice(at, at + HEAD_DIM),
    )


def attn_fwd_kernel(flags, table, table_ref, attn_gain_ref, ffn_gain_ref, x_low, x_high, *refs):
    weights, refs = refs[:N_CHUNK], refs[N_CHUNK:]
    normed_out, qkv_out, lse_out, mixed_out, middle_out, normed_ffn_out = refs[:6]
    x_ref, offsets_ref, normed_ref, qkv_ref, lse_ref, mixed_ref, middle_ref, normed_ffn_ref = refs[6:14]
    wa, sem, asem, zsem = refs[14:]
    weights = Weights(flags, weights, wa, asem)
    def one_head(z, hh, rows, bias):
        qs, ks, vs, ms = head_slices(hh)
        q, k, v = qkv_ref[z, rows, qs], qkv_ref[z, rows, ks], qkv_ref[z, rows, vs]
        scores = mm_t(k, q) + bias
        peak = jnp.max(scores, axis=0, keepdims=True)
        weights = jnp.exp(scores - peak)
        total = jnp.sum(weights, axis=0, keepdims=True)
        mixed = t_mm(v, weights.astype(bf16)) * (1.0 / total)
        lse_ref[z, hh : hh + 1, rows] = peak + jnp.log(total)
        mixed_ref[z, rows, ms] = mixed.T.astype(bf16)

    def body(rows, doc):
        put = Copies(sem)
        outs = []
        get_x = get_rows(put, (x_low, x_high), x_ref, doc)
        weights.start()
        offsets_ref[...] = offset_bias(table_ref[...])
        wait_all(get_x)

        def send(source, target):
            outs.append(put(source.at[pl.ds(0, rows)], target.at[pl.ds(0, rows)]))

        def parts(z):
            return [
                pltpu.make_async_copy(a.at[z, pl.ds(0, rows)], b.at[z, pl.ds(0, rows)], zsem.at[z, i])
                for i, (a, b) in enumerate(((qkv_ref, qkv_out), (mixed_ref, mixed_out)))
            ]

        x = x_ref[:rows].astype(f32)
        normed_ref[:rows] = (x * rms_parts(x) * attn_gain_ref[...]).astype(bf16)
        send(normed_ref, normed_out)

        @pl.loop(0, MP)
        def _(s):
            z = flags[ZPOS] ^ s
            weights.wait_slot(s)
            qkv_ref[z, :rows] = mm_t(normed_ref[:rows], wa[z, :QKV]).astype(bf16)
            for hh in range(HEADS_Q):
                head = z * HEADS_Q + hh
                if doc:
                    one_head(z, hh, slice(0, DOC_LEN), bias_matrix(offsets_ref, table, head))
                else:
                    bias = query_bias(offsets_ref, head)
                    for b in range(QRY_ROWS // BLK):
                        one_head(z, hh, slice(b * BLK, (b + 1) * BLK), bias)
            start_all(parts(z))

        outs.append(put(lse_ref, lse_out))
        middle_ref[:rows] = x_ref[:rows].astype(f32)

        @pl.loop(0, MP)
        def _(z):
            middle_ref[:rows] += mm(mixed_ref[z, :rows], wa[z, QKV:])

        middle = middle_ref[:rows]
        send(middle_ref, middle_out)
        normed_ffn_ref[:rows] = (middle * rms_parts(middle) * ffn_gain_ref[...]).astype(bf16)
        send(normed_ffn_ref, normed_ffn_out)

        @pl.loop(0, MP)
        def _(z):
            wait_all(parts(z))

        wait_all(outs)

    @pl.when(flags[ACT] == 1)
    def _():
        by_kind(flags, body)


def ffn_fwd_kernel(flags, final_gain_ref, proj_ref, middle_hbm, normed_hbm, *refs):
    first, second, refs = refs[:N_CHUNK], refs[N_CHUNK : 2 * N_CHUNK], refs[2 * N_CHUNK :]
    out_out, low_low, low_high, hidden_out, ga_out, gb_out, final_out, embed_out = refs[:8]
    normed_ref, out_ref, low_ref, hidden_ref, ga_ref, gb_ref, final_ref, embed_ref = refs[8:16]
    wf, sem, fsem, gsem, zsem = refs[16:]
    first = Weights(flags, first, wf, fsem, pl.ds(0, F_HALF))
    second = Weights(flags, second, wf, gsem, pl.ds(F_HALF, F_HALF))

    def body(rows, doc):
        copy = Copies(sem)
        get_normed = copy(normed_hbm.at[pl.ds(0, rows)], normed_ref.at[pl.ds(0, rows)])
        get_middle = copy(middle_hbm.at[pl.ds(0, rows)], out_ref.at[pl.ds(0, rows)])
        first.start_slot(0)
        second.start_slot(0)

        def parts(z):
            pairs = ((hidden_ref, hidden_out), (ga_ref, ga_out), (gb_ref, gb_out))
            return [
                pltpu.make_async_copy(a.at[z, pl.ds(0, rows)], b.at[z, pl.ds(0, rows)], zsem.at[z, i])
                for i, (a, b) in enumerate(pairs)
            ]

        get_normed.wait()
        get_middle.wait()

        @pl.loop(0, MP)
        def _(s):
            z = flags[ZPOS] ^ s

            first.start_slot(s + 1)
            second.start_slot(s + 1)
            first.wait_slot(s)
            second.wait_slot(s)
            normed = normed_ref[:rows]
            gate = mm(normed, wf[z, :, :FQ])
            up = mm(normed, wf[z, :, FQ : 2 * FQ])
            coef = 0.7978845608028654
            square = gate * gate
            tanh = jnp.tanh(coef * gate * (1.0 + 0.044715 * square))
            half = 0.5 + 0.5 * tanh
            gelu = gate * half
            slope = half + (0.5 * coef) * gate * (1.0 - tanh * tanh) * (1.0 + 3 * 0.044715 * square)
            hidden = (gelu * up).astype(bf16)
            hidden_ref[z, :rows] = hidden
            ga_ref[z, :rows] = (up * slope).astype(bf16)
            gb_ref[z, :rows] = gelu.astype(bf16)
            start_all(parts(z))
            out_ref[:rows] += mm_t(hidden, wf[z, :, 2 * FQ :])

        low_ref[:rows] = out_ref[:rows].astype(bf16)
        if not doc:
            out_ref[rows:] = jnp.zeros((DOC_LEN - rows, D), f32)
            final_ref[rows:] = jnp.zeros((DOC_LEN - rows, D), bf16)
        outs = put_rows(copy, low_ref, (low_low, low_high), doc) + [copy(out_ref, out_out)]
        out = out_ref[:rows]
        final_ref[:rows] = (out * rms_parts(out) * final_gain_ref[...]).astype(bf16)
        embed_ref[:rows] = mm(final_ref[:rows], proj_ref[...]).astype(bf16)
        outs.append(copy(embed_ref.at[pl.ds(0, rows)], embed_out.at[pl.ds(0, rows)]))
        outs.append(copy(final_ref, final_out))

        @pl.loop(0, MP)
        def _(z):
            wait_all(parts(z))

        wait_all(outs)

    @pl.when(flags[ACT] == 1)
    def _():
        by_kind(flags, body)


def ffn_bwd_kernel(
    flags, gain_ref, gout_low, gout_high, middle_hbm, normed_hbm, hidden_hbm, ga_hbm, gb_hbm,
    *refs,
):
    gmid_out, dgain_out, *df_outs = refs[-24:-18]
    gout_ref, middle_ref, normed_ref, hidden_ref, ga_ref, gb_ref, gmid_ref, dgain_ref = refs[-18:-10]
    wf, gout_t, normed_t, df_buf, gn, sem, fsem, gsem, ksem, osem = refs[-10:]
    first = Weights(flags, refs[:N_CHUNK], wf, fsem, pl.ds(0, F_HALF))
    second = Weights(flags, refs[N_CHUNK : 2 * N_CHUNK], wf, gsem, pl.ds(F_HALF, F_HALF))

    def outs(s, core):
        slot, half, z = s % 2, D // 2, flags[ZPOS] ^ s
        copies = []
        for i, out in enumerate(df_outs):
            rows = pl.ds((core if i % 2 == 0 else 1 - core) * half, half)
            lanes = pl.ds(i // 2 * F_HALF, F_HALF)
            copies.append(pltpu.make_async_copy(df_buf.at[slot, rows, lanes], out.at[z], osem.at[slot, i]))
        return copies

    def body(rows, doc):
        core = 0 if doc else 1
        copy = Copies(sem)

        def get(source, target):
            return copy(source.at[pl.ds(0, rows)], target.at[pl.ds(0, rows)])

        get_gout = get_rows(copy, (gout_low, gout_high), gout_ref, doc)
        get_normed = get(normed_hbm, normed_ref)
        kept = ((ga_hbm, ga_ref), (gb_hbm, gb_ref), (hidden_hbm, hidden_ref))

        def part(z):
            return [
                pltpu.make_async_copy(a.at[z, pl.ds(0, rows)], b.at[z, pl.ds(0, rows)], ksem.at[z, i])
                for i, (a, b) in enumerate(kept)
            ]

        first.start_slot(0)
        second.start_slot(0)
        start_all(part(flags[ZPOS]))
        get_middle = get(middle_hbm, middle_ref)
        wait_all(get_gout)
        gout_t[:, :rows] = gout_ref[:rows].T
        get_normed.wait()
        normed_t[:, :rows] = normed_ref[:rows].T
        gn[:rows] = jnp.zeros((rows, D), f32)

        @pl.loop(0, MP)
        def _(s):
            z = flags[ZPOS] ^ s
            pl.when(s >= 2)(lambda: wait_all(outs(s - 2, core)))

            first.start_slot(s + 1)
            second.start_slot(s + 1)
            pl.when(s + 1 < MP)(lambda: start_all(part(flags[ZPOS] ^ (s + 1))))
            first.wait_slot(s)
            second.wait_slot(s)
            wait_all(part(z))
            slot = s % 2
            grad_hidden = mm(gout_ref[:rows], wf[z, :, 2 * FQ :])
            grad_gate = (grad_hidden * ga_ref[z, :rows].astype(f32)).astype(bf16)
            grad_up = (grad_hidden * gb_ref[z, :rows].astype(f32)).astype(bf16)
            df_buf[slot, :, :FQ] = mm(normed_t[:, :rows], grad_gate).astype(bf16)
            df_buf[slot, :, FQ : 2 * FQ] = mm(normed_t[:, :rows], grad_up).astype(bf16)
            df_buf[slot, :, 2 * FQ :] = mm(gout_t[:, :rows], hidden_ref[z, :rows]).astype(bf16)
            start_all(outs(s, core))
            gn[:rows] += mm_t(grad_gate, wf[z, :, :FQ]) + mm_t(grad_up, wf[z, :, FQ : 2 * FQ])

        get_middle.wait()
        back, gain_grad = rms_back(middle_ref[:rows], gain_ref[...], gn[:rows])
        gmid_ref[:rows] = gout_ref[:rows].astype(f32) + back
        dgain_ref[...] = gain_grad
        last = [copy(gmid_ref.at[pl.ds(0, rows)], gmid_out.at[pl.ds(0, rows)]), copy(dgain_ref, dgain_out)]
        for s in (MP - 2, MP - 1):
            wait_all(outs(s, core))
        wait_all(last)

    @pl.when(flags[ACT] == 1)
    def _():
        by_kind(flags, body)


def attn_bwd_kernel(
    flags, table, table_ref, gain_ref, band_ref, ffn_gain_ref, early_ref, gmid_hbm, x_low, x_high, normed_hbm, qkv_hbm, lse_hbm,
    mixed_hbm, *refs,
):
    gx_low, gx_high, dgain_out, *da_outs = refs[-27:-22]
    gmid_ref, x_ref, offsets_ref, normed_ref, qkv_ref, lse_ref, mixed_ref, gx_ref, dgain_ref, diag_ref = refs[-22:-12]
    wa, gmb, gmix, gqkv, da_buf, gn, rows_buf, sem, asem, ksem, osem, rsem = refs[-12:]
    weights = Weights(flags, refs[:N_CHUNK], wa, asem)

    def one_head(z, hh, rows, bias):
        qs, ks, vs, ms = head_slices(hh)
        q, k, v = qkv_ref[z, rows, qs], qkv_ref[z, rows, ks], qkv_ref[z, rows, vs]
        go = gmix[rows, ms]
        out = mixed_ref[z, rows, ms].astype(f32)
        delta = jnp.sum((go.astype(f32) * out).T, axis=0, keepdims=True)
        probs = jnp.exp(mm_t(k, q) + bias - lse_ref[z, hh : hh + 1, rows])
        grad_scores = probs * (mm_t(v, go) - delta)
        low = grad_scores.astype(bf16)
        gqkv[rows, qs] = t_mm(k, low).T.astype(bf16)
        gqkv[rows, ks] = mm(low, q).astype(bf16)
        gqkv[rows, vs] = mm(probs.astype(bf16), go).astype(bf16)
        return grad_scores

    def band_sums(up, mid, low):
        blank = jnp.zeros((BLK, BLK), f32)
        band = jnp.concatenate([up, mid, low, blank], axis=1)
        width = 4 * BLK

        def left(part, by):
            return pltpu.roll(part, width - by, 1) if by else part

        eight = functools.reduce(jnp.add, [left(band[g : g + 8], g) for g in range(0, BLK, 8)])
        return functools.reduce(jnp.add, [left(eight[r : r + 1], r) for r in range(8)])

    def outs(s, core):
        slot, z = s % 2, flags[ZPOS] ^ s
        copies = []
        for i, out in enumerate(da_outs):
            for half in range(2):
                rows = pl.ds((core if i == 0 else 1 - core) * (D // 2) + half * QUARTER, QUARTER)
                target = out.at[z, half, pl.ds(0, QUARTER), :]
                copies.append(pltpu.make_async_copy(da_buf.at[slot, rows, :], target, osem.at[slot, 2 * i + half]))
        return copies

    def body(rows, doc):
        core = 0 if doc else 1
        copy = Copies(sem)

        def get(source, target):
            return copy(source.at[pl.ds(0, rows)], target.at[pl.ds(0, rows)])

        get_gmid = get(gmid_hbm, gmid_ref)
        get_lse = copy(lse_hbm, lse_ref)
        kept = ((qkv_hbm, qkv_ref), (mixed_hbm, mixed_ref))

        def part(z):
            return [
                pltpu.make_async_copy(a.at[z, pl.ds(0, rows)], b.at[z, pl.ds(0, rows)], ksem.at[z, i])
                for i, (a, b) in enumerate(kept)
            ]

        weights.start_slot(0)
        start_all(part(flags[ZPOS]))
        offsets_ref[...] = offset_bias(table_ref[...])
        get_normed = get(normed_hbm, normed_ref)
        get_x = get_rows(copy, (x_low, x_high), x_ref, doc)
        get_gmid.wait()
        gmb[:rows] = gmid_ref[:rows].astype(bf16)
        gn[:rows] = jnp.zeros((rows, D), f32)
        get_lse.wait()
        get_normed.wait()

        @pl.loop(0, MP)
        def _(s):
            z = flags[ZPOS] ^ s
            pl.when(s >= 2)(lambda: wait_all(outs(s - 2, core)))

            weights.start_slot(s + 1)
            pl.when(s + 1 < MP)(lambda: start_all(part(flags[ZPOS] ^ (s + 1))))
            weights.wait_slot(s)
            wait_all(part(z))
            slot = s % 2
            gmix[:rows] = mm_t(gmb[:rows], wa[z, QKV:]).astype(bf16)
            for hh in range(HEADS_Q):
                head = z * HEADS_Q + hh
                if doc:
                    grads = one_head(z, hh, slice(0, DOC_LEN), bias_matrix(offsets_ref, table, head))

                    def blocks(test):
                        picked = [
                            grads[bj * BLK : (bj + 1) * BLK, bi * BLK : (bi + 1) * BLK]
                            for bj in range(NBLK)
                            for bi in range(NBLK)
                            if test(bj - bi)
                        ]
                        return functools.reduce(jnp.add, picked)

                    sums = band_sums(blocks(lambda d: d == 1), blocks(lambda d: d == 0), blocks(lambda d: d == -1))
                    far_up = jnp.sum(blocks(lambda d: d > 1), axis=0, keepdims=True)
                    far_low = jnp.sum(blocks(lambda d: d < -1), axis=0, keepdims=True)
                    diag_ref[z, hh : hh + 1, :] = jnp.concatenate([sums, far_up, far_low], axis=1)
                else:
                    grads = jnp.zeros((BLK, BLK), f32)
                    bias = query_bias(offsets_ref, head)
                    for b in range(QRY_ROWS // BLK):
                        grads = grads + one_head(z, hh, slice(b * BLK, (b + 1) * BLK), bias)
                    blank = jnp.zeros((BLK, BLK), f32)
                    sums = band_sums(blank, grads, blank)
                    diag_ref[z, hh : hh + 1, :] = jnp.concatenate([sums, jnp.zeros((1, 2 * BLK), f32)], axis=1)
            grads = gqkv[:rows]
            da_buf[slot, :QKV] = t_mm(grads, normed_ref[:rows]).astype(bf16)
            da_buf[slot, QKV:] = t_mm(mixed_ref[z, :rows], gmb[:rows]).astype(bf16)
            start_all(outs(s, core))
            gn[:rows] += mm(grads, wa[z, :QKV])

        wait_all(get_x)
        back, gain_grad = rms_back(x_ref[:rows].astype(f32), gain_ref[...], gn[:rows])
        gx_ref[:rows] = (gmid_ref[:rows] + back).astype(bf16)
        dgain_ref[...] = gain_grad
        last = put_rows(copy, gx_ref, (gx_low, gx_high), doc) + [copy(dgain_ref, dgain_out)]
        for z in range(MP):
            sums = jnp.dot(diag_ref[z], band_ref[...], precision=highest, preferred_element_type=f32)
            shared = [
                jnp.concatenate([sums[:HEADS_Q], jnp.zeros((HEADS_Q, D - BLK), f32)], axis=1),
                gain_grad,
                ffn_gain_ref[...],
                early_ref[PROJ : PROJ + 3],
            ]
            shared = jnp.concatenate(shared, axis=0)
            for which, side in enumerate((core, 1 - core)):
                for half in range(2):
                    first = z * (PROJ // MP) + side * 16 + half * 8
                    both = jnp.concatenate([shared, early_ref[first : first + 8]], axis=0)
                    rows_buf[which, z, half] = both.astype(bf16)
        for which, out in enumerate(da_outs):
            target = out.at[:, :, pl.ds(QUARTER, SMALL), :]
            last.append(pltpu.make_async_copy(rows_buf.at[which], target, rsem.at[which]))
            last[-1].start()
        for s in (MP - 2, MP - 1):
            wait_all(outs(s, core))
        wait_all(last)

    @pl.when(flags[ACT] == 1)
    def _():
        by_kind(flags, body)


def put_all(refs):
    count = len(refs) // 2
    copies = [pltpu.make_async_copy(refs[count + i], refs[i], refs[-1].at[i]) for i in range(count)]
    start_all(copies)
    wait_all(copies)


def finish_ffn_kernel(flags, mine1, other1, mine2, other2, *refs):
    gate_ref, up_ref, down_ref = refs[3:6]
    core = flags[RPOS] % 2
    half = D // 2
    for side, first, second in ((core, mine1, mine2), (1 - core, other1, other2)):
        rows = rows_at(side, half)
        low = first[...].reshape(half, F_HALF).astype(f32)
        high = second[...].reshape(half, F_HALF).astype(f32)
        gate_ref[rows, :] = low[:, :FQ]
        up_ref[rows, : F_HALF - FQ] = low[:, FQ:]
        up_ref[rows, F_HALF - FQ :] = high[:, : 2 * FQ - F_HALF]
        down = high[:, 2 * FQ - F_HALF :].T

        @pl.when(side == 0)
        def _():
            down_ref[:, :half] = down

        @pl.when(side == 1)
        def _():
            down_ref[:, half:] = down

    put_all(refs)


def finish_attn_kernel(flags, mine, other, *refs):
    buffers = refs[4:8]
    core = flags[RPOS] % 2
    for side in range(2):

        @pl.when(core == side)
        def _():
            for i in range(2):
                buffers[2 * side + i][...] = mine[i, :QUARTER].astype(f32)
                buffers[2 - 2 * side + i][...] = other[i, :QUARTER].astype(f32)

    put_all(refs)


def vmem():
    return pl.BlockSpec(memory_space=pltpu.VMEM)


def smem():
    return pl.BlockSpec(memory_space=pltpu.SMEM)


def hbm():
    return pl.BlockSpec(memory_space=pl.ANY)


def shape(dims, kind):
    return jax.ShapeDtypeStruct(dims, kind)


def params():
    return pltpu.CompilerParams(vmem_limit_bytes=VMEM_LIMIT)


def cost(microseconds):
    return pl.CostEstimate(flops=int(microseconds * 1e9), bytes_accessed=16 * 1024 * 1024, transcendentals=0)


def count_kernel(flags, hits_ref, counts_out, buffer, sem):
    width = buffer.shape[2]
    blocks = hits_ref.shape[1] // width

    def put(i):
        lanes = pl.ds(pl.multiple_of(i * width, width), width)
        return pltpu.make_async_copy(buffer.at[i % 2], counts_out.at[:, lanes], sem.at[i % 2])

    @pl.when(jnp.logical_and(flags[ACT] == 1, flags[IS_DOC] == 1))
    def _():
        @pl.loop(0, blocks)
        def _(i):
            pl.when(i >= 2)(lambda: put(i - 2).wait())
            hits = hits_ref[:, pl.ds(pl.multiple_of(i * width, width), width)]
            for row in range(0, DOC_LEN, BLK):
                places = lax.broadcasted_iota(jnp.int32, (BLK, width), 0) + row
                total = jnp.zeros((BLK, width), f32)
                for k in range(hits.shape[0]):
                    total = total + (hits[k : k + 1] == places).astype(f32)
                buffer[i % 2, row : row + BLK] = total.astype(bf16)
            put(i).start()

        put(blocks - 2).wait()
        put(blocks - 1).wait()


def count_hits(flags, hits):
    width = BLK
    return pl.pallas_call(
        count_kernel,
        in_specs=[smem(), vmem()],
        out_specs=hbm(),
        out_shape=shape((DOC_LEN, hits.shape[1]), bf16),
        scratch_shapes=[pltpu.VMEM((2, DOC_LEN, width), bf16), pltpu.SemaphoreType.DMA((2,))],
        compiler_params=params(),
        cost_estimate=cost(8),
        name="count_hits",
    )(flags, hits)


QUARTERS = (MP, DOC_LEN, FQ)
ROWS = (DOC_LEN, D)
HALF_ROWS = (QRY_ROWS, D)


def on_vmem(shapes):
    return [pltpu.VMEM(s.shape, s.dtype) for s in shapes]


def attn_fwd(flags, table, x, attn_gain, ffn_gain, attn_weights):
    results = [
        shape(ROWS, bf16),
        shape((MP, DOC_LEN, QKV), bf16),
        shape((MP, 8, DOC_LEN), f32),
        shape((MP, DOC_LEN, QUARTER), bf16),
        shape(ROWS, f32),
        shape(ROWS, bf16),
    ]
    return pl.pallas_call(
        attn_fwd_kernel,
        in_specs=[smem()] * 2 + [vmem()] * 3 + [hbm()] * (2 + N_CHUNK),
        out_specs=[hbm()] * 6,
        out_shape=results,
        scratch_shapes=on_vmem([shape(ROWS, bf16), shape((table.shape[1], 4 * BLK), f32)] + results)
        + [
            pltpu.VMEM((MP, D, D), bf16),
            pltpu.SemaphoreType.DMA((10,)),
            pltpu.SemaphoreType.DMA((MP, 4)),
            pltpu.SemaphoreType.DMA((MP, 2)),
        ],
        compiler_params=params(),
        cost_estimate=cost(14),
        name="attn_fwd",
    )(flags, table, table, attn_gain, ffn_gain, *x, *attn_weights)


def ffn_fwd(flags, final_gain, w_proj, middle, normed, ffn_weights):
    buffers = [shape(ROWS, f32), shape(ROWS, bf16)] + [shape(QUARTERS, bf16)] * 3
    buffers += [shape(ROWS, bf16), shape((DOC_LEN, PROJ), bf16)]
    results = buffers[:1] + [shape(HALF_ROWS, bf16)] * 2 + buffers[2:]
    return pl.pallas_call(
        ffn_fwd_kernel,
        in_specs=[smem()] + [vmem()] * 2 + [hbm()] * (2 + 2 * N_CHUNK),
        out_specs=[hbm()] * 8,
        out_shape=results,
        scratch_shapes=on_vmem([shape(ROWS, bf16)] + buffers)
        + [
            pltpu.VMEM((MP, D, 3 * FQ), bf16),
            pltpu.SemaphoreType.DMA((8,)),
            pltpu.SemaphoreType.DMA((MP, 4)),
            pltpu.SemaphoreType.DMA((MP, 4)),
            pltpu.SemaphoreType.DMA((MP, 3)),
        ],
        compiler_params=params(),
        cost_estimate=cost(10),
        name="ffn_fwd",
    )(flags, final_gain, w_proj, middle, normed, *ffn_weights)


def score_kernel(flags, query_ref, embed_ref, counts_ref, shares_ref, share_query_ref, mass_ref):
    @pl.when(jnp.logical_and(flags[ACT] == 1, flags[IS_DOC] == 1))
    def _():
        sims = mm_t(embed_ref[...], query_ref[...])
        weighted = jnp.exp(sims * PROJ ** (-0.5)) * counts_ref[...].astype(f32)
        mass = jnp.sum(weighted, axis=0, keepdims=True)
        mass_ref[...] = mass
        shares = (weighted * (1.0 / (1.0 + mass))).astype(bf16)
        shares_ref[...] = shares
        share_query_ref[...] = t_mm(shares, embed_ref[...])


def score(flags, query_slots, embed, counts):
    tokens = query_slots.shape[0]
    width = DOC_LEN
    return pl.pallas_call(
        score_kernel,
        grid=(tokens // width,),
        in_specs=[
            smem(),
            pl.BlockSpec((width, PROJ), lambda i: (i, 0)),
            pl.BlockSpec((DOC_LEN, PROJ), lambda i: (0, 0)),
            pl.BlockSpec((DOC_LEN, width), lambda i: (0, i)),
        ],
        out_specs=[
            pl.BlockSpec((DOC_LEN, width), lambda i: (0, i)),
            pl.BlockSpec((width, PROJ), lambda i: (i, 0)),
            pl.BlockSpec((1, width), lambda i: (0, i)),
        ],
        out_shape=[shape((DOC_LEN, tokens), bf16), shape((tokens, PROJ), f32), shape((1, tokens), f32)],
        compiler_params=params(),
        cost_estimate=cost(4),
        name="score",
    )(flags, query_slots, embed, counts)


def coef_kernel(flags, logits_ref, chosen_ref, expand_ref, share_ref, coef_ref, grad_ref, loss_ref):
    @pl.when(jnp.logical_and(flags[ACT] == 1, flags[IS_DOC] == 1))
    def _():
        logits = logits_ref[...]
        n_queries = logits.shape[1]
        spread = jnp.exp(logits - jnp.max(logits, axis=0, keepdims=True))
        all_total = jnp.sum(spread, axis=0, keepdims=True)
        pos_total = jnp.sum(chosen_ref[...] * spread, axis=0, keepdims=True)
        own = spread[0:1]
        grad = own / all_total - chosen_ref[0:1] * own / pos_total
        loss = jnp.sum(jnp.log(all_total) - jnp.log(pos_total), axis=1, keepdims=True) / n_queries
        loss_ref[...] = jnp.broadcast_to(loss, loss_ref.shape)
        grad = jnp.broadcast_to(grad * (logit_scale / QRY_LEN * PROJ ** (-0.5) / n_queries), (8, n_queries))
        coef = jnp.dot(grad, expand_ref[...], precision=highest, preferred_element_type=f32)
        coef_ref[...] = coef[0:1]
        grad_ref[...] = (share_ref[...] * coef.T[:, 0:1]).astype(bf16)


def coefs(flags, logits, chosen, expand, share_query):
    return pl.pallas_call(
        coef_kernel,
        in_specs=[smem()] + [vmem()] * 4,
        out_specs=[vmem()] * 3,
        out_shape=[
            shape((1, share_query.shape[0]), f32),
            shape(share_query.shape, bf16),
            shape((1, BLK), f32),
        ],
        compiler_params=params(),
        cost_estimate=cost(3),
        name="coefs",
    )(flags, logits, chosen, expand, share_query)


def head_bwd_kernel(
    flags, shares_ref, query_ref, coef_ref, grad_query_ref, loss_ref, normed_ref, out_ref, gain_ref, proj_ref,
    gout_low, gout_high, early_ref, grad_embed,
):
    @pl.when(jnp.logical_and(flags[ACT] == 1, flags[IS_DOC] == 1))
    def _():
        scaled = (shares_ref[...].astype(f32) * coef_ref[...]).astype(bf16)
        grad_embed[...] = mm(scaled, query_ref[...]).astype(bf16)

    @pl.when(flags[IS_DOC] == 0)
    def _():
        grad_embed[:QRY_ROWS] = grad_query_ref[...]
        grad_embed[QRY_ROWS:] = jnp.zeros((DOC_LEN - QRY_ROWS, PROJ), bf16)

    @pl.when(flags[ACT] == 1)
    def _():
        back, gain_grad = rms_back(out_ref[...], gain_ref[...], mm_t(grad_embed[...], proj_ref[...]))
        back = back.astype(bf16)
        gout_low[...] = back[:QRY_ROWS]
        gout_high[...] = back[QRY_ROWS:]
        early_ref[:PROJ] = t_mm(grad_embed[...], normed_ref[...]).astype(bf16)
        loss = jnp.concatenate([loss_ref[...]] * (D // BLK), axis=1)
        high = loss.astype(bf16).astype(f32)
        rest = jnp.zeros((13, D), f32)
        early_ref[PROJ:] = jnp.concatenate([gain_grad, high, loss - high, rest], axis=0).astype(bf16)

    @pl.when(flags[ACT] == 0)
    def _():
        early_ref[...] = jnp.zeros_like(early_ref)


def head_bwd(flags, shares, query_slots, coef, grad_query, loss, normed, out, gain, proj):
    return pl.pallas_call(
        head_bwd_kernel,
        in_specs=[smem()] + [vmem()] * 9,
        out_specs=[vmem()] * 3,
        out_shape=[shape(HALF_ROWS, bf16)] * 2 + [shape((PROJ + 16, D), bf16)],
        scratch_shapes=[pltpu.VMEM((DOC_LEN, PROJ), bf16)],
        compiler_params=params(),
        cost_estimate=cost(5),
        name="head_bwd",
    )(flags, shares, query_slots, coef, grad_query, loss, normed, out, gain, proj)


def finish(kernel, flags, results, *values):
    return pl.pallas_call(
        kernel,
        in_specs=[smem()] + [vmem()] * len(values),
        out_specs=[pl.BlockSpec(memory_space=pltpu.HBM)] * len(results),
        out_shape=[pltpu.HBM(r, f32) for r in results],
        scratch_shapes=on_vmem([shape(r, f32) for r in results]) + [pltpu.SemaphoreType.DMA((len(results),))],
        compiler_params=params(),
        cost_estimate=cost(3),
        name="finish",
    )(flags, *values)


def ffn_bwd(flags, gout, middle, gain, normed, hidden, ga, gb, ffn_weights, prev):
    results = [shape(ROWS, f32), shape((1, D), f32)]
    results += [shape((MP, D // 2, F_HALF), bf16)] * 4
    prev = prev or []
    return pl.pallas_call(
        ffn_bwd_kernel,
        in_specs=[smem(), vmem()] + [hbm()] * (7 + 2 * N_CHUNK + len(prev)),
        out_specs=[hbm()] * 6,
        out_shape=results,
        input_output_aliases={9 + 2 * N_CHUNK + i: 1 + i for i in range(len(prev))},
        scratch_shapes=on_vmem([shape(ROWS, bf16), shape(ROWS, f32), shape(ROWS, bf16)] + [shape(QUARTERS, bf16)] * 3)
        + on_vmem(results[:2])
        + [
            pltpu.VMEM((MP, D, 3 * FQ), bf16),
            pltpu.VMEM((D, DOC_LEN), bf16),
            pltpu.VMEM((D, DOC_LEN), bf16),
            pltpu.VMEM((2, D, 3 * FQ), bf16),
            pltpu.VMEM(ROWS, f32),
            pltpu.SemaphoreType.DMA((8,)),
            pltpu.SemaphoreType.DMA((MP, 4)),
            pltpu.SemaphoreType.DMA((MP, 4)),
            pltpu.SemaphoreType.DMA((MP, 3)),
            pltpu.SemaphoreType.DMA((2, 4)),
        ],
        compiler_params=params(),
        cost_estimate=cost(20),
        name="ffn_bwd",
    )(flags, gain, *gout, middle, normed, hidden, ga, gb, *ffn_weights, *prev)


def attn_bwd(flags, table, gmid, x, gain, band, ffn_gain, early, normed, qkv, lse, mixed, attn_weights, prev):
    results = [shape(HALF_ROWS, bf16)] * 2 + [shape((1, D), f32)] + [shape((MP, 2, QUARTER + SMALL, D), bf16)] * 2
    prev = prev or []
    held = (gmid, normed, shape((table.shape[1], 4 * BLK), f32), normed, qkv, lse, mixed)
    return pl.pallas_call(
        attn_bwd_kernel,
        in_specs=[smem()] * 2 + [vmem()] * 5 + [hbm()] * (7 + N_CHUNK + len(prev)),
        out_specs=[hbm()] * 5,
        out_shape=results,
        input_output_aliases={14 + N_CHUNK + i: i for i in range(len(prev))},
        scratch_shapes=on_vmem(held)
        + on_vmem([shape(ROWS, bf16), shape((1, D), f32)])
        + [
            pltpu.VMEM((MP, 8, 6 * BLK), f32),
            pltpu.VMEM((MP, D, D), bf16),
            pltpu.VMEM(ROWS, bf16),
            pltpu.VMEM((DOC_LEN, QUARTER), bf16),
            pltpu.VMEM((DOC_LEN, QKV), bf16),
            pltpu.VMEM((2, D, D), bf16),
            pltpu.VMEM(ROWS, f32),
            pltpu.VMEM((2, MP, 2, SMALL, D), bf16),
            pltpu.SemaphoreType.DMA((10,)),
            pltpu.SemaphoreType.DMA((MP, 4)),
            pltpu.SemaphoreType.DMA((MP, 2)),
            pltpu.SemaphoreType.DMA((2, 4)),
            pltpu.SemaphoreType.DMA((2,)),
        ],
        compiler_params=params(),
        cost_estimate=cost(25),
        name="attn_bwd",
    )(flags, table, table, gain, band, ffn_gain, early, gmid, *x, normed, qkv, lse, mixed, *attn_weights, *prev)


def swap(values, axis, bit):
    count = lax.axis_size(axis)
    return lax.ppermute(values, axis, [(i, i ^ bit) for i in range(count)])


def swap_cores(values, axis, bit, core):
    dp_count, mp_count = lax.axis_size("dp"), lax.axis_size("mp")
    perm = []
    for i in range(core, dp_count, 2):
        for j in range(mp_count):
            to = (i ^ bit) * mp_count + j if axis == "dp" else i * mp_count + (j ^ bit)
            perm.append((i * mp_count + j, to))
    return lax.ppermute(values, ("dp", "mp"), perm)


def hop(rows, source):
    first = lax.ppermute(rows[0], "section", [(source, 1 - source)])
    dp_count = lax.axis_size("dp")
    perm = [(source * dp_count + i, (1 - source) * dp_count + i) for i in range(0, dp_count, 2)]
    return first, lax.ppermute(rows[1], ("section", "dp"), perm)


def pick(values, axis, index):
    return lax.dynamic_index_in_dim(values, index, axis, keepdims=False)


def add_low(a, b):
    return (a.astype(f32) + b.astype(f32)).astype(bf16)


def fence(*values):
    return lax.optimization_barrier(values)


def total_of(terms, more=()):
    def part(array, picks):
        for dim, index in picks:
            array = pick(array, dim, index)
        return array.astype(f32)

    return functools.reduce(jnp.add, [part(array, picks + more) for array, picks in terms]).astype(bf16)


def give(terms, dim, axis, bit, mine):
    return swap(total_of(terms, ((dim, 1 - mine),)), axis, bit)


def take(terms, dim, mine, got):
    return [(array, picks + ((dim, mine),)) for array, picks in terms] + [(got, ())]


def fence_terms(terms, *values):
    arrays, values = lax.optimization_barrier(([[array for array, _ in one] for one in terms], values))
    terms = [[(array, picks) for array, (_, picks) in zip(new, old)] for new, old in zip(arrays, terms)]
    return *terms, *values


def in_order(mine, values, other):
    return jnp.where(mine == 0, jnp.stack([values, other]), jnp.stack([other, values]))


def over_rest(total):
    bit = 4
    while bit < lax.axis_size("dp"):
        total = add_low(total, swap(total, "dp", bit))
        bit *= 2
    return total


def spread_tokens(tokens, place, pairs):
    z = place[2]
    got = []
    for turn in range(2):
        perm = []
        for j in range(pairs):
            for c in range(2):
                for zz in range(MP):
                    u = (turn + zz) % 2
                    perm.append(((2 * j + c) * MP + zz, (2 * j + zz // 2) * MP + 2 * c + u))
        block = pick(tokens, 0, (turn + z) % 2)
        got.append(lax.ppermute(block, ("dp", "mp"), perm))
    return got


def arrange_tokens(got, place):
    core, _, z = place
    low, high = jnp.where(z % 2 == 0, jnp.stack(got), jnp.stack(got[::-1]))
    cut = DOC_LEN - 2 * QUARTER
    tail = swap(low[:cut], "dp", 1)
    doc = jnp.concatenate([low, high, tail])
    qry = jnp.concatenate([low[cut:], high, jnp.zeros((DOC_LEN - QRY_ROWS, D), low.dtype)])
    rows = jnp.where(core == 0, doc, qry)
    return rows[:QRY_ROWS], rows[QRY_ROWS:]


def split_rows(rows, place):
    core = place[0]
    cut = DOC_LEN - 2 * QUARTER
    tail = swap(rows[2 * QUARTER :], "dp", 1)
    low_q = jnp.concatenate([tail, rows[: QUARTER - cut]])
    high_q = rows[QUARTER - cut : QRY_ROWS]
    low = jnp.where(core == 0, rows[:QUARTER], low_q)
    high = jnp.where(core == 0, rows[QUARTER : 2 * QUARTER], high_q)
    return low, high


def collect_rows(blocks, place, pairs):
    low, high = blocks
    z = place[2]
    got = []
    for turn in range(2):
        perm = []
        for j in range(pairs):
            for c in range(2):
                for zz in range(MP):
                    u = (turn + zz) % 2
                    perm.append(((2 * j + zz // 2) * MP + 2 * c + u, (2 * j + c) * MP + zz))
        block = jnp.where((z + turn) % 2 == 0, low, high)
        got.append(lax.ppermute(block, ("dp", "mp"), perm))
    return jnp.where(z % 2 == 0, jnp.stack(got), jnp.stack(got[::-1]))


def gather_slots(values, steps, core):
    for axis, bit in steps:
        values = jnp.concatenate([values, swap_cores(values, axis, bit, core)])
    return values


def scatter_slots(values, steps, core):
    for axis, bit in reversed(steps):
        half = values.shape[0] // 2
        values = add_low(values[:half], swap_cores(values[half:], axis, bit, core))
    return values[0]


def on_device(
    tokens,
    attn_gain,
    w_query,
    w_key,
    w_value,
    w_out,
    ffn_gain,
    w_gate,
    w_up,
    w_down,
    rel_table,
    final_gain,
    w_proj,
    positives,
    retrieved,
):
    section = lax.axis_index("section")
    dp = lax.axis_index("dp")
    dp_count = lax.axis_size("dp")
    z = lax.axis_index("mp")
    core, y = dp % 2, (dp // 2) % 2
    place = (core, y, z)
    pairs = dp_count // 2
    chip = (dp // 2) * MP + z
    chips = pairs * MP
    is_doc = core == 0
    first = section == 0
    quad = dp % 4

    def piece_of(quarter):
        return lax.dynamic_slice_in_dim(quarter, quad * QUARTER, QUARTER, 0)

    attn_own = jnp.concatenate([w_query[0].T, w_key[0].T, w_value[0].T, w_out[0]])
    def ffn_owns(gate, up, down):
        whole = jnp.concatenate([gate[0], up[0], down[0].T], axis=1)
        return [whole[:, :F_HALF], whole[:, F_HALF:]]

    owns = [attn_own]
    own_pieces = [piece_of(attn_own)]
    got = {}

    def along_z(k, *which):
        for at in which:
            source = own_pieces[k] if at < 3 else got[k, 2, 0]
            got[k, at, 0] = swap(source, "mp", 1 if at == 3 else at)

    def along_y(k, *which):
        for at in which:
            got[k, at, 1] = swap(got[k, at, 0], "dp", 2)

    def to_core(k, m, *which):
        for at in which:
            got[k, at, 2 + m] = swap(got[k, at, m], "dp", 1)

    def hold(keys, *values):
        held, values = lax.optimization_barrier(([got[key] for key in keys], values))
        got.update(zip(keys, held))
        return values

    def chunk_of(k):
        return (owns[k],) + tuple(got[k, at, m] for at in range(1, MP) for m in range(4))

    heads_dev = rel_table.shape[1]
    buckets = rel_table.shape[0]
    half_count = buckets // 2
    bucket_ids = jnp.arange(buckets, dtype=jnp.int32)

    def flags_for(active):
        return jnp.stack([jnp.asarray(active).astype(jnp.int32), is_doc.astype(jnp.int32), z, quad])

    def whole_table(table):
        table = jnp.take(jnp.stack(table), z ^ jnp.arange(MP), axis=0, mode="clip")
        return jnp.swapaxes(table, 0, 1).reshape(buckets, -1)

    def band_picks(lanes):
        band_offset = jnp.where(lanes <= 2 * BLK + BLK - 1, BLK - lanes, 5 * BLK - lanes)
        ends = [jnp.full((BLK,), buckets - 1, jnp.int32), jnp.full((BLK,), half_count - 1, jnp.int32)]
        band_bucket = jnp.concatenate([bucket_of(band_offset, half_count)] + ends)
        return (band_bucket[:, None] == jnp.arange(BLK, dtype=jnp.int32)).astype(f32)

    topk = retrieved.shape[2]
    mb_of_slot = chip ^ jnp.arange(chips, dtype=jnp.int32)

    def counts_of(hits):
        hits = jnp.take(jnp.concatenate(hits), dp ^ jnp.arange(dp_count), axis=0, mode="clip").reshape(chips * QRYS_MB, -1)
        slot_retrieved = jnp.take(hits[:, : QRY_LEN * topk].reshape(chips, QRY_ROWS, topk), mb_of_slot, axis=0, mode="clip")
        flags = flags_for(jnp.logical_not(first))
        positives_slot = jnp.take(
            hits[:, QRY_LEN * topk :].reshape(chips, QRYS_MB, -1), mb_of_slot, axis=0, mode="clip"
        ).reshape(chips * QRYS_MB, -1)
        chosen = jnp.any(positives_slot[None] == mb_of_slot[:, None, None], axis=2).astype(f32)
        return chosen, count_hits(flags, slot_retrieved.reshape(-1, topk).T - chip * DOC_LEN)

    along_z(0, 2, 1)
    table = [rel_table] + [swap(rel_table, "mp", by) for by in range(1, MP)]
    w_gate, w_up, w_down, tokens, table, retrieved, positives = hold(
        [(0, 1, 0), (0, 2, 0)], w_gate, w_up, w_down, tokens, table, retrieved, positives
    )
    along_z(0, 3)
    along_y(0, 1, 2)
    to_core(0, 0, 1, 2)
    tokens = spread_tokens(tokens, place, pairs)
    owns += ffn_owns(w_gate, w_up, w_down)
    own_pieces += [piece_of(own) for own in owns[1:]]
    owns, own_pieces, tokens, table, retrieved, positives = hold(
        [(0, 3, 0), (0, 1, 1), (0, 2, 1)], owns, own_pieces, tokens, table, retrieved, positives
    )
    along_y(0, 3)
    to_core(0, 0, 3)
    to_core(0, 1, 1, 2)
    along_z(1, 2, 1)
    x_first = arrange_tokens(tokens, place)
    table = whole_table(table)
    x_first, table, own_pieces[2], retrieved, positives = hold(
        [(0, 3, 1), (1, 1, 0), (1, 2, 0)], x_first, table, own_pieces[2], retrieved, positives
    )
    hits = jnp.concatenate([retrieved.reshape(retrieved.shape[0], -1), positives], axis=1)[None]
    hits = [hits] + [swap(hits, "dp", by) for by in range(1, dp_count)]
    lanes = jnp.arange(chips * QRY_ROWS, dtype=jnp.int32)
    to_core(0, 1, 3)
    along_z(1, 3)
    along_z(2, 2, 1)
    along_y(1, 1, 2)
    to_core(1, 0, 1, 2)
    attn_weights = chunk_of(0)

    kept = []
    x = x_first
    for step in range(2):
        flags = flags_for(section == step)
        normed, qkv, lse, mixed, middle, normed_ffn = attn_fwd(flags, table, x, attn_gain, ffn_gain, attn_weights)
        if step == 0:
            middle, normed_ffn, hits, lanes = hold(
                [(1, 3, 0), (1, 1, 1), (1, 2, 1), (2, 1, 0), (2, 2, 0)], middle, normed_ffn, hits, lanes
            )
            along_z(2, 3)
            along_y(2, 1, 2)
            along_y(1, 3)
            to_core(1, 0, 3)
            to_core(1, 1, 1, 2)
            to_core(2, 0, 1, 2)
            chosen, counts = counts_of(hits)
            expand = (lanes // QRY_LEN == jnp.arange(chips * QRYS_MB)[:, None]).astype(f32)
            chosen, counts, expand, pick_band = hold(
                [(2, 3, 0), (2, 1, 1), (2, 2, 1), (1, 3, 1)], chosen, counts, expand, band_picks(lanes[: 4 * BLK])
            )
            along_y(2, 3)
            to_core(1, 1, 3)
            to_core(2, 0, 3)
            to_core(2, 1, 1, 2)
            hold([(2, 3, 1)])
            to_core(2, 1, 3)
            ffn_weights = chunk_of(1) + chunk_of(2)
        out, low, low_high, hidden, ga, gb, normed_final, embed = ffn_fwd(
            flags, final_gain[None], w_proj, middle, normed_ffn, ffn_weights
        )
        kept.append((x, normed, qkv, lse, mixed, middle, normed_ffn, hidden, ga, gb))
        if step == 0:
            x = hop((low, low_high), 0)

    live = jnp.logical_not(first)
    scale = PROJ ** (-0.5)
    steps = [("mp", 1), ("mp", 2)]
    bit = 2
    while bit < dp_count:
        steps.append(("dp", bit))
        bit *= 2
    query_slots = swap(gather_slots(embed[None, :QRY_ROWS], steps, 1), "dp", 1).reshape(-1, PROJ)
    shares, share_query, mass = score(flags_for(live), query_slots, embed, counts)
    logit = logit_scale * jnp.mean(jnp.log1p(mass).reshape(chips * QRYS_MB, QRY_LEN), axis=1)
    logits = logit[None]
    for at, (axis, bit) in enumerate(steps):
        got_logits = swap_cores(logits, axis, bit, 0)
        turned = got_logits.reshape(got_logits.shape[0], -1, 2, QRYS_MB << at)[:, :, ::-1]
        logits = jnp.concatenate([logits, turned.reshape(got_logits.shape)])
    coef, grad_query, loss_here = coefs(flags_for(live), logits, chosen, expand, share_query)
    grad_query = scatter_slots(swap(grad_query.reshape(chips, QRY_ROWS, PROJ), "dp", 1), steps, 1)
    lead = jnp.logical_and(live, jnp.logical_and(dp == 0, z == 0))
    loss_here = jnp.where(lead, loss_here, 0.0)
    *grad_final, early_own = head_bwd(
        flags_for(live), shares, query_slots, coef, grad_query, loss_here, normed_final, out, final_gain[None], w_proj
    )
    early = (early_own + swap(early_own, "section", 1)).astype(f32)

    def ffn_back(step, grad_out, prev):
        x, normed, qkv, lse, mixed, middle, normed_ffn, hidden, ga, gb = kept[step]
        flags = flags_for(section == step)
        return ffn_bwd(flags, grad_out, middle, ffn_gain, normed_ffn, hidden, ga, gb, ffn_weights, prev)

    def attn_back(step, gmid, ffn_gain_grad, prev):
        x, normed, qkv, lse, mixed, middle, normed_ffn, hidden, ga, gb = kept[step]
        flags = flags_for(section == step)
        return attn_bwd(
            flags, table, gmid, x, attn_gain, pick_band, ffn_gain_grad, early, normed, qkv, lse, mixed, attn_weights, prev
        )

    gmid, *ffn_prev = ffn_back(1, grad_final, None)
    attn_prev = attn_back(1, gmid, ffn_prev[0], None)
    gmid, grad_ffn_gain, f1_keep, f1_send, f2_keep, f2_send = ffn_back(0, hop(attn_prev[:2], 1), ffn_prev)

    zl, zh = z % 2, z // 2

    def parts(values):
        return values.reshape(2, 2, 2, -1, values.shape[-1])

    def both(keep, send):
        return [(parts(keep), ()), (parts(swap(send, "dp", 1)), ())]

    f1, f2, gmid = fence_terms((both(f1_keep, f1_send), both(f2_keep, f2_send)), gmid)
    f1_got = give(f1, 2, "dp", 2, y)
    f2_got = give(f2, 1, "mp", 1, zl)
    gx, gx_high, _, a_keep, a_send = attn_back(0, gmid, grad_ffn_gain, attn_prev)
    f1, f2, f1_got, f2_got, a_keep, a_send, gx = fence_terms((f1, f2), f1_got, f2_got, a_keep, a_send, gx)
    f1, f2 = take(f1, 2, y, f1_got), take(f2, 1, zl, f2_got)
    out_f1, out_f2 = total_of(f1, ((1, 1 - zl),)), total_of(f2, ((0, 1 - zh),))
    n_small = SMALL - 8
    a = both(a_keep, a_send)
    a, out_f1, out_f2 = fence_terms((a,), out_f1, out_f2)
    f1_got, f2_got = swap(out_f1, "mp", 1), swap(out_f2, "mp", 2)
    a_got = give(a, 2, "dp", 2, y)
    f1, f2, a, f1_got, f2_got, a_got, gx = fence_terms((f1, f2, a), f1_got, f2_got, a_got, gx)

    blocks = split_rows(jnp.concatenate([gx, gx_high]), place)
    f1, f2, a = take(f1, 1, zl, f1_got), take(f2, 0, zh, f2_got), take(a, 2, y, a_got)
    a_got = give(a, 1, "mp", 1, zl)
    f1_got = give(f1, 0, "mp", 2, zh)
    f2 = total_of(f2)
    f2_got = swap(f2, "dp", 2)

    a = take(a, 1, zl, a_got)
    a_got = give(a, 0, "mp", 2, zh)
    f1 = over_rest(total_of(take(f1, 0, zh, f1_got)))
    f1_got = swap(f1, "dp", 2)
    f2 = over_rest(add_low(f2, f2_got))
    f2_other = swap(f2, "dp", 1)

    a, blocks = fence(over_rest(total_of(take(a, 0, zh, a_got))), blocks)
    a_got = swap(a, "dp", 2)
    d_inputs = collect_rows(blocks, place, pairs)[None]
    f1 = in_order(y, f1, f1_got)
    f1_other = swap(f1, "dp", 1)
    flags_end = flags_for(1)
    ffn_sums = finish(finish_ffn_kernel, flags_end, [(D, FQ), (D, FQ), (FQ, D)], f1, f1_other, f2, f2_other)

    a, a_got, d_inputs = fence(a, a_got, d_inputs)
    small_sum = a[QUARTER : QUARTER + n_small].astype(f32)
    table_other = swap(small_sum[:heads_dev], "section", 1)
    a = in_order(y, a, a_got)
    a_other = swap(a, "dp", 1)
    attn_sums = finish(finish_attn_kernel, flags_end, [(QUARTER, D)] * 4, a, a_other)
    proj_sum = in_order(core, a[:, QUARTER + n_small :], a_other[:, QUARTER + n_small :])
    proj_sum = proj_sum.astype(f32).reshape(PROJ // MP, D)
    shared_sum = small_sum[heads_dev:]
    grad_table = (small_sum[:heads_dev] + table_other)[:, :buckets].T
    return (
        shared_sum[3, 0] + shared_sum[4, 0],
        d_inputs,
        shared_sum[0:1],
        attn_sums[0].T[None],
        attn_sums[1].T[None],
        attn_sums[2].T[None],
        attn_sums[3][None],
        shared_sum[1:2],
        ffn_sums[0][None],
        ffn_sums[1][None],
        ffn_sums[2][None],
        grad_table,
        shared_sum[2],
        proj_sum.T,
    )


def solution(mesh):
    return jax.shard_map(
        on_device,
        mesh=mesh,
        in_specs=(
            P("dp", "mp", None),
            P("section", None),
            P("section", None, "mp"),
            P("section", None, "mp"),
            P("section", None, "mp"),
            P("section", "mp", None),
            P("section", None),
            P("section", None, "mp"),
            P("section", None, "mp"),
            P("section", "mp", None),
            P(None, "mp"),
            P(),
            P(),
            P("dp", None),
            P("dp", None, None),
        ),
        out_specs=(
            P(),
            P("section", "dp", "mp", None),
            P("section", None),
            P("section", None, "mp"),
            P("section", None, "mp"),
            P("section", None, "mp"),
            P("section", "mp", None),
            P("section", None),
            P("section", None, "mp"),
            P("section", None, "mp"),
            P("section", "mp", None),
            P(None, "mp"),
            P(),
            P(None, "mp"),
        ),
        check_vma=False,
    )
```

```python
import functools

import jax
import jax.numpy as jnp
from jax import lax
from jax.experimental import pallas as pl
from jax.experimental.pallas import tpu as pltpu
from jax.sharding import PartitionSpec as P

D = 768
HEAD_DIM = 64
FF = 2048
PROJ = 128
DOC_LEN = 512
QRY_LEN = 32
QRYS_MB = 8
QRY_ROWS = QRYS_MB * QRY_LEN
MP = 4
QUARTER = D // MP
FQ = FF // MP
HEADS_Q = QUARTER // HEAD_DIM
BLK = 128
NBLK = DOC_LEN // BLK
QKV = 3 * QUARTER
SMALL = 16
F_HALF = 3 * FQ // 2

bucket_edges = (8, 12, 16, 23, 32, 46, 64, 91)
norm_eps = 1e-06
logit_scale = 16.0
highest = lax.Precision.HIGHEST
f32 = jnp.float32
bf16 = jnp.bfloat16

ACT, IS_DOC, ZPOS, RPOS, LAST = range(5)
VMEM_LIMIT = 56 * 1024 * 1024


def mm(a, b):
    return jnp.dot(a, b, preferred_element_type=f32)


def mm_t(a, b):
    return lax.dot_general(a, b, (((1,), (1,)), ((), ())), preferred_element_type=f32)


def t_mm(a, b):
    return lax.dot_general(a, b, (((0,), (0,)), ((), ())), preferred_element_type=f32)


def bucket_of(offset, half_count):
    spread = jnp.abs(offset)
    far_bucket = 7 + sum((spread >= edge).astype(jnp.int32) for edge in bucket_edges)
    near_bucket = jnp.where(spread < 8, spread, far_bucket)
    return near_bucket + half_count * (offset > 0).astype(jnp.int32)


class Copies:
    def __init__(self, sem, first=0):
        self.sem = sem
        self.next = first

    def __call__(self, source, target):
        copy = pltpu.make_async_copy(source, target, self.sem.at[self.next])
        self.next += 1
        copy.start()
        return copy


def get_rows(copy, halves, target, doc):
    count = 2 if doc else 1
    return [copy(halves[i], target.at[pl.ds(i * QRY_ROWS, QRY_ROWS)]) for i in range(count)]


def put_rows(copy, source, halves, doc):
    count = 2 if doc else 1
    return [copy(source.at[pl.ds(i * QRY_ROWS, QRY_ROWS)], halves[i]) for i in range(count)]


def wait_all(copies):
    for copy in copies:
        copy.wait()


class Weights:
    def __init__(self, flags, chunk, target, sem, lanes=None):
        self.z, self.r = flags[ZPOS], flags[RPOS]
        self.own, self.pieces = chunk[0], chunk[1:]
        self.target, self.sem = target, sem
        self.lanes = pl.ds(0, target.shape[2]) if lanes is None else lanes

    def copies(self, s):
        if s == 0:
            return [pltpu.make_async_copy(self.own, self.target.at[self.z, :, self.lanes], self.sem.at[0, 0])]
        return [
            pltpu.make_async_copy(
                self.pieces[4 * (s - 1) + k],
                self.target.at[self.z ^ s, rows_at(self.r ^ bits, QUARTER), self.lanes],
                self.sem.at[s, k],
            )
            for k, bits in enumerate((0, 2, 1, 3))
        ]

    def start(self):
        for s in range(MP):
            start_all(self.copies(s))

    def each(self, s, act):
        for k in range(MP):
            pl.when(s == k)(lambda k=k: act(self.copies(k)))

    def start_slot(self, s):
        self.each(s, start_all)

    def wait_slot(self, s):
        self.each(s, wait_all)


N_CHUNK = 13


def start_all(copies):
    for copy in copies:
        copy.start()


def rows_at(index, size):
    return pl.ds(pl.multiple_of(index * size, size), size)


def offset_bias(table):
    column = lax.broadcasted_iota(jnp.int32, (table.shape[0], 4 * BLK), 1)
    bucket = lax.broadcasted_iota(jnp.int32, (table.shape[0], 4 * BLK), 0)
    offset = jnp.where(column < 2 * BLK, -column, 4 * BLK - column)
    hot = (bucket_of(offset, table.shape[0] // 2) == bucket).astype(f32)
    return lax.dot_general(table, hot, (((0,), (0,)), ((), ())), precision=highest, preferred_element_type=f32)


def near_blocks(offsets_ref, head):
    row = jnp.broadcast_to(offsets_ref[pl.ds(head, 1), :], (BLK, 4 * BLK))
    rolled = pltpu.roll(row, 0, 1, stride=1, stride_axis=0)
    return {0: rolled[:, :BLK], -1: rolled[:, BLK : 2 * BLK], 1: rolled[:, 3 * BLK :]}


def bias_matrix(offsets_ref, table_ref, head):
    far_up = jnp.full((BLK, BLK), table_ref[31, head], f32)
    far_low = jnp.full((BLK, BLK), table_ref[15, head], f32)
    near = near_blocks(offsets_ref, head)

    def block(bj, bi):
        if bj - bi in near:
            return near[bj - bi]
        return far_up if bj > bi else far_low

    return jnp.concatenate(
        [jnp.concatenate([block(bj, bi) for bi in range(NBLK)], axis=1) for bj in range(NBLK)], axis=0
    )


def query_bias(offsets_ref, head):
    j = lax.broadcasted_iota(jnp.int32, (BLK, BLK), 0) // QRY_LEN
    i = lax.broadcasted_iota(jnp.int32, (BLK, BLK), 1) // QRY_LEN
    return jnp.where(i == j, near_blocks(offsets_ref, head)[0], -1e30)


def rms_parts(values):
    return lax.rsqrt(jnp.mean(values * values, axis=-1, keepdims=True) + norm_eps)


def rms_back(values, gain, grad):
    scale = rms_parts(values)
    weighted = grad * gain
    inner = jnp.mean(values * weighted, axis=-1, keepdims=True)
    out = scale * (weighted - values * (scale * scale * inner))
    gain_grad = jnp.sum(grad * values * scale, axis=0, keepdims=True)
    return out, gain_grad


def by_kind(flags, body):
    pl.when(flags[IS_DOC] == 1)(lambda: body(DOC_LEN, True))
    pl.when(flags[IS_DOC] == 0)(lambda: body(QRY_ROWS, False))


def head_slices(hh):
    at = hh * HEAD_DIM
    return (
        slice(at, at + HEAD_DIM),
        slice(QUARTER + at, QUARTER + at + HEAD_DIM),
        slice(2 * QUARTER + at, 2 * QUARTER + at + HEAD_DIM),
        slice(at, at + HEAD_DIM),
    )


def attn_fwd_kernel(flags, table, table_ref, attn_gain_ref, ffn_gain_ref, x_low, x_high, *refs):
    weights, refs = refs[:N_CHUNK], refs[N_CHUNK:]
    normed_out, qkv_out, lse_out, mixed_out, middle_out, normed_ffn_out = refs[:6]
    x_ref, offsets_ref, normed_ref, qkv_ref, lse_ref, mixed_ref, middle_ref, normed_ffn_ref = refs[6:14]
    wa, sem, asem, zsem = refs[14:]
    weights = Weights(flags, weights, wa, asem)
    def one_head(z, hh, rows, bias):
        qs, ks, vs, ms = head_slices(hh)
        q, k, v = qkv_ref[z, rows, qs], qkv_ref[z, rows, ks], qkv_ref[z, rows, vs]
        scores = mm_t(k, q) + bias
        peak = jnp.max(scores, axis=0, keepdims=True)
        weights = jnp.exp(scores - peak)
        total = jnp.sum(weights, axis=0, keepdims=True)
        mixed = t_mm(v, weights.astype(bf16)) * (1.0 / total)
        lse_ref[z, hh : hh + 1, rows] = peak + jnp.log(total)
        mixed_ref[z, rows, ms] = mixed.T.astype(bf16)

    def body(rows, doc):
        put = Copies(sem)
        outs = []
        get_x = get_rows(put, (x_low, x_high), x_ref, doc)
        weights.start()
        offsets_ref[...] = offset_bias(table_ref[...])
        wait_all(get_x)

        def send(source, target):
            outs.append(put(source.at[pl.ds(0, rows)], target.at[pl.ds(0, rows)]))

        def parts(z):
            return [
                pltpu.make_async_copy(a.at[z, pl.ds(0, rows)], b.at[z, pl.ds(0, rows)], zsem.at[z, i])
                for i, (a, b) in enumerate(((qkv_ref, qkv_out), (mixed_ref, mixed_out)))
            ]

        x = x_ref[:rows].astype(f32)
        normed_ref[:rows] = (x * rms_parts(x) * attn_gain_ref[...]).astype(bf16)
        send(normed_ref, normed_out)

        @pl.loop(0, MP)
        def _(s):
            z = flags[ZPOS] ^ s
            weights.wait_slot(s)
            qkv_ref[z, :rows] = mm_t(normed_ref[:rows], wa[z, :QKV]).astype(bf16)
            for hh in range(HEADS_Q):
                head = z * HEADS_Q + hh
                if doc:
                    one_head(z, hh, slice(0, DOC_LEN), bias_matrix(offsets_ref, table, head))
                else:
                    bias = query_bias(offsets_ref, head)
                    for b in range(QRY_ROWS // BLK):
                        one_head(z, hh, slice(b * BLK, (b + 1) * BLK), bias)
            start_all(parts(z))

        outs.append(put(lse_ref, lse_out))
        middle_ref[:rows] = x_ref[:rows].astype(f32)

        @pl.loop(0, MP)
        def _(z):
            middle_ref[:rows] += mm(mixed_ref[z, :rows], wa[z, QKV:])

        middle = middle_ref[:rows]
        send(middle_ref, middle_out)
        normed_ffn_ref[:rows] = (middle * rms_parts(middle) * ffn_gain_ref[...]).astype(bf16)
        send(normed_ffn_ref, normed_ffn_out)

        @pl.loop(0, MP)
        def _(z):
            wait_all(parts(z))

        wait_all(outs)

    @pl.when(flags[ACT] == 1)
    def _():
        by_kind(flags, body)


def ffn_fwd_kernel(flags, final_gain_ref, proj_ref, middle_hbm, normed_hbm, *refs):
    first, second, refs = refs[:N_CHUNK], refs[N_CHUNK : 2 * N_CHUNK], refs[2 * N_CHUNK :]
    out_out, low_low, low_high, hidden_out, ga_out, gb_out, final_out, embed_out = refs[:8]
    normed_ref, out_ref, low_ref, hidden_ref, ga_ref, gb_ref, final_ref, embed_ref = refs[8:16]
    wf, sem, fsem, gsem, zsem = refs[16:]
    first = Weights(flags, first, wf, fsem, pl.ds(0, F_HALF))
    second = Weights(flags, second, wf, gsem, pl.ds(F_HALF, F_HALF))

    def body(rows, doc):
        copy = Copies(sem)
        get_normed = copy(normed_hbm.at[pl.ds(0, rows)], normed_ref.at[pl.ds(0, rows)])
        get_middle = copy(middle_hbm.at[pl.ds(0, rows)], out_ref.at[pl.ds(0, rows)])
        first.start_slot(0)
        second.start_slot(0)

        def parts(z):
            pairs = ((hidden_ref, hidden_out), (ga_ref, ga_out), (gb_ref, gb_out))
            return [
                pltpu.make_async_copy(a.at[z, pl.ds(0, rows)], b.at[z, pl.ds(0, rows)], zsem.at[z, i])
                for i, (a, b) in enumerate(pairs)
            ]

        get_normed.wait()
        get_middle.wait()

        @pl.loop(0, MP)
        def _(s):
            z = flags[ZPOS] ^ s

            first.start_slot(s + 1)
            second.start_slot(s + 1)
            first.wait_slot(s)
            second.wait_slot(s)
            normed = normed_ref[:rows]
            gate = mm(normed, wf[z, :, :FQ])
            up = mm(normed, wf[z, :, FQ : 2 * FQ])
            coef = 0.7978845608028654
            square = gate * gate
            tanh = jnp.tanh(coef * gate * (1.0 + 0.044715 * square))
            half = 0.5 + 0.5 * tanh
            gelu = gate * half
            slope = half + (0.5 * coef) * gate * (1.0 - tanh * tanh) * (1.0 + 3 * 0.044715 * square)
            hidden = (gelu * up).astype(bf16)
            hidden_ref[z, :rows] = hidden
            ga_ref[z, :rows] = (up * slope).astype(bf16)
            gb_ref[z, :rows] = gelu.astype(bf16)
            start_all(parts(z))
            out_ref[:rows] += mm_t(hidden, wf[z, :, 2 * FQ :])

        low_ref[:rows] = out_ref[:rows].astype(bf16)
        if not doc:
            out_ref[rows:] = jnp.zeros((DOC_LEN - rows, D), f32)
            final_ref[rows:] = jnp.zeros((DOC_LEN - rows, D), bf16)
        outs = put_rows(copy, low_ref, (low_low, low_high), doc)

        @pl.when(flags[LAST] == 1)
        def _():
            out = out_ref[:rows]
            final_ref[:rows] = (out * rms_parts(out) * final_gain_ref[...]).astype(bf16)
            embed_ref[:rows] = mm(final_ref[:rows], proj_ref[...]).astype(bf16)
            lasts = [
                copy(embed_ref.at[pl.ds(0, rows)], embed_out.at[pl.ds(0, rows)]),
                copy(out_ref, out_out),
                copy(final_ref, final_out),
            ]
            wait_all(lasts)


        @pl.loop(0, MP)
        def _(z):
            wait_all(parts(z))

        wait_all(outs)

    @pl.when(flags[ACT] == 1)
    def _():
        by_kind(flags, body)


def ffn_bwd_kernel(
    flags, gain_ref, gout_low, gout_high, middle_hbm, normed_hbm, hidden_hbm, ga_hbm, gb_hbm,
    *refs,
):
    gmid_out, dgain_out, *df_outs = refs[-24:-18]
    gout_ref, middle_ref, normed_ref, hidden_ref, ga_ref, gb_ref, gmid_ref, dgain_ref = refs[-18:-10]
    wf, gout_t, normed_t, df_buf, gn, sem, fsem, gsem, ksem, osem = refs[-10:]
    first = Weights(flags, refs[:N_CHUNK], wf, fsem, pl.ds(0, F_HALF))
    second = Weights(flags, refs[N_CHUNK : 2 * N_CHUNK], wf, gsem, pl.ds(F_HALF, F_HALF))

    def outs(s, core):
        slot, half, z = s % 2, D // 2, flags[ZPOS] ^ s
        copies = []
        for i, out in enumerate(df_outs):
            rows = pl.ds((core if i % 2 == 0 else 1 - core) * half, half)
            lanes = pl.ds(i // 2 * F_HALF, F_HALF)
            copies.append(pltpu.make_async_copy(df_buf.at[slot, rows, lanes], out.at[z], osem.at[slot, i]))
        return copies

    def body(rows, doc):
        core = 0 if doc else 1
        copy = Copies(sem)

        def get(source, target):
            return copy(source.at[pl.ds(0, rows)], target.at[pl.ds(0, rows)])

        get_gout = get_rows(copy, (gout_low, gout_high), gout_ref, doc)
        get_normed = get(normed_hbm, normed_ref)
        kept = ((ga_hbm, ga_ref), (gb_hbm, gb_ref), (hidden_hbm, hidden_ref))

        def part(z):
            return [
                pltpu.make_async_copy(a.at[z, pl.ds(0, rows)], b.at[z, pl.ds(0, rows)], ksem.at[z, i])
                for i, (a, b) in enumerate(kept)
            ]

        first.start_slot(0)
        second.start_slot(0)
        start_all(part(flags[ZPOS]))
        get_middle = get(middle_hbm, middle_ref)
        wait_all(get_gout)
        gout_t[:, :rows] = gout_ref[:rows].T
        get_normed.wait()
        normed_t[:, :rows] = normed_ref[:rows].T
        gn[:rows] = jnp.zeros((rows, D), f32)

        @pl.loop(0, MP)
        def _(s):
            z = flags[ZPOS] ^ s
            pl.when(s >= 2)(lambda: wait_all(outs(s - 2, core)))

            first.start_slot(s + 1)
            second.start_slot(s + 1)
            pl.when(s + 1 < MP)(lambda: start_all(part(flags[ZPOS] ^ (s + 1))))
            first.wait_slot(s)
            second.wait_slot(s)
            wait_all(part(z))
            slot = s % 2
            grad_hidden = mm(gout_ref[:rows], wf[z, :, 2 * FQ :])
            grad_gate = (grad_hidden * ga_ref[z, :rows].astype(f32)).astype(bf16)
            grad_up = (grad_hidden * gb_ref[z, :rows].astype(f32)).astype(bf16)
            df_buf[slot, :, :FQ] = mm(normed_t[:, :rows], grad_gate).astype(bf16)
            df_buf[slot, :, FQ : 2 * FQ] = mm(normed_t[:, :rows], grad_up).astype(bf16)
            df_buf[slot, :, 2 * FQ :] = mm(gout_t[:, :rows], hidden_ref[z, :rows]).astype(bf16)
            start_all(outs(s, core))
            gn[:rows] += mm_t(grad_gate, wf[z, :, :FQ]) + mm_t(grad_up, wf[z, :, FQ : 2 * FQ])

        get_middle.wait()
        back, gain_grad = rms_back(middle_ref[:rows], gain_ref[...], gn[:rows])
        gmid_ref[:rows] = gout_ref[:rows].astype(f32) + back
        dgain_ref[...] = gain_grad
        last = [copy(gmid_ref.at[pl.ds(0, rows)], gmid_out.at[pl.ds(0, rows)]), copy(dgain_ref, dgain_out)]
        for s in (MP - 2, MP - 1):
            wait_all(outs(s, core))
        wait_all(last)

    @pl.when(flags[ACT] == 1)
    def _():
        by_kind(flags, body)


def attn_bwd_kernel(
    flags, table, table_ref, gain_ref, band_ref, ffn_gain_ref, early_ref, gmid_hbm, x_low, x_high, normed_hbm, qkv_hbm, lse_hbm,
    mixed_hbm, *refs,
):
    gx_low, gx_high, dgain_out, *da_outs = refs[-27:-22]
    gmid_ref, x_ref, offsets_ref, normed_ref, qkv_ref, lse_ref, mixed_ref, gx_ref, dgain_ref, diag_ref = refs[-22:-12]
    wa, gmb, gmix, gqkv, da_buf, gn, rows_buf, sem, asem, ksem, osem, rsem = refs[-12:]
    weights = Weights(flags, refs[:N_CHUNK], wa, asem)

    def one_head(z, hh, rows, bias):
        qs, ks, vs, ms = head_slices(hh)
        q, k, v = qkv_ref[z, rows, qs], qkv_ref[z, rows, ks], qkv_ref[z, rows, vs]
        go = gmix[rows, ms]
        out = mixed_ref[z, rows, ms].astype(f32)
        delta = jnp.sum((go.astype(f32) * out).T, axis=0, keepdims=True)
        probs = jnp.exp(mm_t(k, q) + bias - lse_ref[z, hh : hh + 1, rows])
        grad_scores = probs * (mm_t(v, go) - delta)
        low = grad_scores.astype(bf16)
        gqkv[rows, qs] = t_mm(k, low).T.astype(bf16)
        gqkv[rows, ks] = mm(low, q).astype(bf16)
        gqkv[rows, vs] = mm(probs.astype(bf16), go).astype(bf16)
        return grad_scores

    def band_sums(up, mid, low):
        blank = jnp.zeros((BLK, BLK), f32)
        band = jnp.concatenate([up, mid, low, blank], axis=1)
        width = 4 * BLK

        def left(part, by):
            return pltpu.roll(part, width - by, 1) if by else part

        eight = functools.reduce(jnp.add, [left(band[g : g + 8], g) for g in range(0, BLK, 8)])
        return functools.reduce(jnp.add, [left(eight[r : r + 1], r) for r in range(8)])

    def outs(s, core):
        slot, z = s % 2, flags[ZPOS] ^ s
        copies = []
        for i, out in enumerate(da_outs):
            for half in range(2):
                rows = pl.ds((core if i == 0 else 1 - core) * (D // 2) + half * QUARTER, QUARTER)
                target = out.at[z, half, pl.ds(0, QUARTER), :]
                copies.append(pltpu.make_async_copy(da_buf.at[slot, rows, :], target, osem.at[slot, 2 * i + half]))
        return copies

    def body(rows, doc):
        core = 0 if doc else 1
        copy = Copies(sem)

        def get(source, target):
            return copy(source.at[pl.ds(0, rows)], target.at[pl.ds(0, rows)])

        get_gmid = get(gmid_hbm, gmid_ref)
        get_lse = copy(lse_hbm, lse_ref)
        kept = ((qkv_hbm, qkv_ref), (mixed_hbm, mixed_ref))

        def part(z):
            return [
                pltpu.make_async_copy(a.at[z, pl.ds(0, rows)], b.at[z, pl.ds(0, rows)], ksem.at[z, i])
                for i, (a, b) in enumerate(kept)
            ]

        weights.start_slot(0)
        start_all(part(flags[ZPOS]))
        offsets_ref[...] = offset_bias(table_ref[...])
        get_normed = get(normed_hbm, normed_ref)
        get_x = get_rows(copy, (x_low, x_high), x_ref, doc)
        get_gmid.wait()
        gmb[:rows] = gmid_ref[:rows].astype(bf16)
        gn[:rows] = jnp.zeros((rows, D), f32)
        get_lse.wait()
        get_normed.wait()

        @pl.loop(0, MP)
        def _(s):
            z = flags[ZPOS] ^ s
            pl.when(s >= 2)(lambda: wait_all(outs(s - 2, core)))

            weights.start_slot(s + 1)
            pl.when(s + 1 < MP)(lambda: start_all(part(flags[ZPOS] ^ (s + 1))))
            weights.wait_slot(s)
            wait_all(part(z))
            slot = s % 2
            gmix[:rows] = mm_t(gmb[:rows], wa[z, QKV:]).astype(bf16)
            for hh in range(HEADS_Q):
                head = z * HEADS_Q + hh
                if doc:
                    grads = one_head(z, hh, slice(0, DOC_LEN), bias_matrix(offsets_ref, table, head))

                    def blocks(test):
                        picked = [
                            grads[bj * BLK : (bj + 1) * BLK, bi * BLK : (bi + 1) * BLK]
                            for bj in range(NBLK)
                            for bi in range(NBLK)
                            if test(bj - bi)
                        ]
                        return functools.reduce(jnp.add, picked)

                    sums = band_sums(blocks(lambda d: d == 1), blocks(lambda d: d == 0), blocks(lambda d: d == -1))
                    far_up = jnp.sum(blocks(lambda d: d > 1), axis=0, keepdims=True)
                    far_low = jnp.sum(blocks(lambda d: d < -1), axis=0, keepdims=True)
                    diag_ref[z, hh : hh + 1, :] = jnp.concatenate([sums, far_up, far_low], axis=1)
                else:
                    grads = jnp.zeros((BLK, BLK), f32)
                    bias = query_bias(offsets_ref, head)
                    for b in range(QRY_ROWS // BLK):
                        grads = grads + one_head(z, hh, slice(b * BLK, (b + 1) * BLK), bias)
                    blank = jnp.zeros((BLK, BLK), f32)
                    sums = band_sums(blank, grads, blank)
                    diag_ref[z, hh : hh + 1, :] = jnp.concatenate([sums, jnp.zeros((1, 2 * BLK), f32)], axis=1)
            grads = gqkv[:rows]
            da_buf[slot, :QKV] = t_mm(grads, normed_ref[:rows]).astype(bf16)
            da_buf[slot, QKV:] = t_mm(mixed_ref[z, :rows], gmb[:rows]).astype(bf16)
            start_all(outs(s, core))
            gn[:rows] += mm(grads, wa[z, :QKV])

        wait_all(get_x)
        back, gain_grad = rms_back(x_ref[:rows].astype(f32), gain_ref[...], gn[:rows])
        gx_ref[:rows] = (gmid_ref[:rows] + back).astype(bf16)
        dgain_ref[...] = gain_grad
        last = put_rows(copy, gx_ref, (gx_low, gx_high), doc) + [copy(dgain_ref, dgain_out)]
        for z in range(MP):
            sums = jnp.dot(diag_ref[z], band_ref[...], precision=highest, preferred_element_type=f32)
            shared = [
                jnp.concatenate([sums[:HEADS_Q], jnp.zeros((HEADS_Q, D - BLK), f32)], axis=1),
                gain_grad,
                ffn_gain_ref[...],
                early_ref[PROJ : PROJ + 3],
            ]
            shared = jnp.concatenate(shared, axis=0)
            for which, side in enumerate((core, 1 - core)):
                for half in range(2):
                    first = z * (PROJ // MP) + side * 16 + half * 8
                    both = jnp.concatenate([shared, early_ref[first : first + 8]], axis=0)
                    rows_buf[which, z, half] = both.astype(bf16)
        for which, out in enumerate(da_outs):
            target = out.at[:, :, pl.ds(QUARTER, SMALL), :]
            last.append(pltpu.make_async_copy(rows_buf.at[which], target, rsem.at[which]))
            last[-1].start()
        for s in (MP - 2, MP - 1):
            wait_all(outs(s, core))
        wait_all(last)

    @pl.when(flags[ACT] == 1)
    def _():
        by_kind(flags, body)


def put_all(refs):
    count = len(refs) // 2
    copies = [pltpu.make_async_copy(refs[count + i], refs[i], refs[-1].at[i]) for i in range(count)]
    start_all(copies)
    wait_all(copies)


def finish_ffn_kernel(flags, mine1, other1, mine2, other2, *refs):
    gate_ref, up_ref, down_ref = refs[3:6]
    core = flags[RPOS] % 2
    half = D // 2
    for side, first, second in ((core, mine1, mine2), (1 - core, other1, other2)):
        rows = rows_at(side, half)
        low = first[...].reshape(half, F_HALF).astype(f32)
        high = second[...].reshape(half, F_HALF).astype(f32)
        gate_ref[rows, :] = low[:, :FQ]
        up_ref[rows, : F_HALF - FQ] = low[:, FQ:]
        up_ref[rows, F_HALF - FQ :] = high[:, : 2 * FQ - F_HALF]
        down = high[:, 2 * FQ - F_HALF :].T

        @pl.when(side == 0)
        def _():
            down_ref[:, :half] = down

        @pl.when(side == 1)
        def _():
            down_ref[:, half:] = down

    put_all(refs)


def finish_attn_kernel(flags, mine, other, *refs):
    buffers = refs[4:8]
    core = flags[RPOS] % 2
    for side in range(2):

        @pl.when(core == side)
        def _():
            for i in range(2):
                buffers[2 * side + i][...] = mine[i, :QUARTER].astype(f32)
                buffers[2 - 2 * side + i][...] = other[i, :QUARTER].astype(f32)

    put_all(refs)


def vmem():
    return pl.BlockSpec(memory_space=pltpu.VMEM)


def smem():
    return pl.BlockSpec(memory_space=pltpu.SMEM)


def hbm():
    return pl.BlockSpec(memory_space=pl.ANY)


def shape(dims, kind):
    return jax.ShapeDtypeStruct(dims, kind)


def params():
    return pltpu.CompilerParams(vmem_limit_bytes=VMEM_LIMIT)


def cost(microseconds):
    return pl.CostEstimate(flops=int(microseconds * 1e9), bytes_accessed=16 * 1024 * 1024, transcendentals=0)


def count_kernel(flags, hits_ref, counts_out, buffer, sem):
    width = buffer.shape[2]
    blocks = hits_ref.shape[1] // width

    def put(i):
        lanes = pl.ds(pl.multiple_of(i * width, width), width)
        return pltpu.make_async_copy(buffer.at[i % 2], counts_out.at[:, lanes], sem.at[i % 2])

    @pl.when(jnp.logical_and(flags[ACT] == 1, flags[IS_DOC] == 1))
    def _():
        @pl.loop(0, blocks)
        def _(i):
            pl.when(i >= 2)(lambda: put(i - 2).wait())
            hits = hits_ref[:, pl.ds(pl.multiple_of(i * width, width), width)]
            for row in range(0, DOC_LEN, BLK):
                places = lax.broadcasted_iota(jnp.int32, (BLK, width), 0) + row
                total = jnp.zeros((BLK, width), f32)
                for k in range(hits.shape[0]):
                    total = total + (hits[k : k + 1] == places).astype(f32)
                buffer[i % 2, row : row + BLK] = total.astype(bf16)
            put(i).start()

        put(blocks - 2).wait()
        put(blocks - 1).wait()


def count_hits(flags, hits):
    width = BLK
    return pl.pallas_call(
        count_kernel,
        in_specs=[smem(), vmem()],
        out_specs=hbm(),
        out_shape=shape((DOC_LEN, hits.shape[1]), bf16),
        scratch_shapes=[pltpu.VMEM((2, DOC_LEN, width), bf16), pltpu.SemaphoreType.DMA((2,))],
        compiler_params=params(),
        cost_estimate=cost(8),
        name="count_hits",
    )(flags, hits)


QUARTERS = (MP, DOC_LEN, FQ)
ROWS = (DOC_LEN, D)
HALF_ROWS = (QRY_ROWS, D)


def on_vmem(shapes):
    return [pltpu.VMEM(s.shape, s.dtype) for s in shapes]


def attn_fwd(flags, table, x, attn_gain, ffn_gain, attn_weights):
    results = [
        shape(ROWS, bf16),
        shape((MP, DOC_LEN, QKV), bf16),
        shape((MP, 8, DOC_LEN), f32),
        shape((MP, DOC_LEN, QUARTER), bf16),
        shape(ROWS, f32),
        shape(ROWS, bf16),
    ]
    return pl.pallas_call(
        attn_fwd_kernel,
        in_specs=[smem()] * 2 + [vmem()] * 3 + [hbm()] * (2 + N_CHUNK),
        out_specs=[hbm()] * 6,
        out_shape=results,
        scratch_shapes=on_vmem([shape(ROWS, bf16), shape((table.shape[1], 4 * BLK), f32)] + results)
        + [
            pltpu.VMEM((MP, D, D), bf16),
            pltpu.SemaphoreType.DMA((10,)),
            pltpu.SemaphoreType.DMA((MP, 4)),
            pltpu.SemaphoreType.DMA((MP, 2)),
        ],
        compiler_params=params(),
        cost_estimate=cost(14),
        name="attn_fwd",
    )(flags, table, table, attn_gain, ffn_gain, *x, *attn_weights)


def ffn_fwd(flags, final_gain, w_proj, middle, normed, ffn_weights):
    buffers = [shape(ROWS, f32), shape(ROWS, bf16)] + [shape(QUARTERS, bf16)] * 3
    buffers += [shape(ROWS, bf16), shape((DOC_LEN, PROJ), bf16)]
    results = buffers[:1] + [shape(HALF_ROWS, bf16)] * 2 + buffers[2:]
    return pl.pallas_call(
        ffn_fwd_kernel,
        in_specs=[smem()] + [vmem()] * 2 + [hbm()] * (2 + 2 * N_CHUNK),
        out_specs=[hbm()] * 8,
        out_shape=results,
        scratch_shapes=on_vmem([shape(ROWS, bf16)] + buffers)
        + [
            pltpu.VMEM((MP, D, 3 * FQ), bf16),
            pltpu.SemaphoreType.DMA((8,)),
            pltpu.SemaphoreType.DMA((MP, 4)),
            pltpu.SemaphoreType.DMA((MP, 4)),
            pltpu.SemaphoreType.DMA((MP, 3)),
        ],
        compiler_params=params(),
        cost_estimate=cost(10),
        name="ffn_fwd",
    )(flags, final_gain, w_proj, middle, normed, *ffn_weights)


def score_kernel(flags, query_ref, embed_ref, counts_ref, shares_ref, share_query_ref, mass_ref):
    @pl.when(jnp.logical_and(flags[ACT] == 1, flags[IS_DOC] == 1))
    def _():
        sims = mm_t(embed_ref[...], query_ref[...])
        weighted = jnp.exp(sims * PROJ ** (-0.5)) * counts_ref[...].astype(f32)
        mass = jnp.sum(weighted, axis=0, keepdims=True)
        mass_ref[...] = mass
        shares = (weighted * (1.0 / (1.0 + mass))).astype(bf16)
        shares_ref[...] = shares
        share_query_ref[...] = t_mm(shares, embed_ref[...])


def score(flags, query_slots, embed, counts):
    tokens = query_slots.shape[0]
    width = DOC_LEN
    return pl.pallas_call(
        score_kernel,
        grid=(tokens // width,),
        in_specs=[
            smem(),
            pl.BlockSpec((width, PROJ), lambda i: (i, 0)),
            pl.BlockSpec((DOC_LEN, PROJ), lambda i: (0, 0)),
            pl.BlockSpec((DOC_LEN, width), lambda i: (0, i)),
        ],
        out_specs=[
            pl.BlockSpec((DOC_LEN, width), lambda i: (0, i)),
            pl.BlockSpec((width, PROJ), lambda i: (i, 0)),
            pl.BlockSpec((1, width), lambda i: (0, i)),
        ],
        out_shape=[shape((DOC_LEN, tokens), bf16), shape((tokens, PROJ), f32), shape((1, tokens), f32)],
        compiler_params=params(),
        cost_estimate=cost(4),
        name="score",
    )(flags, query_slots, embed, counts)


def coef_kernel(flags, logits_ref, chosen_ref, expand_ref, share_ref, coef_ref, grad_ref, loss_ref):
    @pl.when(jnp.logical_and(flags[ACT] == 1, flags[IS_DOC] == 1))
    def _():
        logits = logits_ref[...]
        n_queries = logits.shape[1]
        spread = jnp.exp(logits - jnp.max(logits, axis=0, keepdims=True))
        all_total = jnp.sum(spread, axis=0, keepdims=True)
        pos_total = jnp.sum(chosen_ref[...] * spread, axis=0, keepdims=True)
        own = spread[0:1]
        grad = own / all_total - chosen_ref[0:1] * own / pos_total
        loss = jnp.sum(jnp.log(all_total) - jnp.log(pos_total), axis=1, keepdims=True) / n_queries
        loss_ref[...] = jnp.broadcast_to(loss, loss_ref.shape)
        grad = jnp.broadcast_to(grad * (logit_scale / QRY_LEN * PROJ ** (-0.5) / n_queries), (8, n_queries))
        coef = jnp.dot(grad, expand_ref[...], precision=highest, preferred_element_type=f32)
        coef_ref[...] = coef[0:1]
        grad_ref[...] = (share_ref[...] * coef.T[:, 0:1]).astype(bf16)


def coefs(flags, logits, chosen, expand, share_query):
    return pl.pallas_call(
        coef_kernel,
        in_specs=[smem()] + [vmem()] * 4,
        out_specs=[vmem()] * 3,
        out_shape=[
            shape((1, share_query.shape[0]), f32),
            shape(share_query.shape, bf16),
            shape((1, BLK), f32),
        ],
        compiler_params=params(),
        cost_estimate=cost(3),
        name="coefs",
    )(flags, logits, chosen, expand, share_query)


def head_bwd_kernel(
    flags, shares_ref, query_ref, coef_ref, grad_query_ref, loss_ref, normed_ref, out_ref, gain_ref, proj_ref,
    gout_low, gout_high, early_ref, grad_embed,
):
    @pl.when(jnp.logical_and(flags[ACT] == 1, flags[IS_DOC] == 1))
    def _():
        scaled = (shares_ref[...].astype(f32) * coef_ref[...]).astype(bf16)
        grad_embed[...] = mm(scaled, query_ref[...]).astype(bf16)

    @pl.when(flags[IS_DOC] == 0)
    def _():
        grad_embed[:QRY_ROWS] = grad_query_ref[...]
        grad_embed[QRY_ROWS:] = jnp.zeros((DOC_LEN - QRY_ROWS, PROJ), bf16)

    @pl.when(flags[ACT] == 1)
    def _():
        back, gain_grad = rms_back(out_ref[...], gain_ref[...], mm_t(grad_embed[...], proj_ref[...]))
        back = back.astype(bf16)
        gout_low[...] = back[:QRY_ROWS]
        gout_high[...] = back[QRY_ROWS:]
        early_ref[:PROJ] = t_mm(grad_embed[...], normed_ref[...]).astype(bf16)
        loss = jnp.concatenate([loss_ref[...]] * (D // BLK), axis=1)
        high = loss.astype(bf16).astype(f32)
        rest = jnp.zeros((13, D), f32)
        early_ref[PROJ:] = jnp.concatenate([gain_grad, high, loss - high, rest], axis=0).astype(bf16)

    @pl.when(flags[ACT] == 0)
    def _():
        early_ref[...] = jnp.zeros_like(early_ref)


def head_bwd(flags, shares, query_slots, coef, grad_query, loss, normed, out, gain, proj):
    return pl.pallas_call(
        head_bwd_kernel,
        in_specs=[smem()] + [vmem()] * 9,
        out_specs=[vmem()] * 3,
        out_shape=[shape(HALF_ROWS, bf16)] * 2 + [shape((PROJ + 16, D), bf16)],
        scratch_shapes=[pltpu.VMEM((DOC_LEN, PROJ), bf16)],
        compiler_params=params(),
        cost_estimate=cost(5),
        name="head_bwd",
    )(flags, shares, query_slots, coef, grad_query, loss, normed, out, gain, proj)


def finish(kernel, flags, results, *values):
    return pl.pallas_call(
        kernel,
        in_specs=[smem()] + [vmem()] * len(values),
        out_specs=[pl.BlockSpec(memory_space=pltpu.HBM)] * len(results),
        out_shape=[pltpu.HBM(r, f32) for r in results],
        scratch_shapes=on_vmem([shape(r, f32) for r in results]) + [pltpu.SemaphoreType.DMA((len(results),))],
        compiler_params=params(),
        cost_estimate=cost(0.1),
        name="finish",
    )(flags, *values)


def ffn_bwd(flags, gout, middle, gain, normed, hidden, ga, gb, ffn_weights, prev):
    results = [shape(ROWS, f32), shape((1, D), f32)]
    results += [shape((MP, D // 2, F_HALF), bf16)] * 4
    prev = prev or []
    return pl.pallas_call(
        ffn_bwd_kernel,
        in_specs=[smem(), vmem()] + [hbm()] * (7 + 2 * N_CHUNK + len(prev)),
        out_specs=[hbm()] * 6,
        out_shape=results,
        input_output_aliases={9 + 2 * N_CHUNK + i: 1 + i for i in range(len(prev))},
        scratch_shapes=on_vmem([shape(ROWS, bf16), shape(ROWS, f32), shape(ROWS, bf16)] + [shape(QUARTERS, bf16)] * 3)
        + on_vmem(results[:2])
        + [
            pltpu.VMEM((MP, D, 3 * FQ), bf16),
            pltpu.VMEM((D, DOC_LEN), bf16),
            pltpu.VMEM((D, DOC_LEN), bf16),
            pltpu.VMEM((2, D, 3 * FQ), bf16),
            pltpu.VMEM(ROWS, f32),
            pltpu.SemaphoreType.DMA((8,)),
            pltpu.SemaphoreType.DMA((MP, 4)),
            pltpu.SemaphoreType.DMA((MP, 4)),
            pltpu.SemaphoreType.DMA((MP, 3)),
            pltpu.SemaphoreType.DMA((2, 4)),
        ],
        compiler_params=params(),
        cost_estimate=cost(20),
        name="ffn_bwd",
    )(flags, gain, *gout, middle, normed, hidden, ga, gb, *ffn_weights, *prev)


def attn_bwd(flags, table, gmid, x, gain, band, ffn_gain, early, normed, qkv, lse, mixed, attn_weights, prev):
    results = [shape(HALF_ROWS, bf16)] * 2 + [shape((1, D), f32)] + [shape((MP, 2, QUARTER + SMALL, D), bf16)] * 2
    prev = prev or []
    held = (gmid, normed, shape((table.shape[1], 4 * BLK), f32), normed, qkv, lse, mixed)
    return pl.pallas_call(
        attn_bwd_kernel,
        in_specs=[smem()] * 2 + [vmem()] * 5 + [hbm()] * (7 + N_CHUNK + len(prev)),
        out_specs=[hbm()] * 5,
        out_shape=results,
        input_output_aliases={14 + N_CHUNK + i: i for i in range(len(prev))},
        scratch_shapes=on_vmem(held)
        + on_vmem([shape(ROWS, bf16), shape((1, D), f32)])
        + [
            pltpu.VMEM((MP, 8, 6 * BLK), f32),
            pltpu.VMEM((MP, D, D), bf16),
            pltpu.VMEM(ROWS, bf16),
            pltpu.VMEM((DOC_LEN, QUARTER), bf16),
            pltpu.VMEM((DOC_LEN, QKV), bf16),
            pltpu.VMEM((2, D, D), bf16),
            pltpu.VMEM(ROWS, f32),
            pltpu.VMEM((2, MP, 2, SMALL, D), bf16),
            pltpu.SemaphoreType.DMA((10,)),
            pltpu.SemaphoreType.DMA((MP, 4)),
            pltpu.SemaphoreType.DMA((MP, 2)),
            pltpu.SemaphoreType.DMA((2, 4)),
            pltpu.SemaphoreType.DMA((2,)),
        ],
        compiler_params=params(),
        cost_estimate=cost(25),
        name="attn_bwd",
    )(flags, table, table, gain, band, ffn_gain, early, gmid, *x, normed, qkv, lse, mixed, *attn_weights, *prev)


def swap(values, axis, bit):
    count = lax.axis_size(axis)
    return lax.ppermute(values, axis, [(i, i ^ bit) for i in range(count)])


def swap_cores(values, axis, bit, core):
    dp_count, mp_count = lax.axis_size("dp"), lax.axis_size("mp")
    perm = []
    for i in range(core, dp_count, 2):
        for j in range(mp_count):
            to = (i ^ bit) * mp_count + j if axis == "dp" else i * mp_count + (j ^ bit)
            perm.append((i * mp_count + j, to))
    return lax.ppermute(values, ("dp", "mp"), perm)


def hop(rows, source):
    first = lax.ppermute(rows[0], "section", [(source, 1 - source)])
    dp_count = lax.axis_size("dp")
    perm = [(source * dp_count + i, (1 - source) * dp_count + i) for i in range(0, dp_count, 2)]
    return first, lax.ppermute(rows[1], ("section", "dp"), perm)


def pick(values, axis, index):
    return lax.dynamic_index_in_dim(values, index, axis, keepdims=False)


def add_low(a, b):
    return (a.astype(f32) + b.astype(f32)).astype(bf16)


def fence(*values):
    return lax.optimization_barrier(values)


def total_of(terms, more=()):
    def part(array, picks):
        for dim, index in picks:
            array = pick(array, dim, index)
        return array.astype(f32)

    return functools.reduce(jnp.add, [part(array, picks + more) for array, picks in terms]).astype(bf16)


def give(terms, dim, axis, bit, mine):
    return swap(total_of(terms, ((dim, 1 - mine),)), axis, bit)


def take(terms, dim, mine, got):
    return [(array, picks + ((dim, mine),)) for array, picks in terms] + [(got, ())]


def fence_terms(terms, *values):
    arrays, values = lax.optimization_barrier(([[array for array, _ in one] for one in terms], values))
    terms = [[(array, picks) for array, (_, picks) in zip(new, old)] for new, old in zip(arrays, terms)]
    return *terms, *values


def in_order(mine, values, other):
    return jnp.where(mine == 0, jnp.stack([values, other]), jnp.stack([other, values]))


def over_rest(total):
    bit = 4
    while bit < lax.axis_size("dp"):
        total = add_low(total, swap(total, "dp", bit))
        bit *= 2
    return total


def spread_tokens(tokens, place, pairs):
    z = place[2]
    got = []
    for turn in range(2):
        perm = []
        for j in range(pairs):
            for c in range(2):
                for zz in range(MP):
                    u = (turn + zz) % 2
                    perm.append(((2 * j + c) * MP + zz, (2 * j + zz // 2) * MP + 2 * c + u))
        block = pick(tokens, 0, (turn + z) % 2)
        got.append(lax.ppermute(block, ("dp", "mp"), perm))
    return got


def arrange_tokens(got, place):
    core, _, z = place
    low, high = jnp.where(z % 2 == 0, jnp.stack(got), jnp.stack(got[::-1]))
    cut = DOC_LEN - 2 * QUARTER
    tail = swap(low[:cut], "dp", 1)
    doc = jnp.concatenate([low, high, tail])
    qry = jnp.concatenate([low[cut:], high, jnp.zeros((DOC_LEN - QRY_ROWS, D), low.dtype)])
    rows = jnp.where(core == 0, doc, qry)
    return rows[:QRY_ROWS], rows[QRY_ROWS:]


def split_rows(rows, place):
    core = place[0]
    cut = DOC_LEN - 2 * QUARTER
    tail = swap(rows[2 * QUARTER :], "dp", 1)
    low_q = jnp.concatenate([tail, rows[: QUARTER - cut]])
    high_q = rows[QUARTER - cut : QRY_ROWS]
    low = jnp.where(core == 0, rows[:QUARTER], low_q)
    high = jnp.where(core == 0, rows[QUARTER : 2 * QUARTER], high_q)
    return low, high


def collect_rows(blocks, place, pairs):
    low, high = blocks
    z = place[2]
    got = []
    for turn in range(2):
        perm = []
        for j in range(pairs):
            for c in range(2):
                for zz in range(MP):
                    u = (turn + zz) % 2
                    perm.append(((2 * j + zz // 2) * MP + 2 * c + u, (2 * j + c) * MP + zz))
        block = jnp.where((z + turn) % 2 == 0, low, high)
        got.append(lax.ppermute(block, ("dp", "mp"), perm))
    return jnp.where(z % 2 == 0, jnp.stack(got), jnp.stack(got[::-1]))


def gather_slots(values, steps, core):
    for axis, bit in steps:
        values = jnp.concatenate([values, swap_cores(values, axis, bit, core)])
    return values


def scatter_slots(values, steps, core):
    for axis, bit in reversed(steps):
        half = values.shape[0] // 2
        values = add_low(values[:half], swap_cores(values[half:], axis, bit, core))
    return values[0]


def on_device(
    tokens,
    attn_gain,
    w_query,
    w_key,
    w_value,
    w_out,
    ffn_gain,
    w_gate,
    w_up,
    w_down,
    rel_table,
    final_gain,
    w_proj,
    positives,
    retrieved,
):
    section = lax.axis_index("section")
    dp = lax.axis_index("dp")
    dp_count = lax.axis_size("dp")
    z = lax.axis_index("mp")
    core, y = dp % 2, (dp // 2) % 2
    place = (core, y, z)
    pairs = dp_count // 2
    chip = (dp // 2) * MP + z
    chips = pairs * MP
    is_doc = core == 0
    first = section == 0
    quad = dp % 4

    def piece_of(quarter):
        return lax.dynamic_slice_in_dim(quarter, quad * QUARTER, QUARTER, 0)

    attn_own = jnp.concatenate([w_query[0].T, w_key[0].T, w_value[0].T, w_out[0]])
    def ffn_owns(gate, up, down):
        whole = jnp.concatenate([gate[0], up[0], down[0].T], axis=1)
        return [whole[:, :F_HALF], whole[:, F_HALF:]]

    owns = [attn_own]
    own_pieces = [piece_of(attn_own)]
    got = {}

    def along_z(k, *which):
        for at in which:
            source = own_pieces[k] if at < 3 else got[k, 2, 0]
            got[k, at, 0] = swap(source, "mp", 1 if at == 3 else at)

    def along_y(k, *which):
        for at in which:
            got[k, at, 1] = swap(got[k, at, 0], "dp", 2)

    def to_core(k, m, *which):
        for at in which:
            got[k, at, 2 + m] = swap(got[k, at, m], "dp", 1)

    def hold(keys, *values):
        held, values = lax.optimization_barrier(([got[key] for key in keys], values))
        got.update(zip(keys, held))
        return values

    def chunk_of(k):
        return (owns[k],) + tuple(got[k, at, m] for at in range(1, MP) for m in range(4))

    heads_dev = rel_table.shape[1]
    buckets = rel_table.shape[0]
    half_count = buckets // 2
    bucket_ids = jnp.arange(buckets, dtype=jnp.int32)

    def flags_for(active):
        return jnp.stack([jnp.asarray(active).astype(jnp.int32), is_doc.astype(jnp.int32), z, quad, section])

    def whole_table(table):
        table = jnp.take(jnp.stack(table), z ^ jnp.arange(MP), axis=0, mode="clip")
        return jnp.swapaxes(table, 0, 1).reshape(buckets, -1)

    def band_picks(lanes):
        band_offset = jnp.where(lanes <= 2 * BLK + BLK - 1, BLK - lanes, 5 * BLK - lanes)
        ends = [jnp.full((BLK,), buckets - 1, jnp.int32), jnp.full((BLK,), half_count - 1, jnp.int32)]
        band_bucket = jnp.concatenate([bucket_of(band_offset, half_count)] + ends)
        return (band_bucket[:, None] == jnp.arange(BLK, dtype=jnp.int32)).astype(f32)

    topk = retrieved.shape[2]
    mb_of_slot = chip ^ jnp.arange(chips, dtype=jnp.int32)

    def counts_of(hits):
        hits = jnp.take(jnp.concatenate(hits), dp ^ jnp.arange(dp_count), axis=0, mode="clip").reshape(chips * QRYS_MB, -1)
        slot_retrieved = jnp.take(hits[:, : QRY_LEN * topk].reshape(chips, QRY_ROWS, topk), mb_of_slot, axis=0, mode="clip")
        flags = flags_for(jnp.logical_not(first))
        positives_slot = jnp.take(
            hits[:, QRY_LEN * topk :].reshape(chips, QRYS_MB, -1), mb_of_slot, axis=0, mode="clip"
        ).reshape(chips * QRYS_MB, -1)
        chosen = jnp.any(positives_slot[None] == mb_of_slot[:, None, None], axis=2).astype(f32)
        return chosen, count_hits(flags, slot_retrieved.reshape(-1, topk).T - chip * DOC_LEN)

    along_z(0, 2, 1)
    table = [rel_table] + [swap(rel_table, "mp", by) for by in range(1, MP)]
    w_gate, w_up, w_down, tokens, table, retrieved, positives = hold(
        [(0, 1, 0), (0, 2, 0)], w_gate, w_up, w_down, tokens, table, retrieved, positives
    )
    along_z(0, 3)
    along_y(0, 1, 2)
    to_core(0, 0, 1, 2)
    tokens = spread_tokens(tokens, place, pairs)
    owns += ffn_owns(w_gate, w_up, w_down)
    own_pieces += [piece_of(own) for own in owns[1:]]
    owns, own_pieces, tokens, table, retrieved, positives = hold(
        [(0, 3, 0), (0, 1, 1), (0, 2, 1)], owns, own_pieces, tokens, table, retrieved, positives
    )
    along_y(0, 3)
    to_core(0, 0, 3)
    to_core(0, 1, 1, 2)
    along_z(1, 2, 1)
    x_first = arrange_tokens(tokens, place)
    table = whole_table(table)
    x_first, table, own_pieces[2], retrieved, positives = hold(
        [(0, 3, 1), (1, 1, 0), (1, 2, 0)], x_first, table, own_pieces[2], retrieved, positives
    )
    hits = jnp.concatenate([retrieved.reshape(retrieved.shape[0], -1), positives], axis=1)[None]
    hits = [hits] + [swap(hits, "dp", by) for by in range(1, dp_count)]
    lanes = jnp.arange(chips * QRY_ROWS, dtype=jnp.int32)
    to_core(0, 1, 3)
    along_z(1, 3)
    along_z(2, 2, 1)
    along_y(1, 1, 2)
    to_core(1, 0, 1, 2)
    attn_weights = chunk_of(0)

    kept = []
    x = x_first
    for step in range(2):
        flags = flags_for(section == step)
        normed, qkv, lse, mixed, middle, normed_ffn = attn_fwd(flags, table, x, attn_gain, ffn_gain, attn_weights)
        if step == 0:
            middle, normed_ffn, hits, lanes = hold(
                [(1, 3, 0), (1, 1, 1), (1, 2, 1), (2, 1, 0), (2, 2, 0)], middle, normed_ffn, hits, lanes
            )
            along_z(2, 3)
            along_y(2, 1, 2)
            along_y(1, 3)
            to_core(1, 0, 3)
            to_core(1, 1, 1, 2)
            to_core(2, 0, 1, 2)
            chosen, counts = counts_of(hits)
            expand = (lanes // QRY_LEN == jnp.arange(chips * QRYS_MB)[:, None]).astype(f32)
            chosen, counts, expand, pick_band = hold(
                [(2, 3, 0), (2, 1, 1), (2, 2, 1), (1, 3, 1)], chosen, counts, expand, band_picks(lanes[: 4 * BLK])
            )
            along_y(2, 3)
            to_core(1, 1, 3)
            to_core(2, 0, 3)
            to_core(2, 1, 1, 2)
            hold([(2, 3, 1)])
            to_core(2, 1, 3)
            ffn_weights = chunk_of(1) + chunk_of(2)
        out, low, low_high, hidden, ga, gb, normed_final, embed = ffn_fwd(
            flags, final_gain[None], w_proj, middle, normed_ffn, ffn_weights
        )
        kept.append((x, normed, qkv, lse, mixed, middle, normed_ffn, hidden, ga, gb))
        if step == 0:
            x = hop((low, low_high), 0)

    live = jnp.logical_not(first)
    scale = PROJ ** (-0.5)
    steps = [("mp", 1), ("mp", 2)]
    bit = 2
    while bit < dp_count:
        steps.append(("dp", bit))
        bit *= 2
    query_slots = swap(gather_slots(embed[None, :QRY_ROWS], steps, 1), "dp", 1).reshape(-1, PROJ)
    shares, share_query, mass = score(flags_for(live), query_slots, embed, counts)
    logit = logit_scale * jnp.mean(jnp.log1p(mass).reshape(chips * QRYS_MB, QRY_LEN), axis=1)
    logits = logit[None]
    for at, (axis, bit) in enumerate(steps):
        got_logits = swap_cores(logits, axis, bit, 0)
        turned = got_logits.reshape(got_logits.shape[0], -1, 2, QRYS_MB << at)[:, :, ::-1]
        logits = jnp.concatenate([logits, turned.reshape(got_logits.shape)])
    coef, grad_query, loss_here = coefs(flags_for(live), logits, chosen, expand, share_query)
    grad_query = scatter_slots(swap(grad_query.reshape(chips, QRY_ROWS, PROJ), "dp", 1), steps, 1)
    lead = jnp.logical_and(live, jnp.logical_and(dp == 0, z == 0))
    loss_here = jnp.where(lead, loss_here, 0.0)
    *grad_final, early_own = head_bwd(
        flags_for(live), shares, query_slots, coef, grad_query, loss_here, normed_final, out, final_gain[None], w_proj
    )
    early = (early_own + swap(early_own, "section", 1)).astype(f32)

    def ffn_back(step, grad_out, prev):
        x, normed, qkv, lse, mixed, middle, normed_ffn, hidden, ga, gb = kept[step]
        flags = flags_for(section == step)
        return ffn_bwd(flags, grad_out, middle, ffn_gain, normed_ffn, hidden, ga, gb, ffn_weights, prev)

    def attn_back(step, gmid, ffn_gain_grad, prev):
        x, normed, qkv, lse, mixed, middle, normed_ffn, hidden, ga, gb = kept[step]
        flags = flags_for(section == step)
        return attn_bwd(
            flags, table, gmid, x, attn_gain, pick_band, ffn_gain_grad, early, normed, qkv, lse, mixed, attn_weights, prev
        )

    gmid, *ffn_prev = ffn_back(1, grad_final, None)
    attn_prev = attn_back(1, gmid, ffn_prev[0], None)
    gmid, grad_ffn_gain, f1_keep, f1_send, f2_keep, f2_send = ffn_back(0, hop(attn_prev[:2], 1), ffn_prev)

    zl, zh = z % 2, z // 2

    def parts(values):
        return values.reshape(2, 2, 2, -1, values.shape[-1])

    def both(keep, send):
        return [(parts(keep), ()), (parts(swap(send, "dp", 1)), ())]

    f1, f2, gmid = fence_terms((both(f1_keep, f1_send), both(f2_keep, f2_send)), gmid)
    f1_got = give(f1, 2, "dp", 2, y)
    f2_got = give(f2, 1, "mp", 1, zl)
    gx, gx_high, _, a_keep, a_send = attn_back(0, gmid, grad_ffn_gain, attn_prev)
    f1, f2, f1_got, f2_got, a_keep, a_send, gx = fence_terms((f1, f2), f1_got, f2_got, a_keep, a_send, gx)
    f1, f2 = take(f1, 2, y, f1_got), take(f2, 1, zl, f2_got)
    out_f1, out_f2 = total_of(f1, ((1, 1 - zl),)), total_of(f2, ((0, 1 - zh),))
    n_small = SMALL - 8
    a = both(a_keep, a_send)
    a, out_f1, out_f2 = fence_terms((a,), out_f1, out_f2)
    f1_got, f2_got = swap(out_f1, "mp", 1), swap(out_f2, "mp", 2)
    a_got = give(a, 2, "dp", 2, y)
    f1, f2, a, f1_got, f2_got, a_got, gx = fence_terms((f1, f2, a), f1_got, f2_got, a_got, gx)

    blocks = split_rows(jnp.concatenate([gx, gx_high]), place)
    f1, f2, a = take(f1, 1, zl, f1_got), take(f2, 0, zh, f2_got), take(a, 2, y, a_got)
    a_got = give(a, 1, "mp", 1, zl)
    f1_got = give(f1, 0, "mp", 2, zh)
    f2 = total_of(f2)
    f2_got = swap(f2, "dp", 2)

    a = take(a, 1, zl, a_got)
    a_got = give(a, 0, "mp", 2, zh)
    f1 = over_rest(total_of(take(f1, 0, zh, f1_got)))
    f1_got = swap(f1, "dp", 2)
    f2 = over_rest(add_low(f2, f2_got))
    f2_other = swap(f2, "dp", 1)

    a, blocks = fence(over_rest(total_of(take(a, 0, zh, a_got))), blocks)
    a_got = swap(a, "dp", 2)
    d_inputs = collect_rows(blocks, place, pairs)[None]
    f1 = in_order(y, f1, f1_got)
    f1_other = swap(f1, "dp", 1)
    flags_end = flags_for(1)
    ffn_sums = finish(finish_ffn_kernel, flags_end, [(D, FQ), (D, FQ), (FQ, D)], f1, f1_other, f2, f2_other)

    a, a_got, d_inputs = fence(a, a_got, d_inputs)
    small_sum = a[QUARTER : QUARTER + n_small].astype(f32)
    table_other = swap(small_sum[:heads_dev], "section", 1)
    a = in_order(y, a, a_got)
    a_other = swap(a, "dp", 1)
    attn_sums = finish(finish_attn_kernel, flags_end, [(QUARTER, D)] * 4, a, a_other)
    proj_sum = in_order(core, a[:, QUARTER + n_small :], a_other[:, QUARTER + n_small :])
    proj_sum = proj_sum.astype(f32).reshape(PROJ // MP, D)
    shared_sum = small_sum[heads_dev:]
    grad_table = (small_sum[:heads_dev] + table_other)[:, :buckets].T
    return (
        shared_sum[3, 0] + shared_sum[4, 0],
        d_inputs,
        shared_sum[0:1],
        attn_sums[0].T[None],
        attn_sums[1].T[None],
        attn_sums[2].T[None],
        attn_sums[3][None],
        shared_sum[1:2],
        ffn_sums[0][None],
        ffn_sums[1][None],
        ffn_sums[2][None],
        grad_table,
        shared_sum[2],
        proj_sum.T,
    )


def solution(mesh):
    return jax.shard_map(
        on_device,
        mesh=mesh,
        in_specs=(
            P("dp", "mp", None),
            P("section", None),
            P("section", None, "mp"),
            P("section", None, "mp"),
            P("section", None, "mp"),
            P("section", "mp", None),
            P("section", None),
            P("section", None, "mp"),
            P("section", None, "mp"),
            P("section", "mp", None),
            P(None, "mp"),
            P(),
            P(),
            P("dp", None),
            P("dp", None, None),
        ),
        out_specs=(
            P(),
            P("section", "dp", "mp", None),
            P("section", None),
            P("section", None, "mp"),
            P("section", None, "mp"),
            P("section", None, "mp"),
            P("section", "mp", None),
            P("section", None),
            P("section", None, "mp"),
            P("section", None, "mp"),
            P("section", "mp", None),
            P(None, "mp"),
            P(),
            P(None, "mp"),
        ),
        check_vma=False,
    )
```
